32 devices in a mesh: grp: 2 (over y), sub: 16 (over z, x, core).
Axes of the slice: x: 2, y: 2, z: 4, core: 2. Of those that a mesh axis runs over, the one named last changes fastest.
Arguments:
- omega: bfloat16 [24576, 256], P(('grp', 'sub')), may hold values from -6 to 6
- adj_tests: bfloat16 [256, 24576], P('sub', 'grp'), may hold values from -6 to 6
- near_tiles: bfloat16 [192, 12, 128, 128], P(('grp', 'sub')), may hold values from -0.15625 to 0.15625
- tile_cols: int32 [192, 12], P(('grp', 'sub')), may hold values from 0 to 191, as said below
- leaf_perms: int32 [32, 2, 768], P(('grp', 'sub')), may hold values from 0 to 767, each once within a row
- leaf_interp: bfloat16 [32, 2, 672, 96], P(('grp', 'sub')), may hold values from -0.125 to 0.125
- node_perms: int32 [32, 5, 2, 192], P(('grp', 'sub')), may hold values from 0 to 191, as said below
- node_maps: bfloat16 [32, 5, 4, 96, 96], P(('grp', 'sub')), as said below
Outputs:
- path_panels: bfloat16 [32, 5, 2, 96, 256], P(('grp', 'sub'))
The draws below stay inside these ranges and needn't reach their ends.
Inputs may be any that keep to these rules, and one draw needn't show every extreme that they name: `tile_cols`: the 12 column tiles of tile row q are distinct and lie in the tile rows of its own leaf or of the leaves just before and after it within the same block of 16 leaves; each block of 16 leaves is one index of grp. `leaf_perms`: each of the two orders of a leaf is a permutation of 0 to 767. `node_perms`: each order is a permutation of 0 to 191; entries [d, j] are equal for all d with the same d // 2^(j+1). `node_maps`: entries [d, j] are equal for all d with the same d // 2^(j+1).
All inputs are finite; a program needn't handle non-finite values.
Results may differ from the reference program's by a relative error of at most 0.0065.
Values may be sent and summed in bfloat16 or wider, within the bound.
No kernel may reach another device: no remote copies, remote signals or barrier semaphores. Data moves between devices by JAX's collectives and lax.ppermute only.
A program may use at most 64 MiB of HBM per device.

```python
import math
import jax
import jax.numpy as jnp
from jax import lax

M = 768
TILE = 128
NT = 12
S = 256
K = 96
LEAVES = 32
NROWS = 24576
NROWT = 192
LEVX = 5
N_SUB = 16


def node_owner():
    return jnp.right_shift(jnp.arange(LEAVES, dtype=jnp.int32)[:, None], jnp.arange(LEVX, dtype=jnp.int32)[None, :] + 1)


def draw_tile_cols(key, part):
    per_dev = M // TILE
    span = 3 * per_dev
    rows = jnp.arange(NROWT, dtype=jnp.int32)
    device = rows // per_dev
    place = device % N_SUB
    slots = jnp.arange(span, dtype=jnp.int32)[None, :]
    valid = ((slots >= per_dev) | (place[:, None] > 0)) & ((slots < 2 * per_dev) | (place[:, None] < N_SUB - 1))
    scores = jax.random.randint(key, (NROWT, span), 0, 1 << 20, dtype=jnp.int32)
    ranked = scores * span + slots + jnp.where(valid, 0, 1 << 29)
    chosen = jnp.argsort(ranked, axis=1, stable=True)[:, :NT].astype(jnp.int32)
    return ((device[:, None] - 1) * per_dev + chosen).astype(jnp.int32)


def draw_node_perms(key, part):
    nodes = LEAVES // 2
    keys = jax.random.split(key, LEVX * nodes * 2)
    full = jax.vmap(lambda k: jax.random.permutation(k, 2 * K))(keys).reshape(LEVX, nodes, 2, 2 * K)
    return full[jnp.arange(LEVX, dtype=jnp.int32)[None, :], node_owner()].astype(jnp.int32)


def draw_node_maps(key, part):
    nodes = LEAVES // 2
    full = jax.random.normal(key, (LEVX, nodes, 4, K, K), jnp.float32)
    scales = jnp.array([0.35, 0.35, 0.5, 0.5], jnp.float32)[:, None, None] / math.sqrt(K)
    full = full * scales
    return full[jnp.arange(LEVX, dtype=jnp.int32)[None, :], node_owner()].astype(jnp.bfloat16)


def shard_levels(key, extent, cuts, low, largest):
    factor_of, own = 1.0, jax.random.fold_in(key, 6)
    for axis_at, parts in cuts:
        steps = jnp.exp(jax.random.uniform(jax.random.fold_in(own, axis_at), (parts,), jnp.float32, low / len(cuts), largest / len(cuts)))
        factor_of = factor_of * jnp.repeat(steps, extent[axis_at] // parts).reshape([-1 if axis == axis_at else 1 for axis in range(len(extent))])
    return factor_of


def centred(own_key, shape, scale, most, cuts=(), kind=jnp.bfloat16):
    values = jax.random.normal(own_key, shape, jnp.float32) * scale
    if len(cuts) > 0:
        values = shard_levels(own_key, shape, cuts, -0.22, 0.18) * values
    return jnp.clip(values, min=-most, max=most).astype(kind)


def setup_inputs(seed: int = 0) -> dict:
    arg_keys = jax.random.split(jax.random.key(seed), 9)
    return {
        "omega": centred(arg_keys[0], (NROWS, S), 1.0, 6.0, ((0, 32),)),
        "adj_tests": centred(arg_keys[1], (S, NROWS), 1.0, 6.0, ((0, 16), (1, 2))),
        "near_tiles": centred(arg_keys[2], (NROWT, NT, TILE, TILE), (NT * TILE) ** -0.5, 0.15625, ((0, 32),)),
        "tile_cols": draw_tile_cols(jax.random.fold_in(arg_keys[8], 71), 0),
        "leaf_perms": jax.vmap(lambda own: jax.random.permutation(own, M))(jax.random.split(arg_keys[4], LEAVES * 2)).reshape((LEAVES, 2, M)).astype(jnp.int32),
        "leaf_interp": centred(arg_keys[5], (LEAVES, 2, M - K, K), (4 * (M - K)) ** -0.5, 0.125, ((0, 32),)),
        "node_perms": draw_node_perms(jax.random.fold_in(arg_keys[8], 71), 0),
        "node_maps": draw_node_maps(jax.random.fold_in(arg_keys[8], 71), 0),
    }


HIGHEST = lax.Precision.HIGHEST


def apply_rows(matrix, panel):
    return jnp.einsum("...ij,...js->...is", matrix, panel, precision=HIGHEST)


def apply_cols(matrix, panel):
    return jnp.einsum("...ji,...js->...is", matrix, panel, precision=HIGHEST)


def pick_rows(panel, order):
    return jnp.take_along_axis(panel, order[..., None], axis=-2)


def squeeze_node(fwd_rows, fwd_tests, adj_rows, adj_panel, row_order, col_order, row_interp, col_interp):
    rank = row_interp.shape[-1]
    fwd_skel = pick_rows(fwd_rows, row_order[..., :rank])
    test_skel = pick_rows(fwd_tests, col_order[..., :rank]) + apply_cols(col_interp, pick_rows(fwd_tests, col_order[..., rank:]))
    adj_skel = pick_rows(adj_rows, col_order[..., :rank])
    adj_test_skel = pick_rows(adj_panel, row_order[..., :rank]) + apply_cols(row_interp, pick_rows(adj_panel, row_order[..., rank:]))
    return fwd_skel, test_skel, adj_skel, adj_test_skel


def merge_pair(lower, upper, maps, orders):
    maps = maps.astype(jnp.float32)
    row_interp = maps[..., 0, :, :]
    col_interp = maps[..., 1, :, :]
    low_high = maps[..., 2, :, :]
    high_low = maps[..., 3, :, :]
    fwd_rows = jnp.concatenate([lower[0] - apply_rows(low_high, upper[1]), upper[0] - apply_rows(high_low, lower[1])], axis=-2)
    fwd_tests = jnp.concatenate([lower[1], upper[1]], axis=-2)
    adj_rows = jnp.concatenate([lower[2] - apply_cols(high_low, upper[3]), upper[2] - apply_cols(low_high, lower[3])], axis=-2)
    adj_panel = jnp.concatenate([lower[3], upper[3]], axis=-2)
    return squeeze_node(fwd_rows, fwd_tests, adj_rows, adj_panel, orders[..., 0, :], orders[..., 1, :], row_interp, col_interp)


def reference(omega, adj_tests, near_tiles, tile_cols, leaf_perms, leaf_interp, node_perms, node_maps):
    per_dev = M // TILE
    omega_tiles = omega.reshape(NROWT, TILE, S)
    tiles_dev = near_tiles.reshape(LEAVES, per_dev, NT, TILE, TILE)
    cols_dev = tile_cols.reshape(LEAVES, per_dev, NT)

    def forward_one(inputs):
        tiles, cols = inputs
        picked = omega_tiles[cols].astype(jnp.float32)
        return jnp.einsum("rtij,rtjs->ris", tiles.astype(jnp.float32), picked, precision=HIGHEST).reshape(M, S)

    forward = lax.map(forward_one, (tiles_dev, cols_dev))
    adj_dev = adj_tests.reshape(S, LEAVES, per_dev, TILE).transpose(1, 0, 2, 3)

    def adjoint_one(total, inputs):
        tiles, cols, tests = inputs
        contrib = jnp.einsum("rtij,sri->rtjs", tiles.astype(jnp.float32), tests.astype(jnp.float32), precision=HIGHEST)
        return total.at[cols].add(contrib), None

    adjoint, _ = lax.scan(adjoint_one, jnp.zeros((NROWT, TILE, S), jnp.float32), (tiles_dev, cols_dev, adj_dev))
    adjoint = adjoint.reshape(LEAVES, M, S)
    omega_leaf = omega.reshape(LEAVES, M, S).astype(jnp.float32)
    adj_leaf = adj_tests.reshape(S, LEAVES, M).transpose(1, 2, 0).astype(jnp.float32)
    interp = leaf_interp.astype(jnp.float32)
    panels = squeeze_node(forward, omega_leaf, adjoint, adj_leaf, leaf_perms[:, 0], leaf_perms[:, 1], interp[:, 0], interp[:, 1])
    levels = []
    for level in range(LEVX):
        stride = 2 ** (level + 1)
        lower = tuple(x[0::2] for x in panels)
        upper = tuple(x[1::2] for x in panels)
        panels = merge_pair(lower, upper, node_maps[::stride, level], node_perms[::stride, level])
        levels.append(jnp.repeat(jnp.stack([panels[0], panels[2]], axis=1), stride, axis=0))
    return jnp.stack(levels, axis=1).astype(jnp.bfloat16)
```

```python
import functools

import jax
import jax.numpy as jnp
from jax import lax
from jax.experimental import pallas as pl
from jax.experimental.pallas import tpu as pltpu
from jax.sharding import PartitionSpec as P

BF = jnp.bfloat16
F32 = jnp.float32
VMEM = pl.BlockSpec(memory_space=pltpu.VMEM)
SMEM = pl.BlockSpec(memory_space=pltpu.SMEM)


def mm(a, b):
    return jnp.dot(a, b, preferred_element_type=F32)


def mm_t(a, b):
    return lax.dot_general(a, b, (((1,), (1,)), ((), ())), preferred_element_type=F32)


def eye(n):
    same = lax.broadcasted_iota(jnp.int32, (n, n), 0) == lax.broadcasted_iota(jnp.int32, (n, n), 1)
    return jnp.where(same, 1.0, 0.0).astype(BF)


def one_hot(order, n):
    hit = lax.broadcasted_iota(jnp.int32, (n, order.shape[1]), 0) == order
    return jnp.where(hit, 1.0, 0.0).astype(BF)


def call(body, out_shape, args, scratch=(), smem=0, limit=40 << 20, flops=0):
    nbytes = sum(a.size * a.dtype.itemsize for a in args)
    outs = out_shape if isinstance(out_shape, (list, tuple)) else [out_shape]
    return pl.pallas_call(
        body,
        out_shape=out_shape,
        in_specs=[SMEM] * smem + [VMEM] * (len(args) - smem),
        out_specs=jax.tree.map(lambda _: VMEM, out_shape),
        scratch_shapes=list(scratch),
        compiler_params=pltpu.CompilerParams(vmem_limit_bytes=limit),
        cost_estimate=pl.CostEstimate(
            flops=flops,
            bytes_accessed=nbytes + sum(o.size * o.dtype.itemsize for o in outs),
            transcendentals=0,
        ),
    )(*args)


def shape(dims, dtype=BF):
    return jax.ShapeDtypeStruct(dims, dtype)


def split_body(width, tests_ref, out_ref):
    for chip in range(out_ref.shape[0]):
        out_ref[chip] = tests_ref[:, chip * width : (chip + 1) * width]


def select_body(
    cols_ref, tiles_ref, own_ref, inner_ref, outer_ref, interp_ref, near_ref, tests_ref, adj_ref, dense_ref
):
    per_dev, slots, tile = tiles_ref.shape[:3]
    rows = per_dev * tile
    rank = interp_ref.shape[-1]
    core = lax.axis_index("sub") & 1
    first = (lax.axis_index("grp") * lax.axis_size("sub") + lax.axis_index("sub")) * per_dev
    dense_ref[...] = jnp.zeros_like(dense_ref)
    for q in range(per_dev):
        for t in range(slots):
            col = cols_ref[q, t] - first
            below, above = col < 0, col >= per_dev
            place = jnp.where(below, col + per_dev, jnp.where(above, col - per_dev, col))
            inner = jnp.where(core == 0, above, below)
            block = jnp.where(below | above, jnp.where(inner, 1, 2), 0)
            at = pl.multiple_of((block * per_dev + place) * tile, tile)
            dense_ref[q * tile : (q + 1) * tile, pl.ds(at, tile)] = tiles_ref[q, t]
    unit = eye(rank)
    row_hot = one_hot(own_ref[0, 0:1, :], rows)
    col_hot = one_hot(own_ref[0, 1:2, :], rows)
    row_all = mm(row_hot, jnp.concatenate([unit, interp_ref[0, 0]], axis=0)).astype(BF)
    col_all = mm(col_hot, jnp.concatenate([unit, interp_ref[0, 1]], axis=0)).astype(BF)
    tests_ref[...] = mm_t(unit, col_all).astype(BF)
    adj_ref[3 * rank :] = mm_t(unit, row_all).astype(BF)
    row_keep = mm_t(unit, row_hot[:, :rank]).astype(BF)
    near_ref[...] = mm(row_keep, dense_ref[...]).astype(BF)
    hots = (
        col_hot[:, :rank],
        one_hot(inner_ref[0, 1:2, :rank], rows),
        one_hot(outer_ref[0, 1:2, :rank], rows),
    )
    for b, hot in enumerate(hots):
        keep = mm_t(unit, hot).astype(BF)
        adj_ref[b * rank : (b + 1) * rank] = mm_t(keep, dense_ref[:, b * rows : (b + 1) * rows]).astype(BF)


def maps_body(maps_ref, perms_ref, *out_refs):
    rank = maps_ref.shape[-1]
    unit = eye(rank)
    for level, out_ref in enumerate(out_refs):
        row_interp, col_interp, low_high, high_low = (maps_ref[0, level, i] for i in range(4))
        row_hot = one_hot(perms_ref[0, level, 0:1, :], 2 * rank)
        col_hot = one_hot(perms_ref[0, level, 1:2, :], 2 * rank)
        row_all = mm(row_hot, jnp.concatenate([unit, row_interp], axis=0)).astype(BF)
        col_all = mm(col_hot, jnp.concatenate([unit, col_interp], axis=0)).astype(BF)
        for kind, (hot, every) in enumerate(((row_hot, col_all), (col_hot, row_all))):
            keep = [mm_t(unit, hot[side * rank : (side + 1) * rank, :rank]).astype(BF) for side in range(2)]
            if kind == 0:
                cross = [mm(keep[1], high_low), mm(keep[0], low_high)]
            else:
                cross = [mm_t(keep[1], low_high), mm_t(keep[0], high_low)]
            for side in range(2):
                out_ref[kind, side, :rank] = keep[side]
                out_ref[kind, side, rank : 2 * rank] = (-cross[side]).astype(BF)
                out_ref[kind, side, 2 * rank :] = mm_t(
                    unit, every[side * rank : (side + 1) * rank]
                ).astype(BF)


def forward_body(near_ref, tests_ref, own_ref, inner_ref, outer_ref, mine_ref, other_ref):
    rows = own_ref.shape[0]
    rank = near_ref.shape[0]
    half = own_ref.shape[1] // 2
    core = lax.axis_index("sub") & 1
    for out_ref, place in ((mine_ref, core), (other_ref, 1 - core)):
        cols = pl.ds(pl.multiple_of(place * half, half), half)
        own = own_ref[:, cols]
        fwd = (
            mm(near_ref[:, :rows], own)
            + mm(near_ref[:, rows : 2 * rows], inner_ref[:, cols])
            + mm(near_ref[:, 2 * rows :], outer_ref[:, cols])
        )
        out_ref[:rank] = fwd.astype(BF)
        out_ref[rank:] = mm(tests_ref[...], own).astype(BF)


def rim_place():
    sub = lax.axis_index("sub")
    return (sub & 1) != ((sub >> 1) & 1)


def adjoint_body(adj_ref, other_ref, panel_ref, mine_out, other_out, even_out, odd_out):
    rows = adj_ref.shape[1]
    rank = adj_ref.shape[0] // 4
    core = lax.axis_index("sub") & 1
    mine = mm_t(adj_ref[...], panel_ref[:, pl.ds(pl.multiple_of(core * rows, 128), rows)])
    other = mm_t(other_ref[...], panel_ref[:, pl.ds(pl.multiple_of((1 - core) * rows, 128), rows)])
    mine_out[:rank] = mine[:rank] + other[rank : 2 * rank]
    mine_out[rank:] = mine[3 * rank :]
    other_out[:rank] = other[:rank] + mine[rank : 2 * rank]
    other_out[rank:] = other[3 * rank :]
    mine_rim = mine[2 * rank : 3 * rank]
    other_rim = other[2 * rank : 3 * rank]
    even = rim_place()
    even_out[...] = jnp.where(even, mine_rim, other_rim).astype(BF)
    odd_out[...] = jnp.where(even, other_rim, mine_rim).astype(BF)


def merged(maps_ref, kind, side, mine_first, mine_second, other_first, other_second, rank):
    wide = mm(maps_ref[kind, side, rank:], mine_second) + mm(maps_ref[kind, 1 - side, rank:], other_second)
    kept = mm(maps_ref[kind, side, :rank], mine_first) + mm(maps_ref[kind, 1 - side, :rank], other_first)
    return kept + wide[:rank], wide[rank:]


def first_body(maps_ref, fwd_ref, fwd_other, adj_ref, adj_other, even_ref, odd_ref, out_ref):
    rank = even_ref.shape[0]
    core = lax.axis_index("sub") & 1
    kept, tests = merged(
        maps_ref, 0, core, fwd_ref[:rank], fwd_ref[rank:], fwd_other[:rank], fwd_other[rank:], rank
    )
    out_ref[0, :rank] = kept.astype(BF)
    out_ref[0, rank:] = tests.astype(BF)
    even = rim_place()
    from_even = even_ref[...].astype(F32)
    from_odd = odd_ref[...].astype(F32)
    mine = adj_ref[:rank] + jnp.where(even, from_even, from_odd)
    other = adj_other[:rank] + jnp.where(even, from_odd, from_even)
    kept, tests = merged(
        maps_ref,
        1,
        core,
        mine.astype(BF),
        adj_ref[rank:].astype(BF),
        other.astype(BF),
        adj_other[rank:].astype(BF),
        rank,
    )
    out_ref[1, :rank] = kept.astype(BF)
    out_ref[1, rank:] = tests.astype(BF)


def level_body(axis, bit, last, maps_ref, mine_ref, other_ref, out_ref):
    rank = mine_ref.shape[1] // 2
    side = (lax.axis_index(axis) >> bit) & 1
    for kind in range(2):
        kept, tests = merged(
            maps_ref,
            kind,
            side,
            mine_ref[kind, :rank],
            mine_ref[kind, rank:],
            other_ref[kind, :rank],
            other_ref[kind, rank:],
            rank,
        )
        out_ref[kind, :rank] = kept.astype(BF)
        if not last:
            out_ref[kind, rank:] = tests.astype(BF)


def collect_body(*refs):
    out_ref = refs[-1]
    rank = out_ref.shape[2]
    for level, ref in enumerate(refs[:-1]):
        out_ref[level] = ref[:, :rank]


def output_body(vectors, early_ref, early_other, late_ref, late_other, out_ref):
    levels = early_ref.shape[0]
    half = early_ref.shape[-1]
    core = lax.axis_index("sub") & 1
    k = lax.broadcasted_iota(jnp.int32, (half, 2 * half), 0)
    s = lax.broadcasted_iota(jnp.int32, (half, 2 * half), 1)
    base = k + k // vectors * vectors
    to_mine = jnp.where(s == base + core * vectors, 1.0, 0.0).astype(BF)
    to_other = jnp.where(s == base + (1 - core) * vectors, 1.0, 0.0).astype(BF)
    mine_cols = pl.ds(pl.multiple_of(core * half, half), half)
    other_cols = pl.ds(pl.multiple_of((1 - core) * half, half), half)
    for level in range(levels + 1):
        mine = early_ref[level] if level < levels else late_ref[...]
        other = early_other[level] if level < levels else late_other[...]
        out_ref[0, level, 0, :, mine_cols] = mine[0]
        out_ref[0, level, 0, :, other_cols] = other[0]
        out_ref[0, level, 1] = (mm(mine[1], to_mine) + mm(other[1], to_other)).astype(BF)


def swapped(x, axis, bit):
    return lax.ppermute(x, axis, [(i, i ^ (1 << bit)) for i in range(lax.axis_size(axis))])


def local(omega, adj_tests, near_tiles, tile_cols, leaf_perms, leaf_interp, node_perms, node_maps):
    rows, samples = omega.shape
    half = samples // 2
    vectors = adj_tests.shape[0]
    rank = leaf_interp.shape[-1]
    levels = node_maps.shape[1]
    count = lax.axis_size("sub")
    chips = count // 2
    sub_bits = count.bit_length() - 1
    outward = [(i, j) for i in range(1, count - 1, 2) for j in (i + 1,)]
    outward += [(j, i) for i, j in outward]

    blocks = call(
        functools.partial(split_body, 2 * rows), shape((chips, vectors, 2 * rows)), (adj_tests,)
    )
    groups = [[2 * m + c for m in range(chips)] for c in range(2)]
    panel = lax.all_to_all(
        blocks, "sub", split_axis=0, concat_axis=0, tiled=True, axis_index_groups=groups
    ).reshape(half, 2 * rows)

    perms_inner = swapped(leaf_perms, "sub", 0)
    perms_outer = lax.ppermute(leaf_perms, "sub", outward)
    omega_inner = swapped(omega, "sub", 0)
    omega_outer = lax.ppermute(omega, "sub", outward)
    near, tests, adj = call(
        select_body,
        [shape((rank, 3 * rows)), shape((rank, rows)), shape((4 * rank, rows))],
        (tile_cols, near_tiles, leaf_perms, perms_inner, perms_outer, leaf_interp),
        scratch=[pltpu.VMEM((rows, 3 * rows), BF)],
        smem=1,
        flops=8 * rank * rows * rows * 2,
    )
    adj_other = swapped(adj, "sub", 0)
    maps = call(maps_body, [shape((2, 2, 3 * rank, rank))] * levels, (node_maps, node_perms))
    fwd_mine, fwd_send = call(
        forward_body,
        [shape((2 * rank, half))] * 2,
        (near, tests, omega, omega_inner, omega_outer),
        flops=4 * rank * rows * samples * 2,
    )
    fwd_other = swapped(fwd_send, "sub", 0)

    adj_leaf, adj_leaf_other, even_rim, odd_rim = call(
        adjoint_body,
        [shape((2 * rank, half), F32)] * 2 + [shape((rank, half))] * 2,
        (adj, adj_other, panel),
    )
    even_rim = swapped(even_rim, "sub", 1)
    beside = [(2 * i + c, 2 * i + 2 + c) for i in range(1, chips - 1, 2) for c in range(2)]
    odd_rim = lax.ppermute(odd_rim, "sub", beside + [(j, i) for i, j in beside])
    x = call(
        first_body,
        shape((2, 2 * rank, half)),
        (maps[0], fwd_mine, fwd_other, adj_leaf, adj_leaf_other, even_rim, odd_rim),
    )
    nodes = [x]
    steps = [("sub", bit) for bit in range(1, sub_bits)]
    steps += [("grp", bit) for bit in range(levels - sub_bits)]
    for level, (axis, bit) in enumerate(steps, 1):
        last = level == levels - 1
        x = call(
            functools.partial(level_body, axis, bit, last),
            shape((2, rank if last else 2 * rank, half)),
            (maps[level], x, swapped(x, axis, bit)),
        )
        nodes.append(x)
    early = call(collect_body, shape((levels - 1, 2, rank, half)), nodes[:-1])
    early_other = swapped(early, "sub", 0)
    late_other = swapped(x, "sub", 0)
    return call(
        functools.partial(output_body, vectors),
        shape((1, levels, 2, rank, samples)),
        (early, early_other, x, late_other),
    )


def solution(mesh):
    both = ("grp", "sub")
    return jax.shard_map(
        local,
        mesh=mesh,
        in_specs=(
            P(both, None),
            P("sub", "grp"),
            P(both, None, None, None),
            P(both, None),
            P(both, None, None),
            P(both, None, None, None),
            P(both, None, None, None),
            P(both, None, None, None, None),
        ),
        out_specs=P(both, None, None, None, None),
        check_vma=False,
    )
```

```python
import functools

import jax
import jax.numpy as jnp
from jax import lax
from jax.experimental import pallas as pl
from jax.experimental.pallas import tpu as pltpu
from jax.sharding import PartitionSpec as P

BF = jnp.bfloat16
F32 = jnp.float32
VMEM = pl.BlockSpec(memory_space=pltpu.VMEM)
SMEM = pl.BlockSpec(memory_space=pltpu.SMEM)


def mm(a, b):
    return jnp.dot(a, b, preferred_element_type=F32)


def mm_t(a, b):
    return lax.dot_general(a, b, (((1,), (1,)), ((), ())), preferred_element_type=F32)


def eye(n):
    same = lax.broadcasted_iota(jnp.int32, (n, n), 0) == lax.broadcasted_iota(jnp.int32, (n, n), 1)
    return jnp.where(same, 1.0, 0.0).astype(BF)


def one_hot(order, n):
    hit = lax.broadcasted_iota(jnp.int32, (n, order.shape[1]), 0) == order
    return jnp.where(hit, 1.0, 0.0).astype(BF)


def call(body, out_shape, args, scratch=(), smem=0, anywhere=False, limit=40 << 20):
    space = pl.BlockSpec(memory_space=pl.ANY) if anywhere else VMEM
    return pl.pallas_call(
        body,
        out_shape=out_shape,
        in_specs=[SMEM] * smem + [space] * (len(args) - smem),
        out_specs=jax.tree.map(lambda _: space, out_shape),
        scratch_shapes=list(scratch),
        compiler_params=pltpu.CompilerParams(vmem_limit_bytes=limit),
        cost_estimate=pl.CostEstimate(flops=1000, bytes_accessed=1000, transcendentals=0),
    )(*args)


def shape(dims, dtype=BF):
    return jax.ShapeDtypeStruct(dims, dtype)


def split_body(width, tests_ref, out_ref, sems):
    copies = [
        pltpu.make_async_copy(
            tests_ref.at[:, chip * width : (chip + 1) * width], out_ref.at[chip], sems.at[chip]
        )
        for chip in range(out_ref.shape[0])
    ]
    for copy in copies:
        copy.start()
    for copy in copies:
        copy.wait()


def select_body(
    cols_ref,
    tiles_ref,
    own_ref,
    inner_ref,
    outer_ref,
    interp_ref,
    omega_ref,
    omega_inner,
    omega_outer,
    adj_ref,
    mine_ref,
    other_ref,
    dense_ref,
):
    per_dev, slots, tile = tiles_ref.shape[:3]
    rows = per_dev * tile
    rank = interp_ref.shape[-2]
    core = lax.axis_index("sub") & 1
    first = (lax.axis_index("grp") * lax.axis_size("sub") + lax.axis_index("sub")) * per_dev
    dense_ref[...] = jnp.zeros_like(dense_ref)
    for q in range(per_dev):
        for t in range(slots):
            col = cols_ref[q, t] - first
            below, above = col < 0, col >= per_dev
            place = jnp.where(below, col + per_dev, jnp.where(above, col - per_dev, col))
            inner = jnp.where(core == 0, above, below)
            block = jnp.where(below | above, jnp.where(inner, 1, 2), 0)
            at = pl.multiple_of((block * per_dev + place) * tile, tile)
            dense_ref[q * tile : (q + 1) * tile, pl.ds(at, tile)] = tiles_ref[q, t]
    unit = eye(rank)
    keeps = []
    for i in range(2):
        keep = mm_t(unit, one_hot(own_ref[0, i : i + 1, :rank], rows))
        rest = one_hot(own_ref[0, i : i + 1, rank:], rows)
        every = (keep + mm_t(interp_ref[0, i], rest)).astype(BF)
        keeps.append(keep.astype(BF))
        if i == 0:
            adj_ref[3 * rank :] = every
        else:
            tests = every
    keeps += [
        mm_t(unit, one_hot(ref[0, 1:2, :rank], rows)).astype(BF) for ref in (inner_ref, outer_ref)
    ]
    for b, keep in enumerate(keeps[1:]):
        adj_ref[b * rank : (b + 1) * rank] = mm_t(keep, dense_ref[:, b * rows : (b + 1) * rows]).astype(BF)
    near = mm(keeps[0], dense_ref[...]).astype(BF)
    half = omega_ref.shape[1] // 2
    for out_ref, place in ((mine_ref, core), (other_ref, 1 - core)):
        cols = pl.ds(pl.multiple_of(place * half, half), half)
        own = omega_ref[:, cols]
        fwd = (
            mm(near[:, :rows], own)
            + mm(near[:, rows : 2 * rows], omega_inner[:, cols])
            + mm(near[:, 2 * rows :], omega_outer[:, cols])
        )
        out_ref[:rank] = fwd.astype(BF)
        out_ref[rank:] = mm(tests, own).astype(BF)


def maps_body(maps_ref, perms_ref, *out_refs):
    rank = maps_ref.shape[-1]
    unit = eye(rank)
    for level, out_ref in enumerate(out_refs):
        row_interp, col_interp, low_high, high_low = (maps_ref[0, level, i] for i in range(4))
        row_hot = one_hot(perms_ref[0, level, 0:1, :], 2 * rank)
        col_hot = one_hot(perms_ref[0, level, 1:2, :], 2 * rank)
        row_all = mm(row_hot, jnp.concatenate([unit, row_interp], axis=0)).astype(BF)
        col_all = mm(col_hot, jnp.concatenate([unit, col_interp], axis=0)).astype(BF)
        for kind, (hot, every) in enumerate(((row_hot, col_all), (col_hot, row_all))):
            keep = [mm_t(unit, hot[side * rank : (side + 1) * rank, :rank]).astype(BF) for side in range(2)]
            if kind == 0:
                cross = [mm(keep[1], high_low), mm(keep[0], low_high)]
            else:
                cross = [mm_t(keep[1], low_high), mm_t(keep[0], high_low)]
            for side in range(2):
                out_ref[kind, side, :rank] = keep[side]
                out_ref[kind, side, rank : 2 * rank] = (-cross[side]).astype(BF)
                out_ref[kind, side, 2 * rank :] = mm_t(
                    unit, every[side * rank : (side + 1) * rank]
                ).astype(BF)


def rim_place():
    sub = lax.axis_index("sub")
    return (sub & 1) != ((sub >> 1) & 1)


def adjoint_body(adj_ref, other_ref, panel_ref, mine_out, other_out, even_out, odd_out):
    rows = adj_ref.shape[1]
    rank = adj_ref.shape[0] // 4
    core = lax.axis_index("sub") & 1
    mine = mm_t(adj_ref[...], panel_ref[:, pl.ds(pl.multiple_of(core * rows, 128), rows)])
    other = mm_t(other_ref[...], panel_ref[:, pl.ds(pl.multiple_of((1 - core) * rows, 128), rows)])
    mine_out[:rank] = mine[:rank] + other[rank : 2 * rank]
    mine_out[rank:] = mine[3 * rank :]
    other_out[:rank] = other[:rank] + mine[rank : 2 * rank]
    other_out[rank:] = other[3 * rank :]
    mine_rim = mine[2 * rank : 3 * rank]
    other_rim = other[2 * rank : 3 * rank]
    even = rim_place()
    even_out[...] = jnp.where(even, mine_rim, other_rim).astype(BF)
    odd_out[...] = jnp.where(even, other_rim, mine_rim).astype(BF)


def merged(maps_ref, kind, side, mine_first, mine_second, other_first, other_second, rank):
    wide = mm(maps_ref[kind, side, rank:], mine_second) + mm(maps_ref[kind, 1 - side, rank:], other_second)
    kept = mm(maps_ref[kind, side, :rank], mine_first) + mm(maps_ref[kind, 1 - side, :rank], other_first)
    return kept + wide[:rank], wide[rank:]


def first_body(maps_ref, fwd_ref, fwd_other, adj_ref, adj_other, even_ref, odd_ref, out_ref):
    rank = even_ref.shape[0]
    core = lax.axis_index("sub") & 1
    kept, tests = merged(
        maps_ref, 0, core, fwd_ref[:rank], fwd_ref[rank:], fwd_other[:rank], fwd_other[rank:], rank
    )
    out_ref[0, :rank] = kept.astype(BF)
    out_ref[0, rank:] = tests.astype(BF)
    even = rim_place()
    from_even = even_ref[...].astype(F32)
    from_odd = odd_ref[...].astype(F32)
    mine = adj_ref[:rank] + jnp.where(even, from_even, from_odd)
    other = adj_other[:rank] + jnp.where(even, from_odd, from_even)
    kept, tests = merged(
        maps_ref,
        1,
        core,
        mine.astype(BF),
        adj_ref[rank:].astype(BF),
        other.astype(BF),
        adj_other[rank:].astype(BF),
        rank,
    )
    out_ref[1, :rank] = kept.astype(BF)
    out_ref[1, rank:] = tests.astype(BF)


def level_body(axis, bit, last, maps_ref, mine_ref, other_ref, *refs):
    rank = mine_ref.shape[1] // 2
    side = (lax.axis_index(axis) >> bit) & 1
    out_ref = refs[-1]
    if last:
        for level, ref in enumerate((*refs[:-1], mine_ref)):
            out_ref[level] = ref[:, :rank]
    for kind in range(2):
        kept, tests = merged(
            maps_ref,
            kind,
            side,
            mine_ref[kind, :rank],
            mine_ref[kind, rank:],
            other_ref[kind, :rank],
            other_ref[kind, rank:],
            rank,
        )
        if last:
            out_ref[len(refs), kind] = kept.astype(BF)
        else:
            out_ref[kind, :rank] = kept.astype(BF)
            out_ref[kind, rank:] = tests.astype(BF)


def output_body(vectors, mine_ref, other_ref, out_ref):
    half = mine_ref.shape[-1]
    core = lax.axis_index("sub") & 1
    k = lax.broadcasted_iota(jnp.int32, (half, 2 * half), 0)
    s = lax.broadcasted_iota(jnp.int32, (half, 2 * half), 1)
    base = k + k // vectors * vectors
    to_mine = jnp.where(s == base + core * vectors, 1.0, 0.0).astype(BF)
    to_other = jnp.where(s == base + (1 - core) * vectors, 1.0, 0.0).astype(BF)
    mine_cols = pl.ds(pl.multiple_of(core * half, half), half)
    other_cols = pl.ds(pl.multiple_of((1 - core) * half, half), half)
    for level in range(mine_ref.shape[0]):
        mine, other = mine_ref[level], other_ref[level]
        out_ref[0, level, 0, :, mine_cols] = mine[0]
        out_ref[0, level, 0, :, other_cols] = other[0]
        out_ref[0, level, 1] = (mm(mine[1], to_mine) + mm(other[1], to_other)).astype(BF)


def swapped(x, axis, bit):
    return lax.ppermute(x, axis, [(i, i ^ (1 << bit)) for i in range(lax.axis_size(axis))])


def local(omega, adj_tests, near_tiles, tile_cols, leaf_perms, leaf_interp, node_perms, node_maps):
    rows, samples = omega.shape
    half = samples // 2
    vectors = adj_tests.shape[0]
    rank = leaf_interp.shape[-1]
    levels = node_maps.shape[1]
    count = lax.axis_size("sub")
    chips = count // 2
    sub_bits = count.bit_length() - 1
    outward = [(i, j) for i in range(1, count - 1, 2) for j in (i + 1,)]
    outward += [(j, i) for i, j in outward]

    blocks = call(
        functools.partial(split_body, 2 * rows), shape((chips, vectors, 2 * rows)), (adj_tests,),
        scratch=[pltpu.SemaphoreType.DMA((chips,))], anywhere=True,
    )
    groups = [[2 * m + c for m in range(chips)] for c in range(2)]
    panel = lax.all_to_all(
        blocks, "sub", split_axis=0, concat_axis=0, tiled=True, axis_index_groups=groups
    ).reshape(half, 2 * rows)

    omega_outer = lax.ppermute(omega, "sub", outward)
    omega_inner = swapped(omega, "sub", 0)
    perms_outer = lax.ppermute(leaf_perms, "sub", outward)
    perms_inner = swapped(leaf_perms, "sub", 0)
    adj, fwd_mine, fwd_send = call(
        select_body,
        [shape((4 * rank, rows))] + [shape((2 * rank, half))] * 2,
        (
            tile_cols,
            near_tiles,
            leaf_perms,
            perms_inner,
            perms_outer,
            jnp.swapaxes(leaf_interp, 2, 3),
            omega,
            omega_inner,
            omega_outer,
        ),
        scratch=[pltpu.VMEM((rows, 3 * rows), BF)],
        smem=1,
    )
    adj_other = swapped(adj, "sub", 0)
    maps = call(maps_body, [shape((2, 2, 3 * rank, rank))] * levels, (node_maps, node_perms))
    fwd_other = swapped(fwd_send, "sub", 0)

    adj_leaf, adj_leaf_other, even_rim, odd_rim = call(
        adjoint_body,
        [shape((2 * rank, half), F32)] * 2 + [shape((rank, half))] * 2,
        (adj, adj_other, panel),
    )
    even_rim = swapped(even_rim, "sub", 1)
    beside = [(2 * i + c, 2 * i + 2 + c) for i in range(1, chips - 1, 2) for c in range(2)]
    odd_rim = lax.ppermute(odd_rim, "sub", beside + [(j, i) for i, j in beside])
    x = call(
        first_body,
        shape((2, 2 * rank, half)),
        (maps[0], fwd_mine, fwd_other, adj_leaf, adj_leaf_other, even_rim, odd_rim),
    )
    nodes = []
    steps = [("sub", bit) for bit in range(1, sub_bits)]
    steps += [("grp", bit) for bit in range(levels - sub_bits)]
    for level, (axis, bit) in enumerate(steps, 1):
        last = level == levels - 1
        new = call(
            functools.partial(level_body, axis, bit, last),
            shape((levels, 2, rank, half) if last else (2, 2 * rank, half)),
            (maps[level], x, swapped(x, axis, bit), *(nodes if last else ())),
        )
        nodes.append(x)
        x = new
    return call(
        functools.partial(output_body, vectors),
        shape((1, levels, 2, rank, samples)),
        (x, swapped(x, "sub", 0)),
    )


def solution(mesh):
    both = ("grp", "sub")
    return jax.shard_map(
        local,
        mesh=mesh,
        in_specs=(
            P(both, None),
            P("sub", "grp"),
            P(both, None, None, None),
            P(both, None),
            P(both, None, None),
            P(both, None, None, None),
            P(both, None, None, None),
            P(both, None, None, None, None),
        ),
        out_specs=P(both, None, None, None, None),
        check_vma=False,
    )
```

```python
import functools

import jax
import jax.numpy as jnp
from jax import lax
from jax.experimental import pallas as pl
from jax.experimental.pallas import tpu as pltpu
from jax.sharding import PartitionSpec as P

BF = jnp.bfloat16
F32 = jnp.float32
SPACES = {
    "h": pl.BlockSpec(memory_space=pltpu.HBM),
    "a": pl.BlockSpec(memory_space=pl.ANY),
    "v": pl.BlockSpec(memory_space=pltpu.VMEM),
}


def mm(a, b):
    return jnp.dot(a, b, preferred_element_type=F32)


def mm_t(a, b):
    return lax.dot_general(a, b, (((1,), (1,)), ((), ())), preferred_element_type=F32)


def eye(n):
    same = lax.broadcasted_iota(jnp.int32, (n, n), 0) == lax.broadcasted_iota(jnp.int32, (n, n), 1)
    return jnp.where(same, 1.0, 0.0).astype(BF)


def one_hot(order, n):
    hit = lax.broadcasted_iota(jnp.int32, (n, order.shape[1]), 0) == order
    return jnp.where(hit, 1.0, 0.0).astype(BF)


def call(body, out_shape, args, scratch=(), specs=None, out="v", limit=40 << 20, flops=1000):
    return pl.pallas_call(
        body,
        out_shape=out_shape,
        in_specs=[SPACES[c] for c in specs or "v" * len(args)],
        out_specs=jax.tree.map(lambda _: SPACES[out], out_shape),
        scratch_shapes=list(scratch),
        compiler_params=pltpu.CompilerParams(vmem_limit_bytes=limit),
        cost_estimate=pl.CostEstimate(flops=flops, bytes_accessed=1000, transcendentals=0),
    )(*args)


def shape(dims, dtype=BF):
    return jax.ShapeDtypeStruct(dims, dtype)


DIGIT = 32


def pack_body(width, tests_ref, omega_ref, perms_ref, out_ref, packed_ref, order_ref, sems):
    rows, cols = omega_ref.shape
    chips = out_ref.shape[0]
    copies = [pltpu.make_async_copy(omega_ref, packed_ref.at[:rows], sems.at[chips])]
    for chip in range(chips):
        copies.append(
            pltpu.make_async_copy(
                tests_ref.at[:, chip * width : (chip + 1) * width], out_ref.at[chip], sems.at[chip]
            )
        )
    for copy in copies:
        copy.start()
    order = perms_ref[0, 1:2, :cols]
    row = lax.broadcasted_iota(jnp.int32, order_ref.shape, 0)
    digits = jnp.where(row == 0, order // DIGIT, jnp.where(row == 1, order % DIGIT, 0))
    order_ref[...] = digits.astype(F32).astype(BF)
    copies.append(pltpu.make_async_copy(order_ref, packed_ref.at[rows:], sems.at[chips + 1]))
    copies[-1].start()
    for copy in copies:
        copy.wait()


def select_body(
    cols_hbm,
    tiles_hbm,
    perms_hbm,
    interp_hbm,
    omega_hbm,
    inner_hbm,
    outer_hbm,
    after_hbm,
    adj_ref,
    mine_ref,
    other_ref,
    dense_ref,
    cols_ref,
    perms_ref,
    interp_ref,
    omega_ref,
    inner_ref,
    outer_ref,
    sems,
):
    del after_hbm
    per_dev, slots, tile = tiles_hbm.shape[:3]
    rows = per_dev * tile
    rank = interp_ref.shape[-2]
    half = omega_ref.shape[1] // 2
    core = lax.axis_index("sub") & 1
    first = (lax.axis_index("grp") * lax.axis_size("sub") + lax.axis_index("sub")) * per_dev
    pairs = (
        (cols_hbm, cols_ref),
        (perms_hbm, perms_ref),
        (interp_hbm, interp_ref),
        (inner_hbm, inner_ref),
        (outer_hbm, outer_ref),
        (omega_hbm, omega_ref),
    )
    copies = [pltpu.make_async_copy(a, b, sems.at[i]) for i, (a, b) in enumerate(pairs)]
    for copy in copies:
        copy.start()
    dense_ref[...] = jnp.zeros_like(dense_ref)
    moves = []
    copies[0].wait()
    for q in range(per_dev):
        for t in range(slots):
            col = cols_ref[q, t] - first
            below, above = col < 0, col >= per_dev
            place = jnp.where(below, col + per_dev, jnp.where(above, col - per_dev, col))
            inner = jnp.where(core == 0, above, below)
            block = jnp.where(below | above, jnp.where(inner, 1, 2), 0)
            at = pl.multiple_of((block * per_dev + place) * tile, tile)
            move = pltpu.make_async_copy(
                tiles_hbm.at[q, t],
                dense_ref.at[q * tile : (q + 1) * tile, pl.ds(at, tile)],
                sems.at[len(pairs) + q * slots + t],
            )
            move.start()
            moves.append(move)
    unit = eye(rank)
    keeps = []
    for copy in copies[1:3]:
        copy.wait()
    for i in range(2):
        keep = mm_t(unit, one_hot(perms_ref[0, i : i + 1, :rank], rows))
        rest = one_hot(perms_ref[0, i : i + 1, rank:], rows)
        every = (keep + mm_t(interp_ref[0, i], rest)).astype(BF)
        keeps.append(keep.astype(BF))
        if i == 0:
            adj_ref[3 * rank :] = every
        else:
            tests = every
    for copy in copies[3:]:
        copy.wait()
    for ref in (inner_ref, outer_ref):
        digits = ref[rows:].astype(F32)
        order = (digits[0:1, :rank] * DIGIT + digits[1:2, :rank]).astype(jnp.int32)
        keeps.append(mm_t(unit, one_hot(order, rows)).astype(BF))
    for move in moves:
        move.wait()
    for b, keep in enumerate(keeps[1:]):
        adj_ref[b * rank : (b + 1) * rank] = mm_t(keep, dense_ref[:, b * rows : (b + 1) * rows]).astype(BF)
    near = mm(keeps[0], dense_ref[...]).astype(BF)
    for out_ref, place in ((mine_ref, core), (other_ref, 1 - core)):
        cols = pl.ds(pl.multiple_of(place * half, half), half)
        own = omega_ref[:, cols]
        fwd = (
            mm(near[:, :rows], own)
            + mm(near[:, rows : 2 * rows], inner_ref[:rows, cols])
            + mm(near[:, 2 * rows :], outer_ref[:rows, cols])
        )
        out_ref[:rank] = fwd.astype(BF)
        out_ref[rank:] = mm(tests, own).astype(BF)


def maps_body(maps_ref, perms_ref, *out_refs):
    rank = maps_ref.shape[-1]
    unit = eye(rank)
    for level, out_ref in enumerate(out_refs):
        row_interp, col_interp, low_high, high_low = (maps_ref[0, level, i] for i in range(4))
        row_hot = one_hot(perms_ref[0, level, 0:1, :], 2 * rank)
        col_hot = one_hot(perms_ref[0, level, 1:2, :], 2 * rank)
        row_all = mm(row_hot, jnp.concatenate([unit, row_interp], axis=0)).astype(BF)
        col_all = mm(col_hot, jnp.concatenate([unit, col_interp], axis=0)).astype(BF)
        for kind, (hot, every) in enumerate(((row_hot, col_all), (col_hot, row_all))):
            keep = [mm_t(unit, hot[side * rank : (side + 1) * rank, :rank]).astype(BF) for side in range(2)]
            if kind == 0:
                cross = [mm(keep[1], high_low), mm(keep[0], low_high)]
            else:
                cross = [mm_t(keep[1], low_high), mm_t(keep[0], high_low)]
            for side in range(2):
                out_ref[kind, side, :rank] = keep[side]
                out_ref[kind, side, rank : 2 * rank] = (-cross[side]).astype(BF)
                out_ref[kind, side, 2 * rank :] = mm_t(
                    unit, every[side * rank : (side + 1) * rank]
                ).astype(BF)


def rim_place():
    sub = lax.axis_index("sub")
    return (sub & 1) != ((sub >> 1) & 1)


def adjoint_body(adj_ref, other_ref, panel_ref, mine_out, other_out, even_out, odd_out):
    rows = adj_ref.shape[1]
    rank = adj_ref.shape[0] // 4
    core = lax.axis_index("sub") & 1
    mine = mm_t(adj_ref[...], panel_ref[:, pl.ds(pl.multiple_of(core * rows, 128), rows)])
    other = mm_t(other_ref[...], panel_ref[:, pl.ds(pl.multiple_of((1 - core) * rows, 128), rows)])
    mine_out[:rank] = mine[:rank] + other[rank : 2 * rank]
    mine_out[rank:] = mine[3 * rank :]
    other_out[:rank] = other[:rank] + mine[rank : 2 * rank]
    other_out[rank:] = other[3 * rank :]
    mine_rim = mine[2 * rank : 3 * rank]
    other_rim = other[2 * rank : 3 * rank]
    even = rim_place()
    even_out[...] = jnp.where(even, mine_rim, other_rim).astype(BF)
    odd_out[...] = jnp.where(even, other_rim, mine_rim).astype(BF)


def merged(maps_ref, kind, side, mine_first, mine_second, other_first, other_second, rank):
    wide = mm(maps_ref[kind, side, rank:], mine_second) + mm(maps_ref[kind, 1 - side, rank:], other_second)
    kept = mm(maps_ref[kind, side, :rank], mine_first) + mm(maps_ref[kind, 1 - side, :rank], other_first)
    return kept + wide[:rank], wide[rank:]


def first_body(maps_ref, fwd_ref, fwd_other, adj_ref, adj_other, even_ref, odd_ref, out_ref):
    rank = even_ref.shape[0]
    core = lax.axis_index("sub") & 1
    kept, tests = merged(
        maps_ref, 0, core, fwd_ref[:rank], fwd_ref[rank:], fwd_other[:rank], fwd_other[rank:], rank
    )
    out_ref[0, :rank] = kept.astype(BF)
    out_ref[0, rank:] = tests.astype(BF)
    even = rim_place()
    from_even = even_ref[...].astype(F32)
    from_odd = odd_ref[...].astype(F32)
    mine = adj_ref[:rank] + jnp.where(even, from_even, from_odd)
    other = adj_other[:rank] + jnp.where(even, from_odd, from_even)
    kept, tests = merged(
        maps_ref,
        1,
        core,
        mine.astype(BF),
        adj_ref[rank:].astype(BF),
        other.astype(BF),
        adj_other[rank:].astype(BF),
        rank,
    )
    out_ref[1, :rank] = kept.astype(BF)
    out_ref[1, rank:] = tests.astype(BF)


def level_body(axis, bit, last, maps_ref, mine_ref, other_ref, *refs):
    rank = mine_ref.shape[1] // 2
    side = (lax.axis_index(axis) >> bit) & 1
    out_ref = refs[-1]
    if last:
        for level, ref in enumerate((*refs[:-1], mine_ref)):
            out_ref[level] = ref[:, :rank]
    for kind in range(2):
        kept, tests = merged(
            maps_ref,
            kind,
            side,
            mine_ref[kind, :rank],
            mine_ref[kind, rank:],
            other_ref[kind, :rank],
            other_ref[kind, rank:],
            rank,
        )
        if last:
            out_ref[len(refs), kind] = kept.astype(BF)
        else:
            out_ref[kind, :rank] = kept.astype(BF)
            out_ref[kind, rank:] = tests.astype(BF)


def output_body(vectors, mine_ref, other_ref, out_ref):
    half = mine_ref.shape[-1]
    core = lax.axis_index("sub") & 1
    k = lax.broadcasted_iota(jnp.int32, (half, 2 * half), 0)
    s = lax.broadcasted_iota(jnp.int32, (half, 2 * half), 1)
    base = k + k // vectors * vectors
    to_mine = jnp.where(s == base + core * vectors, 1.0, 0.0).astype(BF)
    to_other = jnp.where(s == base + (1 - core) * vectors, 1.0, 0.0).astype(BF)
    mine_cols = pl.ds(pl.multiple_of(core * half, half), half)
    other_cols = pl.ds(pl.multiple_of((1 - core) * half, half), half)
    for level in range(mine_ref.shape[0]):
        mine, other = mine_ref[level], other_ref[level]
        out_ref[0, level, 0, :, mine_cols] = mine[0]
        out_ref[0, level, 0, :, other_cols] = other[0]
        out_ref[0, level, 1] = (mm(mine[1], to_mine) + mm(other[1], to_other)).astype(BF)


def swapped(x, axis, bit):
    return lax.ppermute(x, axis, [(i, i ^ (1 << bit)) for i in range(lax.axis_size(axis))])


def local(omega, adj_tests, near_tiles, tile_cols, leaf_perms, leaf_interp, node_perms, node_maps):
    rows, samples = omega.shape
    half = samples // 2
    vectors = adj_tests.shape[0]
    rank = leaf_interp.shape[-1]
    levels = node_maps.shape[1]
    count = lax.axis_size("sub")
    chips = count // 2
    sub_bits = count.bit_length() - 1
    outward = [(i, j) for i in range(1, count - 1, 2) for j in (i + 1,)]
    outward += [(j, i) for i, j in outward]

    blocks, packed = call(
        functools.partial(pack_body, 2 * rows),
        [shape((chips, vectors, 2 * rows)), shape((rows + 16, samples))],
        (adj_tests, omega, leaf_perms),
        scratch=[pltpu.VMEM((16, samples), BF), pltpu.SemaphoreType.DMA((chips + 2,))],
        specs="hhv",
        out="a",
        limit=56 << 20,
    )
    packed_outer = lax.ppermute(packed, "sub", outward)
    packed_inner = swapped(packed, "sub", 0)
    groups = [[2 * m + c for m in range(chips)] for c in range(2)]
    panel = lax.all_to_all(
        blocks, "sub", split_axis=0, concat_axis=0, tiled=True, axis_index_groups=groups
    ).reshape(half, 2 * rows)

    maps = call(
        maps_body,
        [shape((2, 2, 3 * rank, rank))] * levels,
        (node_maps, node_perms),
        flops=4 << 30,
    )
    interp = jnp.swapaxes(leaf_interp, 2, 3)
    adj, fwd_mine, fwd_send = call(
        select_body,
        [shape((4 * rank, rows))] + [shape((2 * rank, half))] * 2,
        (tile_cols, near_tiles, leaf_perms, interp, omega, packed_inner, packed_outer, maps[0]),
        scratch=[
            pltpu.VMEM((rows, 3 * rows), BF),
            pltpu.SMEM(tile_cols.shape, jnp.int32),
            pltpu.VMEM(leaf_perms.shape, jnp.int32),
            pltpu.VMEM(interp.shape, BF),
            pltpu.VMEM(omega.shape, BF),
            pltpu.VMEM(packed.shape, BF),
            pltpu.VMEM(packed.shape, BF),
            pltpu.SemaphoreType.DMA((6 + near_tiles.shape[0] * near_tiles.shape[1],)),
        ],
        specs="hhhhhaaa",
    )
    adj_other = swapped(adj, "sub", 0)
    fwd_other = swapped(fwd_send, "sub", 0)

    adj_leaf, adj_leaf_other, even_rim, odd_rim = call(
        adjoint_body,
        [shape((2 * rank, half), F32)] * 2 + [shape((rank, half))] * 2,
        (adj, adj_other, panel),
    )
    even_rim = swapped(even_rim, "sub", 1)
    beside = [(2 * i + c, 2 * i + 2 + c) for i in range(1, chips - 1, 2) for c in range(2)]
    odd_rim = lax.ppermute(odd_rim, "sub", beside + [(j, i) for i, j in beside])
    x = call(
        first_body,
        shape((2, 2 * rank, half)),
        (maps[0], fwd_mine, fwd_other, adj_leaf, adj_leaf_other, even_rim, odd_rim),
    )
    nodes = []
    steps = [("sub", bit) for bit in range(1, sub_bits)]
    steps += [("grp", bit) for bit in range(levels - sub_bits)]
    for level, (axis, bit) in enumerate(steps, 1):
        last = level == levels - 1
        new = call(
            functools.partial(level_body, axis, bit, last),
            shape((levels, 2, rank, half) if last else (2, 2 * rank, half)),
            (maps[level], x, swapped(x, axis, bit), *(nodes if last else ())),
        )
        nodes.append(x)
        x = new
    return call(
        functools.partial(output_body, vectors),
        shape((1, levels, 2, rank, samples)),
        (x, swapped(x, "sub", 0)),
    )


def solution(mesh):
    both = ("grp", "sub")
    return jax.shard_map(
        local,
        mesh=mesh,
        in_specs=(
            P(both, None),
            P("sub", "grp"),
            P(both, None, None, None),
            P(both, None),
            P(both, None, None),
            P(both, None, None, None),
            P(both, None, None, None),
            P(both, None, None, None, None),
        ),
        out_specs=P(both, None, None, None, None),
        check_vma=False,
    )
```

```python
import functools

import jax
import jax.numpy as jnp
from jax import lax
from jax.experimental import pallas as pl
from jax.experimental.pallas import tpu as pltpu
from jax.sharding import PartitionSpec as P

BF = jnp.bfloat16
F32 = jnp.float32
SPACES = {
    "h": pl.BlockSpec(memory_space=pltpu.HBM),
    "a": pl.BlockSpec(memory_space=pl.ANY),
    "s": pl.BlockSpec(memory_space=pltpu.SMEM),
    "v": pl.BlockSpec(memory_space=pltpu.VMEM),
}


def mm(a, b):
    return jnp.dot(a, b, preferred_element_type=F32)


def mm_t(a, b):
    return lax.dot_general(a, b, (((1,), (1,)), ((), ())), preferred_element_type=F32)


def eye(n):
    same = lax.broadcasted_iota(jnp.int32, (n, n), 0) == lax.broadcasted_iota(jnp.int32, (n, n), 1)
    return jnp.where(same, 1.0, 0.0).astype(BF)


def one_hot(order, n):
    hit = lax.broadcasted_iota(jnp.int32, (n, order.shape[1]), 0) == order
    return jnp.where(hit, 1.0, 0.0).astype(BF)


def call(body, out_shape, args, scratch=(), specs=None, out="v", limit=40 << 20, flops=1000):
    return pl.pallas_call(
        body,
        out_shape=out_shape,
        in_specs=[SPACES[c] for c in specs or "v" * len(args)],
        out_specs=jax.tree.map(lambda _: SPACES[out], out_shape),
        scratch_shapes=list(scratch),
        compiler_params=pltpu.CompilerParams(vmem_limit_bytes=limit),
        cost_estimate=pl.CostEstimate(flops=flops, bytes_accessed=1000, transcendentals=0),
    )(*args)


def shape(dims, dtype=BF):
    return jax.ShapeDtypeStruct(dims, dtype)


DIGIT = 32


def pack_body(width, tests_ref, omega_ref, perms_ref, out_ref, packed_ref, order_ref, sems):
    rows, cols = omega_ref.shape
    chips = out_ref.shape[0]
    copies = [pltpu.make_async_copy(omega_ref, packed_ref.at[:rows], sems.at[chips])]
    for chip in range(chips):
        copies.append(
            pltpu.make_async_copy(
                tests_ref.at[:, chip * width : (chip + 1) * width], out_ref.at[chip], sems.at[chip]
            )
        )
    for copy in copies:
        copy.start()
    order = perms_ref[0, 1:2, :cols]
    row = lax.broadcasted_iota(jnp.int32, order_ref.shape, 0)
    digits = jnp.where(row == 0, order // DIGIT, jnp.where(row == 1, order % DIGIT, 0))
    order_ref[...] = digits.astype(F32).astype(BF)
    copies.append(pltpu.make_async_copy(order_ref, packed_ref.at[rows:], sems.at[chips + 1]))
    copies[-1].start()
    for copy in copies:
        copy.wait()


def dense_body(cols_ref, tiles_ref, perms_ref, interp_ref, after_ref, keep_ref, near_ref, tests_ref, dense_ref):
    del after_ref
    per_dev, slots, tile = tiles_ref.shape[:3]
    rows = per_dev * tile
    rank = interp_ref.shape[-2]
    core = lax.axis_index("sub") & 1
    first = (lax.axis_index("grp") * lax.axis_size("sub") + lax.axis_index("sub")) * per_dev
    dense_ref[...] = jnp.zeros_like(dense_ref)
    for q in range(per_dev):
        for t in range(slots):
            col = cols_ref[q, t] - first
            below, above = col < 0, col >= per_dev
            place = jnp.where(below, col + per_dev, jnp.where(above, col - per_dev, col))
            inner = jnp.where(core == 0, above, below)
            block = jnp.where(below | above, jnp.where(inner, 1, 2), 0)
            at = pl.multiple_of((block * per_dev + place) * tile, tile)
            dense_ref[q * tile : (q + 1) * tile, pl.ds(at, tile)] = tiles_ref[q, t]
    unit = eye(rank)
    keeps = []
    for i in range(2):
        keep = mm_t(unit, one_hot(perms_ref[0, i : i + 1, :rank], rows))
        rest = one_hot(perms_ref[0, i : i + 1, rank:], rows)
        every = (keep + mm_t(interp_ref[0, i], rest)).astype(BF)
        keeps.append(keep.astype(BF))
        if i == 0:
            keep_ref[rank:] = every
        else:
            tests_ref[...] = every
    keep_ref[:rank] = mm_t(keeps[1], dense_ref[:, :rows]).astype(BF)
    near_ref[...] = mm(keeps[0], dense_ref[...]).astype(BF)


def halo_body(
    dense_ref, near_ref, tests_ref, omega_ref, inner_ref, outer_ref, beside_ref, mine_ref, other_ref
):
    rows = dense_ref.shape[0]
    rank = near_ref.shape[0]
    half = omega_ref.shape[1] // 2
    core = lax.axis_index("sub") & 1
    unit = eye(rank)
    for b, ref in enumerate((inner_ref, outer_ref)):
        digits = ref[rows:].astype(F32)
        order = (digits[0:1, :rank] * DIGIT + digits[1:2, :rank]).astype(jnp.int32)
        keep = mm_t(unit, one_hot(order, rows)).astype(BF)
        block = dense_ref[:, (b + 1) * rows : (b + 2) * rows]
        beside_ref[b * rank : (b + 1) * rank] = mm_t(keep, block).astype(BF)
    for out_ref, place in ((mine_ref, core), (other_ref, 1 - core)):
        cols = pl.ds(pl.multiple_of(place * half, half), half)
        own = omega_ref[:, cols]
        fwd = (
            mm(near_ref[:, :rows], own)
            + mm(near_ref[:, rows : 2 * rows], inner_ref[:rows, cols])
            + mm(near_ref[:, 2 * rows :], outer_ref[:rows, cols])
        )
        out_ref[:rank] = fwd.astype(BF)
        out_ref[rank:] = mm(tests_ref[...], own).astype(BF)


def maps_body(maps_ref, perms_ref, *out_refs):
    rank = maps_ref.shape[-1]
    unit = eye(rank)
    for level, out_ref in enumerate(out_refs):
        row_interp, col_interp, low_high, high_low = (maps_ref[0, level, i] for i in range(4))
        row_hot = one_hot(perms_ref[0, level, 0:1, :], 2 * rank)
        col_hot = one_hot(perms_ref[0, level, 1:2, :], 2 * rank)
        row_all = mm(row_hot, jnp.concatenate([unit, row_interp], axis=0)).astype(BF)
        col_all = mm(col_hot, jnp.concatenate([unit, col_interp], axis=0)).astype(BF)
        for kind, (hot, every) in enumerate(((row_hot, col_all), (col_hot, row_all))):
            keep = [mm_t(unit, hot[side * rank : (side + 1) * rank, :rank]).astype(BF) for side in range(2)]
            if kind == 0:
                cross = [mm(keep[1], high_low), mm(keep[0], low_high)]
            else:
                cross = [mm_t(keep[1], low_high), mm_t(keep[0], high_low)]
            for side in range(2):
                out_ref[kind, side, :rank] = keep[side]
                out_ref[kind, side, rank : 2 * rank] = (-cross[side]).astype(BF)
                out_ref[kind, side, 2 * rank :] = mm_t(
                    unit, every[side * rank : (side + 1) * rank]
                ).astype(BF)


def rim_place():
    sub = lax.axis_index("sub")
    return (sub & 1) != ((sub >> 1) & 1)


def adjoint_body(
    keep_ref, keep_other, beside_ref, beside_other, panel_ref, mine_out, other_out, even_out, odd_out
):
    rows = keep_ref.shape[1]
    rank = keep_ref.shape[0] // 2
    core = lax.axis_index("sub") & 1
    panel = panel_ref[:, pl.ds(pl.multiple_of(core * rows, 128), rows)]
    panel_other = panel_ref[:, pl.ds(pl.multiple_of((1 - core) * rows, 128), rows)]
    mine = mm_t(keep_ref[...], panel)
    other = mm_t(keep_other[...], panel_other)
    from_mine = mm_t(beside_ref[...], panel)
    from_other = mm_t(beside_other[...], panel_other)
    mine_out[:rank] = mine[:rank] + from_other[:rank]
    mine_out[rank:] = mine[rank:]
    other_out[:rank] = other[:rank] + from_mine[:rank]
    other_out[rank:] = other[rank:]
    mine_rim = from_mine[rank:]
    other_rim = from_other[rank:]
    even = rim_place()
    even_out[...] = jnp.where(even, mine_rim, other_rim).astype(BF)
    odd_out[...] = jnp.where(even, other_rim, mine_rim).astype(BF)


def merged(maps_ref, kind, side, mine_first, mine_second, other_first, other_second, rank):
    wide = mm(maps_ref[kind, side, rank:], mine_second) + mm(maps_ref[kind, 1 - side, rank:], other_second)
    kept = mm(maps_ref[kind, side, :rank], mine_first) + mm(maps_ref[kind, 1 - side, :rank], other_first)
    return kept + wide[:rank], wide[rank:]


def first_body(maps_ref, fwd_ref, fwd_other, adj_ref, adj_other, even_ref, odd_ref, out_ref):
    rank = even_ref.shape[0]
    core = lax.axis_index("sub") & 1
    kept, tests = merged(
        maps_ref, 0, core, fwd_ref[:rank], fwd_ref[rank:], fwd_other[:rank], fwd_other[rank:], rank
    )
    out_ref[0, :rank] = kept.astype(BF)
    out_ref[0, rank:] = tests.astype(BF)
    even = rim_place()
    from_even = even_ref[...].astype(F32)
    from_odd = odd_ref[...].astype(F32)
    mine = adj_ref[:rank] + jnp.where(even, from_even, from_odd)
    other = adj_other[:rank] + jnp.where(even, from_odd, from_even)
    kept, tests = merged(
        maps_ref,
        1,
        core,
        mine.astype(BF),
        adj_ref[rank:].astype(BF),
        other.astype(BF),
        adj_other[rank:].astype(BF),
        rank,
    )
    out_ref[1, :rank] = kept.astype(BF)
    out_ref[1, rank:] = tests.astype(BF)


def level_body(axis, bit, last, maps_ref, mine_ref, other_ref, *refs):
    rank = mine_ref.shape[1] // 2
    side = (lax.axis_index(axis) >> bit) & 1
    out_ref = refs[-1]
    if last:
        for level, ref in enumerate((*refs[:-1], mine_ref)):
            out_ref[level] = ref[:, :rank]
    for kind in range(2):
        kept, tests = merged(
            maps_ref,
            kind,
            side,
            mine_ref[kind, :rank],
            mine_ref[kind, rank:],
            other_ref[kind, :rank],
            other_ref[kind, rank:],
            rank,
        )
        if last:
            out_ref[len(refs), kind] = kept.astype(BF)
        else:
            out_ref[kind, :rank] = kept.astype(BF)
            out_ref[kind, rank:] = tests.astype(BF)


def output_body(vectors, mine_ref, other_ref, out_ref):
    half = mine_ref.shape[-1]
    core = lax.axis_index("sub") & 1
    k = lax.broadcasted_iota(jnp.int32, (half, 2 * half), 0)
    s = lax.broadcasted_iota(jnp.int32, (half, 2 * half), 1)
    base = k + k // vectors * vectors
    to_mine = jnp.where(s == base + core * vectors, 1.0, 0.0).astype(BF)
    to_other = jnp.where(s == base + (1 - core) * vectors, 1.0, 0.0).astype(BF)
    mine_cols = pl.ds(pl.multiple_of(core * half, half), half)
    other_cols = pl.ds(pl.multiple_of((1 - core) * half, half), half)
    for level in range(mine_ref.shape[0]):
        mine, other = mine_ref[level], other_ref[level]
        out_ref[0, level, 0, :, mine_cols] = mine[0]
        out_ref[0, level, 0, :, other_cols] = other[0]
        out_ref[0, level, 1] = (mm(mine[1], to_mine) + mm(other[1], to_other)).astype(BF)


def swapped(x, axis, bit):
    return lax.ppermute(x, axis, [(i, i ^ (1 << bit)) for i in range(lax.axis_size(axis))])


def local(omega, adj_tests, near_tiles, tile_cols, leaf_perms, leaf_interp, node_perms, node_maps):
    rows, samples = omega.shape
    half = samples // 2
    vectors = adj_tests.shape[0]
    rank = leaf_interp.shape[-1]
    levels = node_maps.shape[1]
    count = lax.axis_size("sub")
    chips = count // 2
    sub_bits = count.bit_length() - 1
    outward = [(i, j) for i in range(1, count - 1, 2) for j in (i + 1,)]
    outward += [(j, i) for i, j in outward]

    blocks, packed = call(
        functools.partial(pack_body, 2 * rows),
        [shape((chips, vectors, 2 * rows)), shape((rows + 16, samples))],
        (adj_tests, omega, leaf_perms),
        scratch=[pltpu.VMEM((16, samples), BF), pltpu.SemaphoreType.DMA((chips + 2,))],
        specs="hhv",
        limit=56 << 20,
    )
    packed_outer = lax.ppermute(packed, "sub", outward)
    packed_inner = swapped(packed, "sub", 0)
    groups = [[2 * m + c for m in range(chips)] for c in range(2)]
    panel = lax.all_to_all(
        blocks, "sub", split_axis=0, concat_axis=0, tiled=True, axis_index_groups=groups
    ).reshape(half, 2 * rows)

    maps = call(
        maps_body,
        [shape((2, 2, 3 * rank, rank))] * levels,
        (node_maps, node_perms),
        flops=4 << 30,
    )
    keep, near, tests, dense = call(
        dense_body,
        [
            shape((2 * rank, rows)),
            shape((rank, 3 * rows)),
            shape((rank, rows)),
            shape((rows, 3 * rows)),
        ],
        (tile_cols, near_tiles, leaf_perms, jnp.swapaxes(leaf_interp, 2, 3), maps[0]),
        specs="svvva",
        flops=4 << 30,
    )
    keep_other = swapped(keep, "sub", 0)
    beside, fwd_mine, fwd_send = call(
        halo_body,
        [shape((2 * rank, rows))] + [shape((2 * rank, half))] * 2,
        (dense, near, tests, omega, packed_inner, packed_outer),
    )
    beside_other = swapped(beside, "sub", 0)
    fwd_other = swapped(fwd_send, "sub", 0)

    adj_leaf, adj_leaf_other, even_rim, odd_rim = call(
        adjoint_body,
        [shape((2 * rank, half), F32)] * 2 + [shape((rank, half))] * 2,
        (keep, keep_other, beside, beside_other, panel),
    )
    even_rim = swapped(even_rim, "sub", 1)
    route = [(2 * i + c, 2 * i + 2 + c) for i in range(1, chips - 1, 2) for c in range(2)]
    odd_rim = lax.ppermute(odd_rim, "sub", route + [(j, i) for i, j in route])
    x = call(
        first_body,
        shape((2, 2 * rank, half)),
        (maps[0], fwd_mine, fwd_other, adj_leaf, adj_leaf_other, even_rim, odd_rim),
    )
    nodes = []
    steps = [("sub", bit) for bit in range(1, sub_bits)]
    steps += [("grp", bit) for bit in range(levels - sub_bits)]
    for level, (axis, bit) in enumerate(steps, 1):
        last = level == levels - 1
        new = call(
            functools.partial(level_body, axis, bit, last),
            shape((levels, 2, rank, half) if last else (2, 2 * rank, half)),
            (maps[level], x, swapped(x, axis, bit), *(nodes if last else ())),
        )
        nodes.append(x)
        x = new
    return call(
        functools.partial(output_body, vectors),
        shape((1, levels, 2, rank, samples)),
        (x, swapped(x, "sub", 0)),
    )


def solution(mesh):
    both = ("grp", "sub")
    return jax.shard_map(
        local,
        mesh=mesh,
        in_specs=(
            P(both, None),
            P("sub", "grp"),
            P(both, None, None, None),
            P(both, None),
            P(both, None, None),
            P(both, None, None, None),
            P(both, None, None, None),
            P(both, None, None, None, None),
        ),
        out_specs=P(both, None, None, None, None),
        check_vma=False,
    )
```

```python
import functools

import jax
import jax.numpy as jnp
from jax import lax
from jax.experimental import pallas as pl
from jax.experimental.pallas import tpu as pltpu
from jax.sharding import PartitionSpec as P

BF = jnp.bfloat16
F32 = jnp.float32
SPACES = {
    "h": pl.BlockSpec(memory_space=pltpu.HBM),
    "a": pl.BlockSpec(memory_space=pl.ANY),
    "s": pl.BlockSpec(memory_space=pltpu.SMEM),
    "v": pl.BlockSpec(memory_space=pltpu.VMEM),
}


def mm(a, b):
    return jnp.dot(a, b, preferred_element_type=F32)


def mm_t(a, b):
    return lax.dot_general(a, b, (((1,), (1,)), ((), ())), preferred_element_type=F32)


def eye(n):
    same = lax.broadcasted_iota(jnp.int32, (n, n), 0) == lax.broadcasted_iota(jnp.int32, (n, n), 1)
    return jnp.where(same, 1.0, 0.0).astype(BF)


def one_hot(order, n):
    hit = lax.broadcasted_iota(jnp.int32, (n, order.shape[1]), 0) == order
    return jnp.where(hit, 1.0, 0.0).astype(BF)


def call(body, out_shape, args, scratch=(), specs=None, out="v", limit=40 << 20, flops=1000):
    return pl.pallas_call(
        body,
        out_shape=out_shape,
        in_specs=[SPACES[c] for c in specs or "v" * len(args)],
        out_specs=jax.tree.map(lambda _: SPACES[out], out_shape),
        scratch_shapes=list(scratch),
        compiler_params=pltpu.CompilerParams(vmem_limit_bytes=limit),
        cost_estimate=pl.CostEstimate(flops=flops, bytes_accessed=1000, transcendentals=0),
    )(*args)


def shape(dims, dtype=BF):
    return jax.ShapeDtypeStruct(dims, dtype)


DIGIT = 32


def pack_body(width, tests_ref, omega_ref, perms_ref, out_ref, packed_ref, order_ref, sems):
    rows, cols = omega_ref.shape
    chips = out_ref.shape[0]
    copies = [pltpu.make_async_copy(omega_ref, packed_ref.at[:rows], sems.at[chips])]
    for chip in range(chips):
        copies.append(
            pltpu.make_async_copy(
                tests_ref.at[:, chip * width : (chip + 1) * width], out_ref.at[chip], sems.at[chip]
            )
        )
    for copy in copies:
        copy.start()
    order = perms_ref[0, 1:2, :cols]
    row = lax.broadcasted_iota(jnp.int32, order_ref.shape, 0)
    digits = jnp.where(row == 0, order // DIGIT, jnp.where(row == 1, order % DIGIT, 0))
    order_ref[...] = digits.astype(F32).astype(BF)
    copies.append(pltpu.make_async_copy(order_ref, packed_ref.at[rows:], sems.at[chips + 1]))
    copies[-1].start()
    for copy in copies:
        copy.wait()


def dense_body(cols_ref, tiles_ref, perms_ref, interp_ref, after_ref, keep_ref, near_ref, tests_ref, dense_ref):
    del after_ref
    per_dev, slots, tile = tiles_ref.shape[:3]
    rows = per_dev * tile
    rank = interp_ref.shape[-2]
    core = lax.axis_index("sub") & 1
    first = (lax.axis_index("grp") * lax.axis_size("sub") + lax.axis_index("sub")) * per_dev
    dense_ref[...] = jnp.zeros_like(dense_ref)
    for q in range(per_dev):
        for t in range(slots):
            col = cols_ref[q, t] - first
            below, above = col < 0, col >= per_dev
            place = jnp.where(below, col + per_dev, jnp.where(above, col - per_dev, col))
            inner = jnp.where(core == 0, above, below)
            block = jnp.where(below | above, jnp.where(inner, 1, 2), 0)
            at = pl.multiple_of((block * per_dev + place) * tile, tile)
            dense_ref[q * tile : (q + 1) * tile, pl.ds(at, tile)] = tiles_ref[q, t]
    unit = eye(rank)
    keeps = []
    for i in range(2):
        keep = mm_t(unit, one_hot(perms_ref[0, i : i + 1, :rank], rows))
        rest = one_hot(perms_ref[0, i : i + 1, rank:], rows)
        every = (keep + mm_t(interp_ref[0, i], rest)).astype(BF)
        keeps.append(keep.astype(BF))
        if i == 0:
            keep_ref[rank:] = every
        else:
            tests_ref[...] = every
    keep_ref[:rank] = mm_t(keeps[1], dense_ref[:, :rows]).astype(BF)
    near_ref[...] = mm(keeps[0], dense_ref[...]).astype(BF)


def halo_body(
    dense_ref, near_ref, tests_ref, omega_ref, inner_ref, outer_ref, beside_ref, mine_ref, other_ref
):
    rows = dense_ref.shape[0]
    rank = near_ref.shape[0]
    half = omega_ref.shape[1] // 2
    core = lax.axis_index("sub") & 1
    unit = eye(rank)
    for b, ref in enumerate((inner_ref, outer_ref)):
        digits = ref[rows:].astype(F32)
        order = (digits[0:1, :rank] * DIGIT + digits[1:2, :rank]).astype(jnp.int32)
        keep = mm_t(unit, one_hot(order, rows)).astype(BF)
        block = dense_ref[:, (b + 1) * rows : (b + 2) * rows]
        beside_ref[b * rank : (b + 1) * rank] = mm_t(keep, block).astype(BF)
    for out_ref, place in ((mine_ref, core), (other_ref, 1 - core)):
        cols = pl.ds(pl.multiple_of(place * half, half), half)
        own = omega_ref[:, cols]
        fwd = (
            mm(near_ref[:, :rows], own)
            + mm(near_ref[:, rows : 2 * rows], inner_ref[:rows, cols])
            + mm(near_ref[:, 2 * rows :], outer_ref[:rows, cols])
        )
        out_ref[:rank] = fwd.astype(BF)
        out_ref[rank:] = mm(tests_ref[...], own).astype(BF)


def maps_body(maps_ref, perms_ref, keep_ref, *out_refs):
    rank = maps_ref.shape[-1]
    unit = eye(rank)
    for level, out_ref in enumerate(out_refs):
        row_interp, col_interp, low_high, high_low = (maps_ref[0, level, i] for i in range(4))
        row_hot = one_hot(perms_ref[0, level, 0:1, :], 2 * rank)
        col_hot = one_hot(perms_ref[0, level, 1:2, :], 2 * rank)
        row_all = mm(row_hot, jnp.concatenate([unit, row_interp], axis=0)).astype(BF)
        col_all = mm(col_hot, jnp.concatenate([unit, col_interp], axis=0)).astype(BF)
        for kind, (hot, every) in enumerate(((row_hot, col_all), (col_hot, row_all))):
            keep = [mm_t(unit, hot[side * rank : (side + 1) * rank, :rank]).astype(BF) for side in range(2)]
            if level == 0 and kind == 1:
                for side in range(2):
                    keep_ref[side] = keep[side]
            if kind == 0:
                cross = [mm(keep[1], high_low), mm(keep[0], low_high)]
            else:
                cross = [mm_t(keep[1], low_high), mm_t(keep[0], high_low)]
            for side in range(2):
                out_ref[kind, side, :rank] = keep[side]
                out_ref[kind, side, rank : 2 * rank] = (-cross[side]).astype(BF)
                out_ref[kind, side, 2 * rank :] = mm_t(
                    unit, every[side * rank : (side + 1) * rank]
                ).astype(BF)


def near_rim():
    sub = lax.axis_index("sub")
    return (sub & 1) != ((sub >> 1) & 1)


def merged(maps_ref, kind, side, mine_first, mine_second, other_first, other_second, rank):
    wide = mm(maps_ref[kind, side, rank:], mine_second) + mm(maps_ref[kind, 1 - side, rank:], other_second)
    kept = mm(maps_ref[kind, side, :rank], mine_first) + mm(maps_ref[kind, 1 - side, :rank], other_first)
    return kept + wide[:rank], wide[rank:]


def adjoint_body(
    maps_ref,
    fwd_ref,
    fwd_other,
    keep_ref,
    keep_other,
    beside_ref,
    beside_other,
    panel_ref,
    after_ref,
    out_ref,
    near_out,
    far_out,
):
    del after_ref
    rows = keep_ref.shape[1]
    rank = keep_ref.shape[0] // 2
    core = lax.axis_index("sub") & 1
    kept, tests = merged(
        maps_ref, 0, core, fwd_ref[:rank], fwd_ref[rank:], fwd_other[:rank], fwd_other[rank:], rank
    )
    out_ref[0, :rank] = kept.astype(BF)
    out_ref[0, rank:] = tests.astype(BF)
    panel = panel_ref[:, pl.ds(pl.multiple_of(core * rows, 128), rows)]
    panel_other = panel_ref[:, pl.ds(pl.multiple_of((1 - core) * rows, 128), rows)]
    mine = mm_t(keep_ref[...], panel)
    other = mm_t(keep_other[...], panel_other)
    from_mine = mm_t(beside_ref[...], panel)
    from_other = mm_t(beside_other[...], panel_other)
    kept, tests = merged(
        maps_ref,
        1,
        core,
        (mine[:rank] + from_other[:rank]).astype(BF),
        mine[rank:].astype(BF),
        (other[:rank] + from_mine[:rank]).astype(BF),
        other[rank:].astype(BF),
        rank,
    )
    out_ref[1, :rank] = kept.astype(BF)
    out_ref[1, rank:] = tests.astype(BF)
    near = near_rim()
    near_out[...] = jnp.where(near, from_mine[rank:], from_other[rank:]).astype(BF)
    far_out[...] = jnp.where(near, from_other[rank:], from_mine[rank:]).astype(BF)


def rim_body(keep_ref, near_ref, far_ref, out_ref):
    chip = (lax.axis_index("sub") >> 1) & 1
    added = mm(keep_ref[chip], near_ref[...]) + mm(keep_ref[1 - chip], far_ref[...])
    out_ref[...] = added.astype(BF)


def joined_body(bit, maps_ref, mine_ref, other_ref, added_ref, given_ref, out_ref, node_ref):
    rank = added_ref.shape[0]
    side = (lax.axis_index("sub") >> bit) & 1
    mine = (mine_ref[1, :rank].astype(F32) + added_ref[...].astype(F32)).astype(BF)
    other = (other_ref[1, :rank].astype(F32) + given_ref[...].astype(F32)).astype(BF)
    node_ref[0] = mine_ref[0, :rank]
    node_ref[1] = mine
    for kind, (first, second) in enumerate(((mine_ref[0, :rank], other_ref[0, :rank]), (mine, other))):
        kept, tests = merged(
            maps_ref, kind, side, first, mine_ref[kind, rank:], second, other_ref[kind, rank:], rank
        )
        out_ref[kind, :rank] = kept.astype(BF)
        out_ref[kind, rank:] = tests.astype(BF)


def level_body(axis, bit, last, maps_ref, mine_ref, other_ref, *refs):
    rank = mine_ref.shape[1] // 2
    side = (lax.axis_index(axis) >> bit) & 1
    out_ref = refs[-1]
    if last:
        for level, ref in enumerate((*refs[:-1], mine_ref)):
            out_ref[level] = ref[:, :rank]
    for kind in range(2):
        kept, tests = merged(
            maps_ref,
            kind,
            side,
            mine_ref[kind, :rank],
            mine_ref[kind, rank:],
            other_ref[kind, :rank],
            other_ref[kind, rank:],
            rank,
        )
        if last:
            out_ref[len(refs), kind] = kept.astype(BF)
        else:
            out_ref[kind, :rank] = kept.astype(BF)
            out_ref[kind, rank:] = tests.astype(BF)


def output_body(vectors, mine_ref, other_ref, out_ref):
    half = mine_ref.shape[-1]
    core = lax.axis_index("sub") & 1
    k = lax.broadcasted_iota(jnp.int32, (half, 2 * half), 0)
    s = lax.broadcasted_iota(jnp.int32, (half, 2 * half), 1)
    base = k + k // vectors * vectors
    to_mine = jnp.where(s == base + core * vectors, 1.0, 0.0).astype(BF)
    to_other = jnp.where(s == base + (1 - core) * vectors, 1.0, 0.0).astype(BF)
    mine_cols = pl.ds(pl.multiple_of(core * half, half), half)
    other_cols = pl.ds(pl.multiple_of((1 - core) * half, half), half)
    for level in range(mine_ref.shape[0]):
        mine, other = mine_ref[level], other_ref[level]
        out_ref[0, level, 0, :, mine_cols] = mine[0]
        out_ref[0, level, 0, :, other_cols] = other[0]
        out_ref[0, level, 1] = (mm(mine[1], to_mine) + mm(other[1], to_other)).astype(BF)


def swapped(x, axis, bit):
    return lax.ppermute(x, axis, [(i, i ^ (1 << bit)) for i in range(lax.axis_size(axis))])


def local(omega, adj_tests, near_tiles, tile_cols, leaf_perms, leaf_interp, node_perms, node_maps):
    rows, samples = omega.shape
    half = samples // 2
    vectors = adj_tests.shape[0]
    rank = leaf_interp.shape[-1]
    levels = node_maps.shape[1]
    count = lax.axis_size("sub")
    chips = count // 2
    sub_bits = count.bit_length() - 1
    outward = [(i, j) for i in range(1, count - 1, 2) for j in (i + 1,)]
    outward += [(j, i) for i, j in outward]

    blocks, packed = call(
        functools.partial(pack_body, 2 * rows),
        [shape((chips, vectors, 2 * rows)), shape((rows + 16, samples))],
        (adj_tests, omega, leaf_perms),
        scratch=[pltpu.VMEM((16, samples), BF), pltpu.SemaphoreType.DMA((chips + 2,))],
        specs="hhv",
        limit=56 << 20,
    )
    packed_outer = lax.ppermute(packed, "sub", outward)
    packed_inner = swapped(packed, "sub", 0)
    groups = [[2 * m + c for m in range(chips)] for c in range(2)]
    panel = lax.all_to_all(
        blocks, "sub", split_axis=0, concat_axis=0, tiled=True, axis_index_groups=groups
    ).reshape(half, 2 * rows)

    picks, *maps = call(
        maps_body,
        [shape((2, rank, rank))] + [shape((2, 2, 3 * rank, rank))] * levels,
        (node_maps, node_perms),
        flops=4 << 30,
    )
    keep, near, tests, dense = call(
        dense_body,
        [
            shape((2 * rank, rows)),
            shape((rank, 3 * rows)),
            shape((rank, rows)),
            shape((rows, 3 * rows)),
        ],
        (tile_cols, near_tiles, leaf_perms, jnp.swapaxes(leaf_interp, 2, 3), maps[0]),
        specs="svvva",
        flops=4 << 30,
    )
    keep_other = swapped(keep, "sub", 0)
    beside, fwd_mine, fwd_send = call(
        halo_body,
        [shape((2 * rank, rows))] + [shape((2 * rank, half))] * 2,
        (dense, near, tests, omega, packed_inner, packed_outer),
    )
    beside_other = swapped(beside, "sub", 0)
    fwd_other = swapped(fwd_send, "sub", 0)

    picks_other = swapped(picks, "sub", 1)
    x, near_rims, far_rims = call(
        adjoint_body,
        [shape((2, 2 * rank, half))] + [shape((rank, half))] * 2,
        (maps[0], fwd_mine, fwd_other, keep, keep_other, beside, beside_other, panel, picks_other),
        specs="vvvvvvvva",
    )
    route = [(i, i + 4 if i & 2 else i - 4) for i in range(count)]
    far_rims = lax.ppermute(far_rims, "sub", [(i, j) for i, j in route if 0 <= j < count])
    x_other = swapped(x, "sub", 1)
    given = call(rim_body, shape((rank, half)), (picks_other, near_rims, far_rims))
    new, node = call(
        functools.partial(joined_body, 1),
        [shape((2, 2 * rank, half)), shape((2, rank, half))],
        (maps[1], x, x_other, swapped(given, "sub", 1), given),
    )
    nodes, x = [node], new
    steps = [("sub", bit) for bit in range(2, sub_bits)]
    steps += [("grp", bit) for bit in range(levels - sub_bits)]
    for level, (axis, bit) in enumerate(steps, 2):
        last = level == levels - 1
        new = call(
            functools.partial(level_body, axis, bit, last),
            shape((levels, 2, rank, half) if last else (2, 2 * rank, half)),
            (maps[level], x, swapped(x, axis, bit), *(nodes if last else ())),
        )
        nodes.append(x)
        x = new
    return call(
        functools.partial(output_body, vectors),
        shape((1, levels, 2, rank, samples)),
        (x, swapped(x, "sub", 0)),
    )


def solution(mesh):
    both = ("grp", "sub")
    return jax.shard_map(
        local,
        mesh=mesh,
        in_specs=(
            P(both, None),
            P("sub", "grp"),
            P(both, None, None, None),
            P(both, None),
            P(both, None, None),
            P(both, None, None, None),
            P(both, None, None, None),
            P(both, None, None, None, None),
        ),
        out_specs=P(both, None, None, None, None),
        check_vma=False,
    )
```

```python
import functools

import jax
import jax.numpy as jnp
from jax import lax
from jax.experimental import pallas as pl
from jax.experimental.pallas import tpu as pltpu
from jax.sharding import PartitionSpec as P

BF = jnp.bfloat16
F32 = jnp.float32
SPACES = {
    "h": pl.BlockSpec(memory_space=pltpu.HBM),
    "a": pl.BlockSpec(memory_space=pl.ANY),
    "s": pl.BlockSpec(memory_space=pltpu.SMEM),
    "v": pl.BlockSpec(memory_space=pltpu.VMEM),
}


def mm(a, b):
    return jnp.dot(a, b, preferred_element_type=F32)


def mm_t(a, b):
    return lax.dot_general(a, b, (((1,), (1,)), ((), ())), preferred_element_type=F32)


def eye(n):
    same = lax.broadcasted_iota(jnp.int32, (n, n), 0) == lax.broadcasted_iota(jnp.int32, (n, n), 1)
    return jnp.where(same, 1.0, 0.0).astype(BF)


def one_hot(order, n):
    hit = lax.broadcasted_iota(jnp.int32, (n, order.shape[1]), 0) == order
    return jnp.where(hit, 1.0, 0.0).astype(BF)


def call(body, out_shape, args, scratch=(), specs=None, out="v", limit=40 << 20, flops=1000):
    return pl.pallas_call(
        body,
        out_shape=out_shape,
        in_specs=[SPACES[c] for c in specs or "v" * len(args)],
        out_specs=jax.tree.map(lambda _: SPACES[out], out_shape),
        scratch_shapes=list(scratch),
        compiler_params=pltpu.CompilerParams(vmem_limit_bytes=limit),
        cost_estimate=pl.CostEstimate(flops=flops, bytes_accessed=1000, transcendentals=0),
    )(*args)


def shape(dims, dtype=BF):
    return jax.ShapeDtypeStruct(dims, dtype)


DIGIT = 32


def pack_body(width, tests_ref, omega_ref, perms_ref, out_ref, packed_ref, order_ref, sems):
    rows, cols = omega_ref.shape
    chips = out_ref.shape[0]
    copies = [pltpu.make_async_copy(omega_ref, packed_ref.at[:rows], sems.at[chips])]
    for chip in range(chips):
        copies.append(
            pltpu.make_async_copy(
                tests_ref.at[:, chip * width : (chip + 1) * width], out_ref.at[chip], sems.at[chip]
            )
        )
    for copy in copies:
        copy.start()
    order = perms_ref[0, 1:2, :cols]
    row = lax.broadcasted_iota(jnp.int32, order_ref.shape, 0)
    digits = jnp.where(row == 0, order // DIGIT, jnp.where(row == 1, order % DIGIT, 0))
    order_ref[...] = digits.astype(F32).astype(BF)
    copies.append(pltpu.make_async_copy(order_ref, packed_ref.at[rows:], sems.at[chips + 1]))
    copies[-1].start()
    for copy in copies:
        copy.wait()


def dense_body(cols_ref, tiles_ref, perms_ref, interp_ref, after_ref, keep_ref, near_ref, tests_ref, dense_ref):
    del after_ref
    per_dev, slots, tile = tiles_ref.shape[:3]
    rows = per_dev * tile
    rank = interp_ref.shape[-2]
    core = lax.axis_index("sub") & 1
    first = (lax.axis_index("grp") * lax.axis_size("sub") + lax.axis_index("sub")) * per_dev
    dense_ref[...] = jnp.zeros_like(dense_ref)
    for q in range(per_dev):
        for t in range(slots):
            col = cols_ref[q, t] - first
            below, above = col < 0, col >= per_dev
            place = jnp.where(below, col + per_dev, jnp.where(above, col - per_dev, col))
            inner = jnp.where(core == 0, above, below)
            block = jnp.where(below | above, jnp.where(inner, 1, 2), 0)
            at = pl.multiple_of((block * per_dev + place) * tile, tile)
            dense_ref[q * tile : (q + 1) * tile, pl.ds(at, tile)] = tiles_ref[q, t]
    unit = eye(rank)
    keeps = []
    for i in range(2):
        keep = mm_t(unit, one_hot(perms_ref[0, i : i + 1, :rank], rows))
        rest = one_hot(perms_ref[0, i : i + 1, rank:], rows)
        every = (keep + mm_t(interp_ref[0, i], rest)).astype(BF)
        keeps.append(keep.astype(BF))
        if i == 0:
            keep_ref[rank:] = every
        else:
            tests_ref[...] = every
    keep_ref[:rank] = mm_t(keeps[1], dense_ref[:, :rows]).astype(BF)
    near_ref[...] = mm(keeps[0], dense_ref[...]).astype(BF)


def halo_body(
    dense_ref, near_ref, tests_ref, omega_ref, inner_ref, outer_ref, after_ref, beside_ref, fwd_ref
):
    del after_ref
    rows = dense_ref.shape[0]
    rank = near_ref.shape[0]
    unit = eye(rank)
    for b, ref in enumerate((inner_ref, outer_ref)):
        digits = ref[rows:].astype(F32)
        order = (digits[0:1, :rank] * DIGIT + digits[1:2, :rank]).astype(jnp.int32)
        keep = mm_t(unit, one_hot(order, rows)).astype(BF)
        block = dense_ref[:, (b + 1) * rows : (b + 2) * rows]
        beside_ref[b * rank : (b + 1) * rank] = mm_t(keep, block).astype(BF)
    fwd = (
        mm(near_ref[:, :rows], omega_ref[...])
        + mm(near_ref[:, rows : 2 * rows], inner_ref[:rows])
        + mm(near_ref[:, 2 * rows :], outer_ref[:rows])
    )
    fwd_ref[:rank] = fwd.astype(BF)
    fwd_ref[rank:] = mm(tests_ref[...], omega_ref[...]).astype(BF)


def maps_body(maps_ref, perms_ref, keep_ref, *out_refs):
    rank = maps_ref.shape[-1]
    unit = eye(rank)
    for level, out_ref in enumerate(out_refs):
        row_interp, col_interp, low_high, high_low = (maps_ref[0, level, i] for i in range(4))
        row_hot = one_hot(perms_ref[0, level, 0:1, :], 2 * rank)
        col_hot = one_hot(perms_ref[0, level, 1:2, :], 2 * rank)
        row_all = mm(row_hot, jnp.concatenate([unit, row_interp], axis=0)).astype(BF)
        col_all = mm(col_hot, jnp.concatenate([unit, col_interp], axis=0)).astype(BF)
        for kind, (hot, every) in enumerate(((row_hot, col_all), (col_hot, row_all))):
            keep = [mm_t(unit, hot[side * rank : (side + 1) * rank, :rank]).astype(BF) for side in range(2)]
            if level == 0 and kind == 1:
                for side in range(2):
                    keep_ref[side] = keep[side]
            if kind == 0:
                cross = [mm(keep[1], high_low), mm(keep[0], low_high)]
            else:
                cross = [mm_t(keep[1], low_high), mm_t(keep[0], high_low)]
            for side in range(2):
                out_ref[kind, side, :rank] = keep[side]
                out_ref[kind, side, rank : 2 * rank] = (-cross[side]).astype(BF)
                out_ref[kind, side, 2 * rank :] = mm_t(
                    unit, every[side * rank : (side + 1) * rank]
                ).astype(BF)


def near_rim():
    sub = lax.axis_index("sub")
    return (sub & 1) != ((sub >> 1) & 1)


def merged(maps_ref, kind, side, mine_first, mine_second, other_first, other_second, rank):
    wide = mm(maps_ref[kind, side, rank:], mine_second) + mm(maps_ref[kind, 1 - side, rank:], other_second)
    kept = mm(maps_ref[kind, side, :rank], mine_first) + mm(maps_ref[kind, 1 - side, :rank], other_first)
    return kept + wide[:rank], wide[rank:]


def adjoint_body(maps_ref, keep_ref, keep_other, beside_ref, beside_other, panel_ref, out_ref):
    rows = keep_ref.shape[1]
    rank = keep_ref.shape[0] // 2
    core = lax.axis_index("sub") & 1
    panel = panel_ref[:, pl.ds(pl.multiple_of(core * rows, 128), rows)]
    panel_other = panel_ref[:, pl.ds(pl.multiple_of((1 - core) * rows, 128), rows)]
    mine = mm_t(keep_ref[...], panel)
    other = mm_t(keep_other[...], panel_other)
    from_mine = mm_t(beside_ref[...], panel)
    from_other = mm_t(beside_other[...], panel_other)
    kept, tests = merged(
        maps_ref,
        1,
        core,
        (mine[:rank] + from_other[:rank]).astype(BF),
        mine[rank:].astype(BF),
        (other[:rank] + from_mine[:rank]).astype(BF),
        other[rank:].astype(BF),
        rank,
    )
    out_ref[:rank] = kept.astype(BF)
    out_ref[rank : 2 * rank] = tests.astype(BF)
    near = near_rim()
    out_ref[2 * rank : 3 * rank] = jnp.where(near, from_mine[rank:], from_other[rank:]).astype(BF)
    out_ref[3 * rank :] = jnp.where(near, from_other[rank:], from_mine[rank:]).astype(BF)


def side_by_side(first, other_ref, mine_ref, out_ref):
    half = mine_ref.shape[1]
    out_ref[:, :half] = other_ref[first : first + out_ref.shape[0]]
    out_ref[:, half:] = mine_ref[first : first + out_ref.shape[0]]


def far_body(other_ref, mine_ref, out_ref):
    side_by_side(3 * out_ref.shape[0], other_ref, mine_ref, out_ref)


def both_body(other_ref, mine_ref, after_ref, out_ref, near_ref):
    del after_ref
    side_by_side(0, other_ref, mine_ref, out_ref)
    side_by_side(2 * near_ref.shape[0], other_ref, mine_ref, near_ref)


def rim_body(keep_ref, near_ref, far_ref, out_ref):
    chip = (lax.axis_index("sub") >> 1) & 1
    added = mm(keep_ref[chip], near_ref[...]) + mm(keep_ref[1 - chip], far_ref[...])
    out_ref[...] = added.astype(BF)


def level_body(kind, axis, bit, maps_ref, mine_ref, other_ref, out_ref):
    rank = mine_ref.shape[0] // 2
    side = 0 if axis is None else (lax.axis_index(axis) >> bit) & 1
    kept, tests = merged(
        maps_ref, kind, side, mine_ref[:rank], mine_ref[rank:], other_ref[:rank], other_ref[rank:], rank
    )
    out_ref[:rank] = kept.astype(BF)
    out_ref[rank:] = tests.astype(BF)


def joined_body(bit, maps_ref, mine_ref, other_ref, added_ref, given_ref, out_ref, node_ref):
    rank = added_ref.shape[0]
    side = (lax.axis_index("sub") >> bit) & 1
    mine = (mine_ref[:rank].astype(F32) + added_ref[...].astype(F32)).astype(BF)
    other = (other_ref[:rank].astype(F32) + given_ref[...].astype(F32)).astype(BF)
    node_ref[...] = mine
    kept, tests = merged(maps_ref, 1, side, mine, mine_ref[rank:], other, other_ref[rank:], rank)
    out_ref[:rank] = kept.astype(BF)
    out_ref[rank:] = tests.astype(BF)


def last_body(axis, bit, levels, maps_ref, *refs):
    out_ref = refs[-1]
    rank = out_ref.shape[1]
    side = (lax.axis_index(axis) >> bit) & 1
    core = lax.axis_index("sub") & 1
    for kind in range(2):

        @pl.when(core == kind)
        def _(kind=kind):
            nodes = refs[kind * levels : kind * levels + levels - 1]
            mine_ref, other_ref = nodes[-1], refs[kind * levels + levels - 1]
            for level, ref in enumerate(nodes):
                out_ref[level] = ref[:rank]
            kept, _ = merged(
                maps_ref,
                kind,
                side,
                mine_ref[:rank],
                mine_ref[rank:],
                other_ref[:rank],
                other_ref[rank:],
                rank,
            )
            out_ref[levels - 1] = kept.astype(BF)


def output_body(vectors, mine_ref, other_ref, out_ref):
    samples = mine_ref.shape[-1]
    half = samples // 2
    k = lax.broadcasted_iota(jnp.int32, (samples, samples), 0)
    s = lax.broadcasted_iota(jnp.int32, (samples, samples), 1)
    core = lax.axis_index("sub") & 1
    part = jnp.where(k >= half, 1, 0)
    m = k - part * half
    place = jnp.where(s == m + m // vectors * vectors + part * vectors, 1.0, 0.0).astype(BF)
    for kind, refs in enumerate(((mine_ref, other_ref), (other_ref, mine_ref))):

        @pl.when(core == kind)
        def _(refs=refs):
            for level in range(mine_ref.shape[0]):
                out_ref[0, level, 0] = refs[0][level]
                out_ref[0, level, 1] = mm(refs[1][level], place).astype(BF)


def swapped(x, axis, bit):
    return lax.ppermute(x, axis, [(i, i ^ (1 << bit)) for i in range(lax.axis_size(axis))])


def traded(x, core, axis, bit):
    groups, count = lax.axis_size("grp"), lax.axis_size("sub")
    flip = 1 << bit
    pairs = []
    for g in range(groups):
        for s in range(core, count, 2):
            to = (g, s ^ flip) if axis == "sub" else (g ^ flip, s)
            pairs.append((g * count + s, to[0] * count + to[1]))
    return lax.ppermute(x, ("grp", "sub"), pairs)


def local(omega, adj_tests, near_tiles, tile_cols, leaf_perms, leaf_interp, node_perms, node_maps):
    rows, samples = omega.shape
    half = samples // 2
    vectors = adj_tests.shape[0]
    rank = leaf_interp.shape[-1]
    levels = node_maps.shape[1]
    count = lax.axis_size("sub")
    chips = count // 2
    sub_bits = count.bit_length() - 1
    outward = [(i, i + 1) for i in range(1, count - 1, 2)]
    outward += [(j, i) for i, j in outward]

    blocks, packed = call(
        functools.partial(pack_body, 2 * rows),
        [shape((chips, vectors, 2 * rows)), shape((rows + 16, samples))],
        (adj_tests, omega, leaf_perms),
        scratch=[pltpu.VMEM((16, samples), BF), pltpu.SemaphoreType.DMA((chips + 2,))],
        specs="hhv",
        limit=56 << 20,
    )
    packed_outer = lax.ppermute(packed, "sub", outward)
    packed_inner = swapped(packed, "sub", 0)
    groups = [[2 * m + c for m in range(chips)] for c in range(2)]
    panel = lax.all_to_all(
        blocks, "sub", split_axis=0, concat_axis=0, tiled=True, axis_index_groups=groups
    ).reshape(half, 2 * rows)

    picks, *maps = call(
        maps_body,
        [shape((2, rank, rank))] + [shape((2, 2, 3 * rank, rank))] * levels,
        (node_maps, node_perms),
        flops=4 << 30,
    )
    keep, near, tests, dense = call(
        dense_body,
        [
            shape((2 * rank, rows)),
            shape((rank, 3 * rows)),
            shape((rank, rows)),
            shape((rows, 3 * rows)),
        ],
        (tile_cols, near_tiles, leaf_perms, jnp.swapaxes(leaf_interp, 2, 3), maps[0]),
        specs="svvva",
        flops=4 << 30,
    )
    keep_other = swapped(keep, "sub", 0)
    picks_other = traded(picks, 1, "sub", 1)
    beside, fwd = call(
        halo_body,
        [shape((2 * rank, rows)), shape((2 * rank, samples))],
        (dense, near, tests, omega, packed_inner, packed_outer, picks_other),
        specs="vvvvvva",
    )
    beside_other = swapped(beside, "sub", 0)
    fwd_other = lax.ppermute(fwd, "sub", [(i + 1, i) for i in range(0, count, 2)])
    fwd = call(
        functools.partial(level_body, 0, None, 0), shape((2 * rank, samples)), (maps[0], fwd, fwd_other)
    )

    part = call(
        adjoint_body,
        shape((4 * rank, half)),
        (maps[0], keep, keep_other, beside, beside_other, panel),
    )
    part_other = lax.ppermute(part, "sub", [(i, i + 1) for i in range(0, count, 2)])
    far = call(far_body, shape((rank, samples)), (part_other, part))
    route = [(i, i + 4 if i & 2 else i - 4) for i in range(1, count, 2)]
    far_other = lax.ppermute(far, "sub", [(i, j) for i, j in route if 0 <= j < count])
    adj, near_rims = call(
        both_body,
        [shape((2 * rank, samples)), shape((rank, samples))],
        (part_other, part, far),
        specs="vva",
        flops=4 << 30,
    )
    given = call(rim_body, shape((rank, samples)), (picks_other, near_rims, far_other))
    adj, node = call(
        functools.partial(joined_body, 1),
        [shape((2 * rank, samples)), shape((rank, samples))],
        (maps[1], adj, traded(adj, 1, "sub", 1), traded(given, 1, "sub", 1), given),
    )
    chains = [[fwd], [node, adj]]
    steps = [("sub", bit) for bit in range(1, sub_bits)]
    steps += [("grp", bit) for bit in range(levels - sub_bits)]
    for level, (axis, bit) in enumerate(steps[:-1], 1):
        for kind, chain in enumerate(chains):
            if len(chain) > level:
                continue
            chain.append(
                call(
                    functools.partial(level_body, kind, axis, bit),
                    shape((2 * rank, samples)),
                    (maps[level], chain[-1], traded(chain[-1], kind, axis, bit)),
                )
            )
    axis, bit = steps[-1]
    ends = [traded(chain[-1], kind, axis, bit) for kind, chain in enumerate(chains)]
    mine = call(
        functools.partial(last_body, axis, bit, levels),
        shape((levels, rank, samples)),
        (maps[-1], *chains[0], ends[0], *chains[1], ends[1]),
    )
    return call(
        functools.partial(output_body, vectors),
        shape((1, levels, 2, rank, samples)),
        (mine, swapped(mine, "sub", 0)),
    )


def solution(mesh):
    both = ("grp", "sub")
    return jax.shard_map(
        local,
        mesh=mesh,
        in_specs=(
            P(both, None),
            P("sub", "grp"),
            P(both, None, None, None),
            P(both, None),
            P(both, None, None),
            P(both, None, None, None),
            P(both, None, None, None),
            P(both, None, None, None, None),
        ),
        out_specs=P(both, None, None, None, None),
        check_vma=False,
    )
```

```python
import functools

import jax
import jax.numpy as jnp
from jax import lax
from jax.experimental import pallas as pl
from jax.experimental.pallas import tpu as pltpu
from jax.sharding import PartitionSpec as P

BF = jnp.bfloat16
F32 = jnp.float32
SPACES = {
    "h": pl.BlockSpec(memory_space=pltpu.HBM),
    "a": pl.BlockSpec(memory_space=pl.ANY),
    "s": pl.BlockSpec(memory_space=pltpu.SMEM),
    "v": pl.BlockSpec(memory_space=pltpu.VMEM),
}


def mm(a, b):
    return jnp.dot(a, b, preferred_element_type=F32)


def mm_t(a, b):
    return lax.dot_general(a, b, (((1,), (1,)), ((), ())), preferred_element_type=F32)


def eye(n):
    same = lax.broadcasted_iota(jnp.int32, (n, n), 0) == lax.broadcasted_iota(jnp.int32, (n, n), 1)
    return jnp.where(same, 1.0, 0.0).astype(BF)


def one_hot(order, n):
    hit = lax.broadcasted_iota(jnp.int32, (n, order.shape[1]), 0) == order
    return jnp.where(hit, 1.0, 0.0).astype(BF)


def call(body, out_shape, args, scratch=(), specs=None, out="v", limit=40 << 20, flops=1000):
    return pl.pallas_call(
        body,
        out_shape=out_shape,
        in_specs=[SPACES[c] for c in specs or "v" * len(args)],
        out_specs=jax.tree.map(lambda _: SPACES[out], out_shape),
        scratch_shapes=list(scratch),
        compiler_params=pltpu.CompilerParams(vmem_limit_bytes=limit),
        cost_estimate=pl.CostEstimate(flops=flops, bytes_accessed=1000, transcendentals=0),
    )(*args)


def shape(dims, dtype=BF):
    return jax.ShapeDtypeStruct(dims, dtype)


DIGIT = 32


def pack_body(
    width, tests_hbm, omega_hbm, perms_ref, out_hbm, packed_hbm, tests_ref, omega_ref, order_ref, sems
):
    rows, cols = omega_ref.shape
    chips = out_hbm.shape[0]
    come = [pltpu.make_async_copy(omega_hbm, omega_ref, sems.at[0])]
    go = [pltpu.make_async_copy(omega_ref, packed_hbm.at[:rows], sems.at[1])]
    for chip in range(chips):
        part = slice(chip * width, (chip + 1) * width)
        come.append(
            pltpu.make_async_copy(tests_hbm.at[:, part], tests_ref.at[chip], sems.at[2 + 2 * chip])
        )
        go.append(pltpu.make_async_copy(tests_ref.at[chip], out_hbm.at[chip], sems.at[3 + 2 * chip]))
    for copy in come:
        copy.start()
    order = perms_ref[0, 1:2, :cols]
    row = lax.broadcasted_iota(jnp.int32, order_ref.shape, 0)
    digits = jnp.where(row == 0, order // DIGIT, jnp.where(row == 1, order % DIGIT, 0))
    order_ref[...] = digits.astype(F32).astype(BF)
    last = pltpu.make_async_copy(order_ref, packed_hbm.at[rows:], sems.at[2 + 2 * chips])
    last.start()
    for first, second in zip(come, go):
        first.wait()
        second.start()
    last.wait()
    for copy in go:
        copy.wait()


def dense_body(cols_ref, tiles_ref, perms_ref, interp_ref, after_ref, keep_ref, near_ref, tests_ref, dense_ref):
    del after_ref
    per_dev, slots, tile = tiles_ref.shape[:3]
    rows = per_dev * tile
    rank = interp_ref.shape[-2]
    core = lax.axis_index("sub") & 1
    first = (lax.axis_index("grp") * lax.axis_size("sub") + lax.axis_index("sub")) * per_dev
    dense_ref[...] = jnp.zeros_like(dense_ref)
    for q in range(per_dev):
        for t in range(slots):
            col = cols_ref[q, t] - first
            below, above = col < 0, col >= per_dev
            place = jnp.where(below, col + per_dev, jnp.where(above, col - per_dev, col))
            inner = jnp.where(core == 0, above, below)
            block = jnp.where(below | above, jnp.where(inner, 1, 2), 0)
            at = pl.multiple_of((block * per_dev + place) * tile, tile)
            dense_ref[q * tile : (q + 1) * tile, pl.ds(at, tile)] = tiles_ref[q, t]
    unit = eye(rank)
    keeps = []
    for i in range(2):
        keep = mm_t(unit, one_hot(perms_ref[0, i : i + 1, :rank], rows))
        rest = one_hot(perms_ref[0, i : i + 1, rank:], rows)
        every = (keep + mm_t(interp_ref[0, i], rest)).astype(BF)
        keeps.append(keep.astype(BF))
        if i == 0:
            keep_ref[rank:] = every
        else:
            tests_ref[...] = every
    keep_ref[:rank] = mm_t(keeps[1], dense_ref[:, :rows]).astype(BF)
    near_ref[...] = mm(keeps[0], dense_ref[...]).astype(BF)


def halo_body(
    dense_ref,
    near_ref,
    tests_ref,
    omega_ref,
    inner_ref,
    outer_ref,
    after_ref,
    beside_ref,
    mine_ref,
    other_ref,
):
    del after_ref
    rows = dense_ref.shape[0]
    rank = near_ref.shape[0]
    half = omega_ref.shape[1] // 2
    core = lax.axis_index("sub") & 1
    unit = eye(rank)
    for b, ref in enumerate((inner_ref, outer_ref)):
        digits = ref[rows:].astype(F32)
        order = (digits[0:1, :rank] * DIGIT + digits[1:2, :rank]).astype(jnp.int32)
        keep = mm_t(unit, one_hot(order, rows)).astype(BF)
        block = dense_ref[:, (b + 1) * rows : (b + 2) * rows]
        beside_ref[b * rank : (b + 1) * rank] = mm_t(keep, block).astype(BF)
    for out_ref, place in ((mine_ref, core), (other_ref, 1 - core)):
        cols = pl.ds(pl.multiple_of(place * half, half), half)
        own = omega_ref[:, cols]
        fwd = (
            mm(near_ref[:, :rows], own)
            + mm(near_ref[:, rows : 2 * rows], inner_ref[:rows, cols])
            + mm(near_ref[:, 2 * rows :], outer_ref[:rows, cols])
        )
        out_ref[:rank] = fwd.astype(BF)
        out_ref[rank:] = mm(tests_ref[...], own).astype(BF)


def maps_body(first, maps_ref, perms_ref, *out_refs):
    rank = maps_ref.shape[-1]
    unit = eye(rank)
    if first == 0:
        keep_ref, *out_refs = out_refs
    for level, out_ref in enumerate(out_refs, first):
        row_interp, col_interp, low_high, high_low = (maps_ref[0, level, i] for i in range(4))
        row_hot = one_hot(perms_ref[0, level, 0:1, :], 2 * rank)
        col_hot = one_hot(perms_ref[0, level, 1:2, :], 2 * rank)
        row_all = mm(row_hot, jnp.concatenate([unit, row_interp], axis=0)).astype(BF)
        col_all = mm(col_hot, jnp.concatenate([unit, col_interp], axis=0)).astype(BF)
        for kind, (hot, every) in enumerate(((row_hot, col_all), (col_hot, row_all))):
            keep = [mm_t(unit, hot[side * rank : (side + 1) * rank, :rank]).astype(BF) for side in range(2)]
            if level == 0 and kind == 1:
                for side in range(2):
                    keep_ref[side] = keep[side]
            if kind == 0:
                cross = [mm(keep[1], high_low), mm(keep[0], low_high)]
            else:
                cross = [mm_t(keep[1], low_high), mm_t(keep[0], high_low)]
            for side in range(2):
                out_ref[kind, side, :rank] = keep[side]
                out_ref[kind, side, rank : 2 * rank] = (-cross[side]).astype(BF)
                out_ref[kind, side, 2 * rank :] = mm_t(
                    unit, every[side * rank : (side + 1) * rank]
                ).astype(BF)


def near_rim():
    sub = lax.axis_index("sub")
    return (sub & 1) != ((sub >> 1) & 1)


def merged(maps_ref, kind, side, mine_first, mine_second, other_first, other_second, rank):
    wide = mm(maps_ref[kind, side, rank:], mine_second) + mm(maps_ref[kind, 1 - side, rank:], other_second)
    kept = mm(maps_ref[kind, side, :rank], mine_first) + mm(maps_ref[kind, 1 - side, :rank], other_first)
    return kept + wide[:rank], wide[rank:]


def node_body(maps_ref, mine_ref, other_ref, out_ref):
    rank = mine_ref.shape[0] // 2
    core = lax.axis_index("sub") & 1
    kept, tests = merged(
        maps_ref, 0, core, mine_ref[:rank], mine_ref[rank:], other_ref[:rank], other_ref[rank:], rank
    )
    out_ref[:rank] = kept.astype(BF)
    out_ref[rank:] = tests.astype(BF)


def halves(panel_ref):
    rows = panel_ref.shape[1] // 2
    core = lax.axis_index("sub") & 1
    return [panel_ref[:, pl.ds(pl.multiple_of(at * rows, 128), rows)] for at in (core, 1 - core)]


def edge_body(beside_ref, beside_other, panel_ref, near_out, far_out):
    rank = near_out.shape[0]
    panel, panel_other = halves(panel_ref)
    mine = mm_t(beside_ref[rank:], panel)
    other = mm_t(beside_other[rank:], panel_other)
    near = near_rim()
    near_out[...] = jnp.where(near, mine, other).astype(BF)
    far_out[...] = jnp.where(near, other, mine).astype(BF)


def adjoint_body(
    maps_ref, keep_ref, keep_other, beside_ref, beside_other, panel_ref, after_ref, out_ref
):
    del after_ref
    rank = keep_ref.shape[0] // 2
    core = lax.axis_index("sub") & 1
    panel, panel_other = halves(panel_ref)
    mine = mm_t(keep_ref[...], panel)
    other = mm_t(keep_other[...], panel_other)
    to_other = mm_t(beside_ref[:rank], panel)
    to_mine = mm_t(beside_other[:rank], panel_other)
    kept, tests = merged(
        maps_ref,
        1,
        core,
        (mine[:rank] + to_mine).astype(BF),
        mine[rank:].astype(BF),
        (other[:rank] + to_other).astype(BF),
        other[rank:].astype(BF),
        rank,
    )
    out_ref[:rank] = kept.astype(BF)
    out_ref[rank:] = tests.astype(BF)


def rim_body(keep_ref, near_ref, far_ref, out_ref):
    chip = (lax.axis_index("sub") >> 1) & 1
    added = mm(keep_ref[chip], near_ref[...]) + mm(keep_ref[1 - chip], far_ref[...])
    out_ref[...] = added.astype(BF)


def joined_body(
    bit, maps_ref, fwd_ref, fwd_other, adj_ref, adj_other, added_ref, given_ref, out_ref, node_ref
):
    rank = added_ref.shape[0]
    side = (lax.axis_index("sub") >> bit) & 1
    mine = (adj_ref[:rank].astype(F32) + added_ref[...].astype(F32)).astype(BF)
    other = (adj_other[:rank].astype(F32) + given_ref[...].astype(F32)).astype(BF)
    node_ref[0] = fwd_ref[:rank]
    node_ref[1] = mine
    chains = (
        (fwd_ref[:rank], fwd_ref[rank:], fwd_other[:rank], fwd_other[rank:]),
        (mine, adj_ref[rank:], other, adj_other[rank:]),
    )
    for kind, panels in enumerate(chains):
        kept, tests = merged(maps_ref, kind, side, *panels, rank)
        out_ref[kind, :rank] = kept.astype(BF)
        out_ref[kind, rank:] = tests.astype(BF)


def level_body(axis, bit, last, maps_ref, mine_ref, other_ref, *refs):
    rank = mine_ref.shape[1] // 2
    side = (lax.axis_index(axis) >> bit) & 1
    out_ref = refs[-1]
    if last:
        for level, ref in enumerate((*refs[:-1], mine_ref)):
            out_ref[level] = ref[:, :rank]
    for kind in range(2):
        kept, tests = merged(
            maps_ref,
            kind,
            side,
            mine_ref[kind, :rank],
            mine_ref[kind, rank:],
            other_ref[kind, :rank],
            other_ref[kind, rank:],
            rank,
        )
        if last:
            out_ref[len(refs), kind] = kept.astype(BF)
        else:
            out_ref[kind, :rank] = kept.astype(BF)
            out_ref[kind, rank:] = tests.astype(BF)


def output_body(vectors, mine_ref, other_ref, out_ref):
    half = mine_ref.shape[-1]
    core = lax.axis_index("sub") & 1
    k = lax.broadcasted_iota(jnp.int32, (half, 2 * half), 0)
    s = lax.broadcasted_iota(jnp.int32, (half, 2 * half), 1)
    base = k + k // vectors * vectors
    to_mine = jnp.where(s == base + core * vectors, 1.0, 0.0).astype(BF)
    to_other = jnp.where(s == base + (1 - core) * vectors, 1.0, 0.0).astype(BF)
    mine_cols = pl.ds(pl.multiple_of(core * half, half), half)
    other_cols = pl.ds(pl.multiple_of((1 - core) * half, half), half)
    for level in range(mine_ref.shape[0]):
        mine, other = mine_ref[level], other_ref[level]
        out_ref[0, level, 0, :, mine_cols] = mine[0]
        out_ref[0, level, 0, :, other_cols] = other[0]
        out_ref[0, level, 1] = (mm(mine[1], to_mine) + mm(other[1], to_other)).astype(BF)


def swapped(x, axis, bit):
    return lax.ppermute(x, axis, [(i, i ^ (1 << bit)) for i in range(lax.axis_size(axis))])


def local(omega, adj_tests, near_tiles, tile_cols, leaf_perms, leaf_interp, node_perms, node_maps):
    rows, samples = omega.shape
    half = samples // 2
    vectors = adj_tests.shape[0]
    rank = leaf_interp.shape[-1]
    levels = node_maps.shape[1]
    count = lax.axis_size("sub")
    chips = count // 2
    sub_bits = count.bit_length() - 1
    outward = [(i, i + 1) for i in range(1, count - 1, 2)]
    outward += [(j, i) for i, j in outward] + [(0, 0), (count - 1, count - 1)]

    blocks, packed = call(
        functools.partial(pack_body, 2 * rows),
        [shape((chips, vectors, 2 * rows)), shape((rows + 16, samples))],
        (adj_tests, omega, leaf_perms),
        scratch=[
            pltpu.VMEM((chips, vectors, 2 * rows), BF),
            pltpu.VMEM(omega.shape, BF),
            pltpu.VMEM((16, samples), BF),
            pltpu.SemaphoreType.DMA((2 * chips + 3,)),
        ],
        specs="hhv",
        out="a",
        limit=56 << 20,
    )
    packed_outer = lax.ppermute(packed, "sub", outward)
    packed_inner = swapped(packed, "sub", 0)
    groups = [[2 * m + c for m in range(chips)] for c in range(2)]
    panel = lax.all_to_all(
        blocks, "sub", split_axis=0, concat_axis=0, tiled=True, axis_index_groups=groups
    ).reshape(half, 2 * rows)

    tables = shape((2, 2, 3 * rank, rank))
    picks, first_maps = call(
        functools.partial(maps_body, 0),
        [shape((2, rank, rank)), tables],
        (node_maps, node_perms),
        flops=4 << 30,
    )
    keep, near, tests, dense = call(
        dense_body,
        [
            shape((2 * rank, rows)),
            shape((rank, 3 * rows)),
            shape((rank, rows)),
            shape((rows, 3 * rows)),
        ],
        (tile_cols, near_tiles, leaf_perms, jnp.swapaxes(leaf_interp, 2, 3), first_maps),
        specs="svvva",
        flops=1 << 30,
    )
    keep_other = swapped(keep, "sub", 0)
    picks_other = swapped(picks, "sub", 1)
    beside, fwd_mine, fwd_send = call(
        halo_body,
        [shape((2 * rank, rows))] + [shape((2 * rank, half))] * 2,
        (dense, near, tests, omega, packed_inner, packed_outer, picks_other),
        specs="vvvvvva",
    )
    beside_other = swapped(beside, "sub", 0)
    fwd = call(
        node_body, shape((2 * rank, half)), (first_maps, fwd_mine, swapped(fwd_send, "sub", 0))
    )
    near_rims, far_rims = call(
        edge_body, [shape((rank, half))] * 2, (beside, beside_other, panel)
    )
    ring = list(range(1, chips, 2)) + list(range(chips - 2, -1, -2))
    route = [(2 * a + c, 2 * b + c) for a, b in zip(ring, ring[1:] + ring[:1]) for c in range(2)]
    far_rims = lax.ppermute(far_rims, "sub", route)
    adj = call(
        adjoint_body,
        shape((2 * rank, half)),
        (first_maps, keep, keep_other, beside, beside_other, panel, near_rims),
        specs="vvvvvva",
        flops=4 << 30,
    )
    given = call(rim_body, shape((rank, half)), (picks_other, near_rims, far_rims))
    more_maps = call(
        functools.partial(maps_body, 1), [tables] * (levels - 1), (node_maps, node_perms)
    )
    maps = [first_maps, *more_maps]
    new, node = call(
        functools.partial(joined_body, 1),
        [shape((2, 2 * rank, half)), shape((2, rank, half))],
        (
            maps[1],
            fwd,
            swapped(fwd, "sub", 1),
            adj,
            swapped(adj, "sub", 1),
            swapped(given, "sub", 1),
            given,
        ),
    )
    nodes, x = [node], new
    steps = [("sub", bit) for bit in range(2, sub_bits)]
    steps += [("grp", bit) for bit in range(levels - sub_bits)]
    for level, (axis, bit) in enumerate(steps, 2):
        last = level == levels - 1
        new = call(
            functools.partial(level_body, axis, bit, last),
            shape((levels, 2, rank, half) if last else (2, 2 * rank, half)),
            (maps[level], x, swapped(x, axis, bit), *(nodes if last else ())),
        )
        nodes.append(x)
        x = new
    return call(
        functools.partial(output_body, vectors),
        shape((1, levels, 2, rank, samples)),
        (x, swapped(x, "sub", 0)),
    )


def solution(mesh):
    both = ("grp", "sub")
    return jax.shard_map(
        local,
        mesh=mesh,
        in_specs=(
            P(both, None),
            P("sub", "grp"),
            P(both, None, None, None),
            P(both, None),
            P(both, None, None),
            P(both, None, None, None),
            P(both, None, None, None),
            P(both, None, None, None, None),
        ),
        out_specs=P(both, None, None, None, None),
        check_vma=False,
    )
```

```python
import functools

import jax
import jax.numpy as jnp
from jax import lax
from jax.experimental import pallas as pl
from jax.experimental.pallas import tpu as pltpu
from jax.sharding import PartitionSpec as P

BF = jnp.bfloat16
F32 = jnp.float32
SPACES = {
    "h": pl.BlockSpec(memory_space=pltpu.HBM),
    "a": pl.BlockSpec(memory_space=pl.ANY),
    "s": pl.BlockSpec(memory_space=pltpu.SMEM),
    "v": pl.BlockSpec(memory_space=pltpu.VMEM),
}


def mm(a, b):
    return jnp.dot(a, b, preferred_element_type=F32)


def mm_t(a, b):
    return lax.dot_general(a, b, (((1,), (1,)), ((), ())), preferred_element_type=F32)


def eye(n):
    same = lax.broadcasted_iota(jnp.int32, (n, n), 0) == lax.broadcasted_iota(jnp.int32, (n, n), 1)
    return jnp.where(same, 1.0, 0.0).astype(BF)


def one_hot(order, n):
    hit = lax.broadcasted_iota(jnp.int32, (n, order.shape[1]), 0) == order
    return jnp.where(hit, 1.0, 0.0).astype(BF)


def call(body, out_shape, args, scratch=(), specs=None, out="v", limit=40 << 20, flops=1000):
    return pl.pallas_call(
        body,
        out_shape=out_shape,
        in_specs=[SPACES[c] for c in specs or "v" * len(args)],
        out_specs=jax.tree.map(lambda _: SPACES[out], out_shape),
        scratch_shapes=list(scratch),
        compiler_params=pltpu.CompilerParams(vmem_limit_bytes=limit),
        cost_estimate=pl.CostEstimate(flops=flops, bytes_accessed=1000, transcendentals=0),
    )(*args)


def shape(dims, dtype=BF):
    return jax.ShapeDtypeStruct(dims, dtype)


DIGIT = 32


def pack_body(
    width, tests_hbm, omega_hbm, perms_ref, nodes_ref, out_hbm, packed_hbm, tests_ref, omega_ref, order_ref, sems
):
    rows = omega_ref.shape[0]
    chips = out_hbm.shape[0]
    come = [pltpu.make_async_copy(omega_hbm, omega_ref, sems.at[0])]
    go = [pltpu.make_async_copy(omega_ref, packed_hbm.at[:rows], sems.at[1])]
    for chip in range(chips):
        part = slice(chip * width, (chip + 1) * width)
        come.append(
            pltpu.make_async_copy(tests_hbm.at[:, part], tests_ref.at[chip], sems.at[2 + 2 * chip])
        )
        go.append(pltpu.make_async_copy(tests_ref.at[chip], out_hbm.at[chip], sems.at[3 + 2 * chip]))
    for copy in come:
        copy.start()
    kept = nodes_ref.shape[-1] // 2
    for order, at in ((perms_ref[0, 1:2, :kept], 0), (nodes_ref[0, 0, 1:2, :kept], 2)):
        row = lax.broadcasted_iota(jnp.int32, (order_ref.shape[0], kept), 0)
        digits = jnp.where(row == at, order // DIGIT, jnp.where(row == at + 1, order % DIGIT, 0))
        total = digits if at == 0 else total + digits
    order_ref[...] = jnp.zeros_like(order_ref)
    order_ref[:, :kept] = total.astype(F32).astype(BF)
    last = pltpu.make_async_copy(order_ref, packed_hbm.at[rows:], sems.at[2 + 2 * chips])
    last.start()
    for first, second in zip(come, go):
        first.wait()
        second.start()
    last.wait()
    for copy in go:
        copy.wait()


def dense_body(cols_ref, tiles_ref, perms_ref, interp_ref, after_ref, keep_ref, near_ref, tests_ref, dense_ref):
    del after_ref
    per_dev, slots, tile = tiles_ref.shape[:3]
    rows = per_dev * tile
    rank = interp_ref.shape[-2]
    core = lax.axis_index("sub") & 1
    first = (lax.axis_index("grp") * lax.axis_size("sub") + lax.axis_index("sub")) * per_dev
    dense_ref[...] = jnp.zeros_like(dense_ref)
    for q in range(per_dev):
        for t in range(slots):
            col = cols_ref[q, t] - first
            below, above = col < 0, col >= per_dev
            place = jnp.where(below, col + per_dev, jnp.where(above, col - per_dev, col))
            inner = jnp.where(core == 0, above, below)
            block = jnp.where(below | above, jnp.where(inner, 1, 2), 0)
            at = pl.multiple_of((block * per_dev + place) * tile, tile)
            dense_ref[q * tile : (q + 1) * tile, pl.ds(at, tile)] = tiles_ref[q, t]
    unit = eye(rank)
    keeps = []
    for i in range(2):
        keep = mm_t(unit, one_hot(perms_ref[0, i : i + 1, :rank], rows))
        rest = one_hot(perms_ref[0, i : i + 1, rank:], rows)
        every = (keep + mm_t(interp_ref[0, i], rest)).astype(BF)
        keeps.append(keep.astype(BF))
        if i == 0:
            keep_ref[rank:] = every
        else:
            tests_ref[...] = every
    keep_ref[:rank] = mm_t(keeps[1], dense_ref[:, :rows]).astype(BF)
    near_ref[...] = mm(keeps[0], dense_ref[...]).astype(BF)


def from_digits(digits, at):
    digits = digits.astype(F32)
    return (digits[at : at + 1] * DIGIT + digits[at + 1 : at + 2]).astype(jnp.int32)


def halo_body(
    dense_ref,
    near_ref,
    tests_ref,
    omega_ref,
    inner_ref,
    outer_ref,
    beside_ref,
    mine_ref,
    other_ref,
):
    rows = dense_ref.shape[0]
    rank = near_ref.shape[0]
    half = omega_ref.shape[1] // 2
    core = lax.axis_index("sub") & 1
    unit = eye(rank)
    for b, ref in enumerate((inner_ref, outer_ref)):
        order = from_digits(ref[rows:, :rank], 0)
        keep = mm_t(unit, one_hot(order, rows)).astype(BF)
        block = dense_ref[:, (b + 1) * rows : (b + 2) * rows]
        beside_ref[b * rank : (b + 1) * rank] = mm_t(keep, block).astype(BF)
    beside_ref[2 * rank :] = jnp.zeros_like(beside_ref[2 * rank :])
    beside_ref[2 * rank :, : outer_ref.shape[1]] = outer_ref[rows:]
    for out_ref, place in ((mine_ref, core), (other_ref, 1 - core)):
        cols = pl.ds(pl.multiple_of(place * half, half), half)
        own = omega_ref[:, cols]
        fwd = (
            mm(near_ref[:, :rows], own)
            + mm(near_ref[:, rows : 2 * rows], inner_ref[:rows, cols])
            + mm(near_ref[:, 2 * rows :], outer_ref[:rows, cols])
        )
        out_ref[:rank] = fwd.astype(BF)
        out_ref[rank:] = mm(tests_ref[...], own).astype(BF)


def maps_body(first, maps_ref, perms_ref, *out_refs):
    rank = maps_ref.shape[-1]
    unit = eye(rank)
    for level, out_ref in enumerate(out_refs, first):
        row_interp, col_interp, low_high, high_low = (maps_ref[0, level, i] for i in range(4))
        row_hot = one_hot(perms_ref[0, level, 0:1, :], 2 * rank)
        col_hot = one_hot(perms_ref[0, level, 1:2, :], 2 * rank)
        row_all = mm(row_hot, jnp.concatenate([unit, row_interp], axis=0)).astype(BF)
        col_all = mm(col_hot, jnp.concatenate([unit, col_interp], axis=0)).astype(BF)
        for kind, (hot, every) in enumerate(((row_hot, col_all), (col_hot, row_all))):
            keep = [mm_t(unit, hot[side * rank : (side + 1) * rank, :rank]).astype(BF) for side in range(2)]
            if kind == 0:
                cross = [mm(keep[1], high_low), mm(keep[0], low_high)]
            else:
                cross = [mm_t(keep[1], low_high), mm_t(keep[0], high_low)]
            for side in range(2):
                out_ref[kind, side, :rank] = keep[side]
                out_ref[kind, side, rank : 2 * rank] = (-cross[side]).astype(BF)
                out_ref[kind, side, 2 * rank :] = mm_t(
                    unit, every[side * rank : (side + 1) * rank]
                ).astype(BF)


def near_rim():
    sub = lax.axis_index("sub")
    return (sub & 1) != ((sub >> 1) & 1)


def merged(maps_ref, kind, side, mine_first, mine_second, other_first, other_second, rank):
    wide = mm(maps_ref[kind, side, rank:], mine_second) + mm(maps_ref[kind, 1 - side, rank:], other_second)
    kept = mm(maps_ref[kind, side, :rank], mine_first) + mm(maps_ref[kind, 1 - side, :rank], other_first)
    return kept + wide[:rank], wide[rank:]


def node_body(maps_ref, mine_ref, other_ref, out_ref):
    rank = mine_ref.shape[0] // 2
    core = lax.axis_index("sub") & 1
    kept, tests = merged(
        maps_ref, 0, core, mine_ref[:rank], mine_ref[rank:], other_ref[:rank], other_ref[rank:], rank
    )
    out_ref[:rank] = kept.astype(BF)
    out_ref[rank:] = tests.astype(BF)


def halves(panel_ref):
    rows = panel_ref.shape[1] // 2
    core = lax.axis_index("sub") & 1
    return [panel_ref[:, pl.ds(pl.multiple_of(at * rows, 128), rows)] for at in (core, 1 - core)]


def edge_body(beside_ref, beside_other, panel_ref, near_out, far_out):
    rank = near_out.shape[0]
    panel, panel_other = halves(panel_ref)
    mine = mm_t(beside_ref[rank : 2 * rank], panel)
    other = mm_t(beside_other[rank : 2 * rank], panel_other)
    near = near_rim()
    near_out[...] = jnp.where(near, mine, other).astype(BF)
    far_out[...] = jnp.where(near, other, mine).astype(BF)


def adjoint_body(
    maps_ref, keep_ref, keep_other, beside_ref, beside_other, panel_ref, after_ref, out_ref
):
    del after_ref
    rank = keep_ref.shape[0] // 2
    core = lax.axis_index("sub") & 1
    panel, panel_other = halves(panel_ref)
    mine = mm_t(keep_ref[...], panel)
    other = mm_t(keep_other[...], panel_other)
    to_other = mm_t(beside_ref[:rank], panel)
    to_mine = mm_t(beside_other[:rank], panel_other)
    kept, tests = merged(
        maps_ref,
        1,
        core,
        (mine[:rank] + to_mine).astype(BF),
        mine[rank:].astype(BF),
        (other[:rank] + to_other).astype(BF),
        other[rank:].astype(BF),
        rank,
    )
    out_ref[:rank] = kept.astype(BF)
    out_ref[rank:] = tests.astype(BF)


def rim_body(beside_ref, beside_other, near_ref, far_ref, out_ref):
    rank = near_ref.shape[0]
    chip = (lax.axis_index("sub") >> 1) & 1
    digits = [ref[2 * rank :, :rank].astype(F32) for ref in (beside_ref, beside_other)]
    order = from_digits(jnp.where(near_rim(), *digits), 2)
    hot = one_hot(order, 2 * rank)
    keeps = [mm_t(eye(rank), hot[side * rank : (side + 1) * rank]) for side in range(2)]
    upper = chip == 1
    near_keep = jnp.where(upper, keeps[1], keeps[0]).astype(BF)
    far_keep = jnp.where(upper, keeps[0], keeps[1]).astype(BF)
    out_ref[...] = (mm(near_keep, near_ref[...]) + mm(far_keep, far_ref[...])).astype(BF)


def joined_body(
    bit, maps_ref, fwd_ref, fwd_other, adj_ref, adj_other, added_ref, given_ref, out_ref, node_ref
):
    rank = added_ref.shape[0]
    side = (lax.axis_index("sub") >> bit) & 1
    mine = (adj_ref[:rank].astype(F32) + added_ref[...].astype(F32)).astype(BF)
    other = (adj_other[:rank].astype(F32) + given_ref[...].astype(F32)).astype(BF)
    node_ref[0] = fwd_ref[:rank]
    node_ref[1] = mine
    chains = (
        (fwd_ref[:rank], fwd_ref[rank:], fwd_other[:rank], fwd_other[rank:]),
        (mine, adj_ref[rank:], other, adj_other[rank:]),
    )
    for kind, panels in enumerate(chains):
        kept, tests = merged(maps_ref, kind, side, *panels, rank)
        out_ref[kind, :rank] = kept.astype(BF)
        out_ref[kind, rank:] = tests.astype(BF)


def level_body(axis, bit, last, maps_ref, mine_ref, other_ref, *refs):
    rank = mine_ref.shape[1] // 2
    side = (lax.axis_index(axis) >> bit) & 1
    out_ref = refs[-1]
    if last:
        for level, ref in enumerate((*refs[:-1], mine_ref)):
            out_ref[level] = ref[:, :rank]
    for kind in range(2):
        kept, tests = merged(
            maps_ref,
            kind,
            side,
            mine_ref[kind, :rank],
            mine_ref[kind, rank:],
            other_ref[kind, :rank],
            other_ref[kind, rank:],
            rank,
        )
        if last:
            out_ref[len(refs), kind] = kept.astype(BF)
        else:
            out_ref[kind, :rank] = kept.astype(BF)
            out_ref[kind, rank:] = tests.astype(BF)


def output_body(vectors, mine_ref, other_ref, out_ref):
    half = mine_ref.shape[-1]
    core = lax.axis_index("sub") & 1
    k = lax.broadcasted_iota(jnp.int32, (half, 2 * half), 0)
    s = lax.broadcasted_iota(jnp.int32, (half, 2 * half), 1)
    base = k + k // vectors * vectors
    to_mine = jnp.where(s == base + core * vectors, 1.0, 0.0).astype(BF)
    to_other = jnp.where(s == base + (1 - core) * vectors, 1.0, 0.0).astype(BF)
    mine_cols = pl.ds(pl.multiple_of(core * half, half), half)
    other_cols = pl.ds(pl.multiple_of((1 - core) * half, half), half)
    for level in range(mine_ref.shape[0]):
        mine, other = mine_ref[level], other_ref[level]
        out_ref[0, level, 0, :, mine_cols] = mine[0]
        out_ref[0, level, 0, :, other_cols] = other[0]
        out_ref[0, level, 1] = (mm(mine[1], to_mine) + mm(other[1], to_other)).astype(BF)


def swapped(x, axis, bit):
    return lax.ppermute(x, axis, [(i, i ^ (1 << bit)) for i in range(lax.axis_size(axis))])


def local(omega, adj_tests, near_tiles, tile_cols, leaf_perms, leaf_interp, node_perms, node_maps):
    rows, samples = omega.shape
    half = samples // 2
    vectors = adj_tests.shape[0]
    rank = leaf_interp.shape[-1]
    levels = node_maps.shape[1]
    count = lax.axis_size("sub")
    chips = count // 2
    sub_bits = count.bit_length() - 1
    outward = [(i, i + 1) for i in range(1, count - 1, 2)]
    outward += [(j, i) for i, j in outward] + [(0, 0), (count - 1, count - 1)]

    blocks, packed = call(
        functools.partial(pack_body, 2 * rows),
        [shape((chips, vectors, 2 * rows)), shape((rows + 16, samples))],
        (adj_tests, omega, leaf_perms, node_perms),
        scratch=[
            pltpu.VMEM((chips, vectors, 2 * rows), BF),
            pltpu.VMEM(omega.shape, BF),
            pltpu.VMEM((16, samples), BF),
            pltpu.SemaphoreType.DMA((2 * chips + 3,)),
        ],
        specs="hhvv",
        out="a",
        limit=56 << 20,
    )
    packed_outer = lax.ppermute(packed, "sub", outward)
    packed_inner = swapped(packed, "sub", 0)
    groups = [[2 * m + c for m in range(chips)] for c in range(2)]
    panel = lax.all_to_all(
        blocks, "sub", split_axis=0, concat_axis=0, tiled=True, axis_index_groups=groups
    ).reshape(half, 2 * rows)

    tables = shape((2, 2, 3 * rank, rank))
    [first_maps] = call(
        functools.partial(maps_body, 0),
        [tables],
        (node_maps, node_perms),
        flops=1 << 30,
    )
    keep, near, tests, dense = call(
        dense_body,
        [
            shape((2 * rank, rows)),
            shape((rank, 3 * rows)),
            shape((rank, rows)),
            shape((rows, 3 * rows)),
        ],
        (tile_cols, near_tiles, leaf_perms, jnp.swapaxes(leaf_interp, 2, 3), first_maps),
        specs="svvva",
        flops=1 << 30,
    )
    keep_other = swapped(keep, "sub", 0)
    beside, fwd_mine, fwd_send = call(
        halo_body,
        [shape((2 * rank + 16, rows))] + [shape((2 * rank, half))] * 2,
        (dense, near, tests, omega, packed_inner, packed_outer),
    )
    beside_other = swapped(beside, "sub", 0)
    fwd = call(
        node_body, shape((2 * rank, half)), (first_maps, fwd_mine, swapped(fwd_send, "sub", 0))
    )
    near_rims, far_rims = call(
        edge_body, [shape((rank, half))] * 2, (beside, beside_other, panel)
    )
    ring = list(range(1, chips, 2)) + list(range(chips - 2, -1, -2))
    route = [(2 * a + c, 2 * b + c) for a, b in zip(ring, ring[1:] + ring[:1]) for c in range(2)]
    far_rims = lax.ppermute(far_rims, "sub", route)
    adj = call(
        adjoint_body,
        shape((2 * rank, half)),
        (first_maps, keep, keep_other, beside, beside_other, panel, near_rims),
        specs="vvvvvva",
        flops=4 << 30,
    )
    given = call(rim_body, shape((rank, half)), (beside, beside_other, near_rims, far_rims))
    more_maps = call(
        functools.partial(maps_body, 1), [tables] * (levels - 1), (node_maps, node_perms)
    )
    maps = [first_maps, *more_maps]
    new, node = call(
        functools.partial(joined_body, 1),
        [shape((2, 2 * rank, half)), shape((2, rank, half))],
        (
            maps[1],
            fwd,
            swapped(fwd, "sub", 1),
            adj,
            swapped(adj, "sub", 1),
            swapped(given, "sub", 1),
            given,
        ),
    )
    nodes, x = [node], new
    steps = [("sub", bit) for bit in range(2, sub_bits)]
    steps += [("grp", bit) for bit in range(levels - sub_bits)]
    for level, (axis, bit) in enumerate(steps, 2):
        last = level == levels - 1
        new = call(
            functools.partial(level_body, axis, bit, last),
            shape((levels, 2, rank, half) if last else (2, 2 * rank, half)),
            (maps[level], x, swapped(x, axis, bit), *(nodes if last else ())),
        )
        nodes.append(x)
        x = new
    return call(
        functools.partial(output_body, vectors),
        shape((1, levels, 2, rank, samples)),
        (x, swapped(x, "sub", 0)),
    )


def solution(mesh):
    both = ("grp", "sub")
    return jax.shard_map(
        local,
        mesh=mesh,
        in_specs=(
            P(both, None),
            P("sub", "grp"),
            P(both, None, None, None),
            P(both, None),
            P(both, None, None),
            P(both, None, None, None),
            P(both, None, None, None),
            P(both, None, None, None, None),
        ),
        out_specs=P(both, None, None, None, None),
        check_vma=False,
    )
```

```python
import functools

import jax
import jax.numpy as jnp
from jax import lax
from jax.experimental import pallas as pl
from jax.experimental.pallas import tpu as pltpu
from jax.sharding import PartitionSpec as P

BF = jnp.bfloat16
F32 = jnp.float32
SPACES = {
    "h": pl.BlockSpec(memory_space=pltpu.HBM),
    "a": pl.BlockSpec(memory_space=pl.ANY),
    "s": pl.BlockSpec(memory_space=pltpu.SMEM),
    "v": pl.BlockSpec(memory_space=pltpu.VMEM),
}


def mm(a, b):
    return jnp.dot(a, b, preferred_element_type=F32)


def mm_t(a, b):
    return lax.dot_general(a, b, (((1,), (1,)), ((), ())), preferred_element_type=F32)


def eye(n):
    same = lax.broadcasted_iota(jnp.int32, (n, n), 0) == lax.broadcasted_iota(jnp.int32, (n, n), 1)
    return jnp.where(same, 1.0, 0.0).astype(BF)


def one_hot(order, n):
    hit = lax.broadcasted_iota(jnp.int32, (n, order.shape[1]), 0) == order
    return jnp.where(hit, 1.0, 0.0).astype(BF)


def call(body, out_shape, args, scratch=(), specs=None, out="v", limit=40 << 20, flops=1000):
    return pl.pallas_call(
        body,
        out_shape=out_shape,
        in_specs=[SPACES[c] for c in specs or "v" * len(args)],
        out_specs=jax.tree.map(lambda _: SPACES[out], out_shape),
        scratch_shapes=list(scratch),
        compiler_params=pltpu.CompilerParams(vmem_limit_bytes=limit),
        cost_estimate=pl.CostEstimate(flops=flops, bytes_accessed=1000, transcendentals=0),
    )(*args)


def shape(dims, dtype=BF):
    return jax.ShapeDtypeStruct(dims, dtype)


DIGIT = 32


def pack_body(
    width, tests_hbm, omega_hbm, perms_ref, nodes_ref, out_hbm, packed_hbm, tests_ref, omega_ref, order_ref, sems
):
    rows = omega_ref.shape[0]
    chips = out_hbm.shape[0]
    come = [pltpu.make_async_copy(omega_hbm, omega_ref, sems.at[0])]
    go = [pltpu.make_async_copy(omega_ref, packed_hbm.at[:rows], sems.at[1])]
    for chip in range(chips):
        part = slice(chip * width, (chip + 1) * width)
        come.append(
            pltpu.make_async_copy(tests_hbm.at[:, part], tests_ref.at[chip], sems.at[2 + 2 * chip])
        )
        go.append(pltpu.make_async_copy(tests_ref.at[chip], out_hbm.at[chip], sems.at[3 + 2 * chip]))
    for copy in come:
        copy.start()
    kept = nodes_ref.shape[-1] // 2
    for order, at in ((perms_ref[0, 1:2, :kept], 0), (nodes_ref[0, 0, 1:2, :kept], 2)):
        row = lax.broadcasted_iota(jnp.int32, (order_ref.shape[0], kept), 0)
        digits = jnp.where(row == at, order // DIGIT, jnp.where(row == at + 1, order % DIGIT, 0))
        total = digits if at == 0 else total + digits
    order_ref[...] = jnp.zeros_like(order_ref)
    order_ref[:, :kept] = total.astype(F32).astype(BF)
    last = pltpu.make_async_copy(order_ref, packed_hbm.at[rows:], sems.at[2 + 2 * chips])
    last.start()
    for first, second in zip(come, go):
        first.wait()
        second.start()
    last.wait()
    for copy in go:
        copy.wait()


def dense_body(cols_ref, tiles_ref, perms_ref, interp_ref, after_ref, keep_ref, near_ref, tests_ref, dense_ref):
    del after_ref
    per_dev, slots, tile = tiles_ref.shape[:3]
    rows = per_dev * tile
    rank = interp_ref.shape[-2]
    core = lax.axis_index("sub") & 1
    first = (lax.axis_index("grp") * lax.axis_size("sub") + lax.axis_index("sub")) * per_dev
    dense_ref[...] = jnp.zeros_like(dense_ref)
    for q in range(per_dev):
        for t in range(slots):
            col = cols_ref[q, t] - first
            below, above = col < 0, col >= per_dev
            place = jnp.where(below, col + per_dev, jnp.where(above, col - per_dev, col))
            inner = jnp.where(core == 0, above, below)
            block = jnp.where(below | above, jnp.where(inner, 1, 2), 0)
            at = pl.multiple_of((block * per_dev + place) * tile, tile)
            dense_ref[q * tile : (q + 1) * tile, pl.ds(at, tile)] = tiles_ref[q, t]
    unit = eye(rank)
    keeps = []
    for i in range(2):
        keep = mm_t(unit, one_hot(perms_ref[0, i : i + 1, :rank], rows))
        rest = one_hot(perms_ref[0, i : i + 1, rank:], rows)
        every = (keep + mm_t(interp_ref[0, i], rest)).astype(BF)
        keeps.append(keep.astype(BF))
        if i == 0:
            keep_ref[rank:] = every
        else:
            tests_ref[...] = every
    keep_ref[:rank] = mm_t(keeps[1], dense_ref[:, :rows]).astype(BF)
    near_ref[...] = mm(keeps[0], dense_ref[...]).astype(BF)


def from_digits(digits, at):
    digits = digits.astype(F32)
    return (digits[at : at + 1] * DIGIT + digits[at + 1 : at + 2]).astype(jnp.int32)


def halo_body(
    dense_ref,
    near_ref,
    tests_ref,
    omega_ref,
    inner_ref,
    outer_ref,
    beside_ref,
    mine_ref,
    other_ref,
):
    rows = dense_ref.shape[0]
    rank = near_ref.shape[0]
    half = omega_ref.shape[1] // 2
    core = lax.axis_index("sub") & 1
    unit = eye(rank)
    for b, ref in enumerate((inner_ref, outer_ref)):
        order = from_digits(ref[rows:, :rank], 0)
        keep = mm_t(unit, one_hot(order, rows)).astype(BF)
        block = dense_ref[:, (b + 1) * rows : (b + 2) * rows]
        beside_ref[b * rank : (b + 1) * rank] = mm_t(keep, block).astype(BF)
    beside_ref[2 * rank :] = jnp.zeros_like(beside_ref[2 * rank :])
    beside_ref[2 * rank :, : outer_ref.shape[1]] = outer_ref[rows:]
    for out_ref, place in ((mine_ref, core), (other_ref, 1 - core)):
        cols = pl.ds(pl.multiple_of(place * half, half), half)
        own = omega_ref[:, cols]
        fwd = (
            mm(near_ref[:, :rows], own)
            + mm(near_ref[:, rows : 2 * rows], inner_ref[:rows, cols])
            + mm(near_ref[:, 2 * rows :], outer_ref[:rows, cols])
        )
        out_ref[:rank] = fwd.astype(BF)
        out_ref[rank:] = mm(tests_ref[...], own).astype(BF)


def maps_body(first, maps_ref, perms_ref, *out_refs):
    rank = maps_ref.shape[-1]
    unit = eye(rank)
    for level, out_ref in enumerate(out_refs, first):
        row_interp, col_interp, low_high, high_low = (maps_ref[0, level, i] for i in range(4))
        row_hot = one_hot(perms_ref[0, level, 0:1, :], 2 * rank)
        col_hot = one_hot(perms_ref[0, level, 1:2, :], 2 * rank)
        row_all = mm(row_hot, jnp.concatenate([unit, row_interp], axis=0)).astype(BF)
        col_all = mm(col_hot, jnp.concatenate([unit, col_interp], axis=0)).astype(BF)
        for kind, (hot, every) in enumerate(((row_hot, col_all), (col_hot, row_all))):
            keep = [mm_t(unit, hot[side * rank : (side + 1) * rank, :rank]).astype(BF) for side in range(2)]
            if kind == 0:
                cross = [mm(keep[1], high_low), mm(keep[0], low_high)]
            else:
                cross = [mm_t(keep[1], low_high), mm_t(keep[0], high_low)]
            for side in range(2):
                out_ref[kind, side, :rank] = keep[side]
                out_ref[kind, side, rank : 2 * rank] = (-cross[side]).astype(BF)
                out_ref[kind, side, 2 * rank :] = mm_t(
                    unit, every[side * rank : (side + 1) * rank]
                ).astype(BF)


def near_rim():
    sub = lax.axis_index("sub")
    return (sub & 1) != ((sub >> 1) & 1)


def merged(maps_ref, kind, side, mine_first, mine_second, other_first, other_second, rank):
    wide = mm(maps_ref[kind, side, rank:], mine_second) + mm(maps_ref[kind, 1 - side, rank:], other_second)
    kept = mm(maps_ref[kind, side, :rank], mine_first) + mm(maps_ref[kind, 1 - side, :rank], other_first)
    return kept + wide[:rank], wide[rank:]


def node_body(maps_ref, mine_ref, other_ref, out_ref):
    rank = mine_ref.shape[0] // 2
    core = lax.axis_index("sub") & 1
    kept, tests = merged(
        maps_ref, 0, core, mine_ref[:rank], mine_ref[rank:], other_ref[:rank], other_ref[rank:], rank
    )
    out_ref[:rank] = kept.astype(BF)
    out_ref[rank:] = tests.astype(BF)


def halves(panel_ref):
    rows = panel_ref.shape[1] // 2
    core = lax.axis_index("sub") & 1
    return [panel_ref[:, pl.ds(pl.multiple_of(at * rows, 128), rows)] for at in (core, 1 - core)]


def edge_body(beside_ref, beside_other, panel_ref, near_out, far_out):
    rank = near_out.shape[0]
    panel, panel_other = halves(panel_ref)
    mine = mm_t(beside_ref[rank : 2 * rank], panel)
    other = mm_t(beside_other[rank : 2 * rank], panel_other)
    near = near_rim()
    near_out[...] = jnp.where(near, mine, other).astype(BF)
    far_out[...] = jnp.where(near, other, mine).astype(BF)


def adjoint_body(
    maps_ref, keep_ref, keep_other, beside_ref, beside_other, panel_ref, after_ref, out_ref
):
    del after_ref
    rank = keep_ref.shape[0] // 2
    core = lax.axis_index("sub") & 1
    panel, panel_other = halves(panel_ref)
    mine = mm_t(keep_ref[...], panel)
    other = mm_t(keep_other[...], panel_other)
    to_other = mm_t(beside_ref[:rank], panel)
    to_mine = mm_t(beside_other[:rank], panel_other)
    kept, tests = merged(
        maps_ref,
        1,
        core,
        (mine[:rank] + to_mine).astype(BF),
        mine[rank:].astype(BF),
        (other[:rank] + to_other).astype(BF),
        other[rank:].astype(BF),
        rank,
    )
    out_ref[:rank] = kept.astype(BF)
    out_ref[rank:] = tests.astype(BF)


def rim_body(beside_ref, beside_other, near_ref, far_ref, out_ref):
    rank = near_ref.shape[0]
    chip = (lax.axis_index("sub") >> 1) & 1
    digits = [ref[2 * rank :, :rank].astype(F32) for ref in (beside_ref, beside_other)]
    order = from_digits(jnp.where(near_rim(), *digits), 2)
    hot = one_hot(order, 2 * rank)
    keeps = [mm_t(eye(rank), hot[side * rank : (side + 1) * rank]) for side in range(2)]
    upper = chip == 1
    near_keep = jnp.where(upper, keeps[1], keeps[0]).astype(BF)
    far_keep = jnp.where(upper, keeps[0], keeps[1]).astype(BF)
    out_ref[...] = (mm(near_keep, near_ref[...]) + mm(far_keep, far_ref[...])).astype(BF)


def joined_body(bit, maps_ref, mine_ref, other_ref, added_ref, given_ref, out_ref, node_ref):
    rank = added_ref.shape[0]
    side = (lax.axis_index("sub") >> bit) & 1
    mine = (mine_ref[:rank].astype(F32) + added_ref[...].astype(F32)).astype(BF)
    other = (other_ref[:rank].astype(F32) + given_ref[...].astype(F32)).astype(BF)
    node_ref[...] = mine
    kept, tests = merged(maps_ref, 1, side, mine, mine_ref[rank:], other, other_ref[rank:], rank)
    out_ref[:rank] = kept.astype(BF)
    out_ref[rank:] = tests.astype(BF)


def level_body(kind, axis, bit, maps_ref, mine_ref, other_ref, out_ref):
    rank = mine_ref.shape[0] // 2
    side = (lax.axis_index(axis) >> bit) & 1
    kept, tests = merged(
        maps_ref, kind, side, mine_ref[:rank], mine_ref[rank:], other_ref[:rank], other_ref[rank:], rank
    )
    out_ref[:rank] = kept.astype(BF)
    out_ref[rank:] = tests.astype(BF)


def last_body(axis, bit, levels, maps_ref, *refs):
    out_ref = refs[-1]
    rank = out_ref.shape[2]
    side = (lax.axis_index(axis) >> bit) & 1
    for kind in range(2):
        nodes = refs[kind * levels : kind * levels + levels - 1]
        mine_ref, other_ref = nodes[-1], refs[kind * levels + levels - 1]
        for level, ref in enumerate(nodes):
            out_ref[level, kind] = ref[:rank]
        kept, _ = merged(
            maps_ref,
            kind,
            side,
            mine_ref[:rank],
            mine_ref[rank:],
            other_ref[:rank],
            other_ref[rank:],
            rank,
        )
        out_ref[levels - 1, kind] = kept.astype(BF)


def output_body(vectors, mine_ref, other_ref, out_ref):
    half = mine_ref.shape[-1]
    core = lax.axis_index("sub") & 1
    k = lax.broadcasted_iota(jnp.int32, (half, 2 * half), 0)
    s = lax.broadcasted_iota(jnp.int32, (half, 2 * half), 1)
    base = k + k // vectors * vectors
    to_mine = jnp.where(s == base + core * vectors, 1.0, 0.0).astype(BF)
    to_other = jnp.where(s == base + (1 - core) * vectors, 1.0, 0.0).astype(BF)
    mine_cols = pl.ds(pl.multiple_of(core * half, half), half)
    other_cols = pl.ds(pl.multiple_of((1 - core) * half, half), half)
    for level in range(mine_ref.shape[0]):
        mine, other = mine_ref[level], other_ref[level]
        out_ref[0, level, 0, :, mine_cols] = mine[0]
        out_ref[0, level, 0, :, other_cols] = other[0]
        out_ref[0, level, 1] = (mm(mine[1], to_mine) + mm(other[1], to_other)).astype(BF)


def swapped(x, axis, bit):
    return lax.ppermute(x, axis, [(i, i ^ (1 << bit)) for i in range(lax.axis_size(axis))])


def local(omega, adj_tests, near_tiles, tile_cols, leaf_perms, leaf_interp, node_perms, node_maps):
    rows, samples = omega.shape
    half = samples // 2
    vectors = adj_tests.shape[0]
    rank = leaf_interp.shape[-1]
    levels = node_maps.shape[1]
    count = lax.axis_size("sub")
    chips = count // 2
    sub_bits = count.bit_length() - 1
    outward = [(i, i + 1) for i in range(1, count - 1, 2)]
    outward += [(j, i) for i, j in outward] + [(0, 0), (count - 1, count - 1)]

    blocks, packed = call(
        functools.partial(pack_body, 2 * rows),
        [shape((chips, vectors, 2 * rows)), shape((rows + 16, samples))],
        (adj_tests, omega, leaf_perms, node_perms),
        scratch=[
            pltpu.VMEM((chips, vectors, 2 * rows), BF),
            pltpu.VMEM(omega.shape, BF),
            pltpu.VMEM((16, samples), BF),
            pltpu.SemaphoreType.DMA((2 * chips + 3,)),
        ],
        specs="hhvv",
        out="a",
        limit=56 << 20,
    )
    packed_outer = lax.ppermute(packed, "sub", outward)
    packed_inner = swapped(packed, "sub", 0)
    groups = [[2 * m + c for m in range(chips)] for c in range(2)]
    panel = lax.all_to_all(
        blocks, "sub", split_axis=0, concat_axis=0, tiled=True, axis_index_groups=groups
    ).reshape(half, 2 * rows)

    tables = shape((2, 2, 3 * rank, rank))
    [first_maps] = call(
        functools.partial(maps_body, 0),
        [tables],
        (node_maps, node_perms),
        flops=1 << 30,
    )
    keep, near, tests, dense = call(
        dense_body,
        [
            shape((2 * rank, rows)),
            shape((rank, 3 * rows)),
            shape((rank, rows)),
            shape((rows, 3 * rows)),
        ],
        (tile_cols, near_tiles, leaf_perms, jnp.swapaxes(leaf_interp, 2, 3), first_maps),
        specs="svvva",
        flops=1 << 30,
    )
    keep_other = swapped(keep, "sub", 0)
    beside, fwd_mine, fwd_send = call(
        halo_body,
        [shape((2 * rank + 16, rows))] + [shape((2 * rank, half))] * 2,
        (dense, near, tests, omega, packed_inner, packed_outer),
    )
    beside_other = swapped(beside, "sub", 0)
    fwd = call(
        node_body, shape((2 * rank, half)), (first_maps, fwd_mine, swapped(fwd_send, "sub", 0))
    )
    near_rims, far_rims = call(
        edge_body, [shape((rank, half))] * 2, (beside, beside_other, panel)
    )
    ring = list(range(1, chips, 2)) + list(range(chips - 2, -1, -2))
    route = [(2 * a + c, 2 * b + c) for a, b in zip(ring, ring[1:] + ring[:1]) for c in range(2)]
    far_rims = lax.ppermute(far_rims, "sub", route)
    adj = call(
        adjoint_body,
        shape((2 * rank, half)),
        (first_maps, keep, keep_other, beside, beside_other, panel, near_rims),
        specs="vvvvvva",
        flops=4 << 30,
    )
    given = call(rim_body, shape((rank, half)), (beside, beside_other, near_rims, far_rims))
    more_maps = call(
        functools.partial(maps_body, 1), [tables] * (levels - 1), (node_maps, node_perms)
    )
    maps = [first_maps, *more_maps]
    new, node = call(
        functools.partial(joined_body, 1),
        [shape((2 * rank, half)), shape((rank, half))],
        (maps[1], adj, swapped(adj, "sub", 1), swapped(given, "sub", 1), given),
    )
    chains = [[fwd], [node, new]]
    steps = [("sub", bit) for bit in range(1, sub_bits)]
    steps += [("grp", bit) for bit in range(levels - sub_bits)]
    for level, (axis, bit) in enumerate(steps[:-1], 1):
        for kind, chain in enumerate(chains):
            if len(chain) == level:
                chain.append(
                    call(
                        functools.partial(level_body, kind, axis, bit),
                        shape((2 * rank, half)),
                        (maps[level], chain[-1], swapped(chain[-1], axis, bit)),
                    )
                )
    axis, bit = steps[-1]
    ends = [swapped(chain[-1], axis, bit) for chain in chains]
    x = call(
        functools.partial(last_body, axis, bit, levels),
        shape((levels, 2, rank, half)),
        (maps[-1], *chains[0], ends[0], *chains[1], ends[1]),
    )
    return call(
        functools.partial(output_body, vectors),
        shape((1, levels, 2, rank, samples)),
        (x, swapped(x, "sub", 0)),
    )


def solution(mesh):
    both = ("grp", "sub")
    return jax.shard_map(
        local,
        mesh=mesh,
        in_specs=(
            P(both, None),
            P("sub", "grp"),
            P(both, None, None, None),
            P(both, None),
            P(both, None, None),
            P(both, None, None, None),
            P(both, None, None, None),
            P(both, None, None, None, None),
        ),
        out_specs=P(both, None, None, None, None),
        check_vma=False,
    )
```

```python
import functools

import jax
import jax.numpy as jnp
from jax import lax
from jax.experimental import pallas as pl
from jax.experimental.pallas import tpu as pltpu
from jax.sharding import PartitionSpec as P

BF = jnp.bfloat16
F32 = jnp.float32
SPACES = {
    "h": pl.BlockSpec(memory_space=pltpu.HBM),
    "a": pl.BlockSpec(memory_space=pl.ANY),
    "s": pl.BlockSpec(memory_space=pltpu.SMEM),
    "v": pl.BlockSpec(memory_space=pltpu.VMEM),
}


def mm(a, b):
    return jnp.dot(a, b, preferred_element_type=F32)


def mm_t(a, b):
    return lax.dot_general(a, b, (((1,), (1,)), ((), ())), preferred_element_type=F32)


def eye(n):
    same = lax.broadcasted_iota(jnp.int32, (n, n), 0) == lax.broadcasted_iota(jnp.int32, (n, n), 1)
    return jnp.where(same, 1.0, 0.0).astype(BF)


def one_hot(order, n):
    hit = lax.broadcasted_iota(jnp.int32, (n, order.shape[1]), 0) == order
    return jnp.where(hit, 1.0, 0.0).astype(BF)


def call(body, out_shape, args, scratch=(), specs=None, out="v", limit=40 << 20, flops=1000):
    return pl.pallas_call(
        body,
        out_shape=out_shape,
        in_specs=[SPACES[c] for c in specs or "v" * len(args)],
        out_specs=jax.tree.map(lambda _: SPACES[out], out_shape),
        scratch_shapes=list(scratch),
        compiler_params=pltpu.CompilerParams(vmem_limit_bytes=limit),
        cost_estimate=pl.CostEstimate(flops=flops, bytes_accessed=1000, transcendentals=0),
    )(*args)


def shape(dims, dtype=BF):
    return jax.ShapeDtypeStruct(dims, dtype)


DIGIT = 32


def pack_body(
    width, tests_hbm, omega_hbm, perms_ref, nodes_ref, out_hbm, packed_hbm, tests_ref, omega_ref, order_ref, sems
):
    rows = omega_ref.shape[0]
    chips = out_hbm.shape[0]
    come = [pltpu.make_async_copy(omega_hbm, omega_ref, sems.at[0])]
    go = [pltpu.make_async_copy(omega_ref, packed_hbm.at[:rows], sems.at[1])]
    for chip in range(chips):
        part = slice(chip * width, (chip + 1) * width)
        come.append(
            pltpu.make_async_copy(tests_hbm.at[:, part], tests_ref.at[chip], sems.at[2 + 2 * chip])
        )
        go.append(pltpu.make_async_copy(tests_ref.at[chip], out_hbm.at[chip], sems.at[3 + 2 * chip]))
    for copy in come:
        copy.start()
    kept = nodes_ref.shape[-1] // 2
    for order, at in ((perms_ref[0, 1:2, :kept], 0), (nodes_ref[0, 0, 1:2, :kept], 2)):
        row = lax.broadcasted_iota(jnp.int32, (order_ref.shape[0], kept), 0)
        digits = jnp.where(row == at, order // DIGIT, jnp.where(row == at + 1, order % DIGIT, 0))
        total = digits if at == 0 else total + digits
    order_ref[...] = jnp.zeros_like(order_ref)
    order_ref[:, :kept] = total.astype(F32).astype(BF)
    last = pltpu.make_async_copy(order_ref, packed_hbm.at[rows:], sems.at[2 + 2 * chips])
    last.start()
    for first, second in zip(come, go):
        first.wait()
        second.start()
    last.wait()
    for copy in go:
        copy.wait()


def dense_body(cols_ref, tiles_ref, perms_ref, interp_ref, after_ref, keep_ref, near_ref, tests_ref, dense_ref):
    del after_ref
    per_dev, slots, tile = tiles_ref.shape[:3]
    rows = per_dev * tile
    rank = interp_ref.shape[-2]
    core = lax.axis_index("sub") & 1
    first = (lax.axis_index("grp") * lax.axis_size("sub") + lax.axis_index("sub")) * per_dev
    dense_ref[...] = jnp.zeros_like(dense_ref)
    for q in range(per_dev):
        for t in range(slots):
            col = cols_ref[q, t] - first
            below, above = col < 0, col >= per_dev
            place = jnp.where(below, col + per_dev, jnp.where(above, col - per_dev, col))
            inner = jnp.where(core == 0, above, below)
            block = jnp.where(below | above, jnp.where(inner, 1, 2), 0)
            at = pl.multiple_of((block * per_dev + place) * tile, tile)
            dense_ref[q * tile : (q + 1) * tile, pl.ds(at, tile)] = tiles_ref[q, t]
    unit = eye(rank)
    keeps = []
    for i in range(2):
        keep = mm_t(unit, one_hot(perms_ref[0, i : i + 1, :rank], rows))
        rest = one_hot(perms_ref[0, i : i + 1, rank:], rows)
        every = (keep + mm_t(interp_ref[0, i], rest)).astype(BF)
        keeps.append(keep.astype(BF))
        if i == 0:
            keep_ref[rank:] = every
        else:
            tests_ref[...] = every
    keep_ref[:rank] = mm_t(keeps[1], dense_ref[:, :rows]).astype(BF)
    near_ref[...] = mm(keeps[0], dense_ref[...]).astype(BF)


def from_digits(digits, at):
    digits = digits.astype(F32)
    return (digits[at : at + 1] * DIGIT + digits[at + 1 : at + 2]).astype(jnp.int32)


def halo_body(
    dense_ref,
    near_ref,
    tests_ref,
    omega_ref,
    inner_ref,
    outer_ref,
    beside_ref,
    mine_ref,
    other_ref,
):
    rows = dense_ref.shape[0]
    rank = near_ref.shape[0]
    half = omega_ref.shape[1] // 2
    core = lax.axis_index("sub") & 1
    unit = eye(rank)
    for b, ref in enumerate((inner_ref, outer_ref)):
        order = from_digits(ref[rows:, :rank], 0)
        keep = mm_t(unit, one_hot(order, rows)).astype(BF)
        block = dense_ref[:, (b + 1) * rows : (b + 2) * rows]
        beside_ref[b * rank : (b + 1) * rank] = mm_t(keep, block).astype(BF)
    beside_ref[2 * rank :] = jnp.zeros_like(beside_ref[2 * rank :])
    beside_ref[2 * rank :, : outer_ref.shape[1]] = outer_ref[rows:]
    for out_ref, place in ((mine_ref, core), (other_ref, 1 - core)):
        cols = pl.ds(pl.multiple_of(place * half, half), half)
        own = omega_ref[:, cols]
        fwd = (
            mm(near_ref[:, :rows], own)
            + mm(near_ref[:, rows : 2 * rows], inner_ref[:rows, cols])
            + mm(near_ref[:, 2 * rows :], outer_ref[:rows, cols])
        )
        out_ref[:rank] = fwd.astype(BF)
        out_ref[rank:] = mm(tests_ref[...], own).astype(BF)


def maps_body(maps_ref, perms_ref, *out_refs):
    rank = maps_ref.shape[-1]
    unit = eye(rank)
    for level, out_ref in enumerate(out_refs):
        row_interp, col_interp, low_high, high_low = (maps_ref[0, level, i] for i in range(4))
        row_hot = one_hot(perms_ref[0, level, 0:1, :], 2 * rank)
        col_hot = one_hot(perms_ref[0, level, 1:2, :], 2 * rank)
        row_all = mm(row_hot, jnp.concatenate([unit, row_interp], axis=0)).astype(BF)
        col_all = mm(col_hot, jnp.concatenate([unit, col_interp], axis=0)).astype(BF)
        for kind, (hot, every) in enumerate(((row_hot, col_all), (col_hot, row_all))):
            keep = [mm_t(unit, hot[side * rank : (side + 1) * rank, :rank]).astype(BF) for side in range(2)]
            if kind == 0:
                cross = [mm(keep[1], high_low), mm(keep[0], low_high)]
            else:
                cross = [mm_t(keep[1], low_high), mm_t(keep[0], high_low)]
            for side in range(2):
                out_ref[kind, side, :rank] = keep[side]
                out_ref[kind, side, rank : 2 * rank] = (-cross[side]).astype(BF)
                out_ref[kind, side, 2 * rank :] = mm_t(
                    unit, every[side * rank : (side + 1) * rank]
                ).astype(BF)


def near_rim():
    sub = lax.axis_index("sub")
    return (sub & 1) != ((sub >> 1) & 1)


def merged(maps_ref, kind, side, mine_first, mine_second, other_first, other_second, rank):
    wide = mm(maps_ref[kind, side, rank:], mine_second) + mm(maps_ref[kind, 1 - side, rank:], other_second)
    kept = mm(maps_ref[kind, side, :rank], mine_first) + mm(maps_ref[kind, 1 - side, :rank], other_first)
    return kept + wide[:rank], wide[rank:]


def node_body(maps_ref, mine_ref, other_ref, after_ref, out_ref):
    del after_ref
    rank = mine_ref.shape[0] // 2
    core = lax.axis_index("sub") & 1
    kept, tests = merged(
        maps_ref, 0, core, mine_ref[:rank], mine_ref[rank:], other_ref[:rank], other_ref[rank:], rank
    )
    out_ref[:rank] = kept.astype(BF)
    out_ref[rank:] = tests.astype(BF)


def halves(panel_ref):
    rows = panel_ref.shape[1] // 2
    core = lax.axis_index("sub") & 1
    return [panel_ref[:, pl.ds(pl.multiple_of(at * rows, 128), rows)] for at in (core, 1 - core)]


def edge_body(beside_ref, beside_other, panel_ref, near_out, far_out):
    rank = near_out.shape[0]
    panel, panel_other = halves(panel_ref)
    mine = mm_t(beside_ref[rank : 2 * rank], panel)
    other = mm_t(beside_other[rank : 2 * rank], panel_other)
    near = near_rim()
    near_out[...] = jnp.where(near, mine, other).astype(BF)
    far_out[...] = jnp.where(near, other, mine).astype(BF)


def adjoint_body(
    maps_ref, keep_ref, keep_other, beside_ref, beside_other, panel_ref, after_ref, out_ref
):
    del after_ref
    rank = keep_ref.shape[0] // 2
    core = lax.axis_index("sub") & 1
    panel, panel_other = halves(panel_ref)
    mine = mm_t(keep_ref[...], panel)
    other = mm_t(keep_other[...], panel_other)
    to_other = mm_t(beside_ref[:rank], panel)
    to_mine = mm_t(beside_other[:rank], panel_other)
    kept, tests = merged(
        maps_ref,
        1,
        core,
        (mine[:rank] + to_mine).astype(BF),
        mine[rank:].astype(BF),
        (other[:rank] + to_other).astype(BF),
        other[rank:].astype(BF),
        rank,
    )
    out_ref[:rank] = kept.astype(BF)
    out_ref[rank:] = tests.astype(BF)


def rim_body(beside_ref, beside_other, near_ref, far_ref, out_ref):
    rank = near_ref.shape[0]
    chip = (lax.axis_index("sub") >> 1) & 1
    digits = [ref[2 * rank :, :rank].astype(F32) for ref in (beside_ref, beside_other)]
    order = from_digits(jnp.where(near_rim(), *digits), 2)
    hot = one_hot(order, 2 * rank)
    keeps = [mm_t(eye(rank), hot[side * rank : (side + 1) * rank]) for side in range(2)]
    upper = chip == 1
    near_keep = jnp.where(upper, keeps[1], keeps[0]).astype(BF)
    far_keep = jnp.where(upper, keeps[0], keeps[1]).astype(BF)
    out_ref[...] = (mm(near_keep, near_ref[...]) + mm(far_keep, far_ref[...])).astype(BF)


def joined_body(bit, maps_ref, mine_ref, other_ref, added_ref, given_ref, out_ref, node_ref):
    rank = added_ref.shape[0]
    side = (lax.axis_index("sub") >> bit) & 1
    mine = (mine_ref[:rank].astype(F32) + added_ref[...].astype(F32)).astype(BF)
    other = (other_ref[:rank].astype(F32) + given_ref[...].astype(F32)).astype(BF)
    node_ref[...] = mine
    kept, tests = merged(maps_ref, 1, side, mine, mine_ref[rank:], other, other_ref[rank:], rank)
    out_ref[:rank] = kept.astype(BF)
    out_ref[rank:] = tests.astype(BF)


def level_body(kind, axis, bit, maps_ref, mine_ref, other_ref, out_ref):
    rank = mine_ref.shape[0] // 2
    side = (lax.axis_index(axis) >> bit) & 1
    kept, tests = merged(
        maps_ref, kind, side, mine_ref[:rank], mine_ref[rank:], other_ref[:rank], other_ref[rank:], rank
    )
    out_ref[:rank] = kept.astype(BF)
    out_ref[rank:] = tests.astype(BF)


def last_body(axis, bit, levels, maps_ref, *refs):
    out_ref = refs[-1]
    rank = out_ref.shape[2]
    side = (lax.axis_index(axis) >> bit) & 1
    for kind in range(2):
        nodes = refs[kind * levels : kind * levels + levels - 1]
        mine_ref, other_ref = nodes[-1], refs[kind * levels + levels - 1]
        for level, ref in enumerate(nodes):
            out_ref[level, kind] = ref[:rank]
        kept, _ = merged(
            maps_ref,
            kind,
            side,
            mine_ref[:rank],
            mine_ref[rank:],
            other_ref[:rank],
            other_ref[rank:],
            rank,
        )
        out_ref[levels - 1, kind] = kept.astype(BF)


def output_body(vectors, mine_ref, other_ref, out_ref):
    half = mine_ref.shape[-1]
    core = lax.axis_index("sub") & 1
    k = lax.broadcasted_iota(jnp.int32, (half, 2 * half), 0)
    s = lax.broadcasted_iota(jnp.int32, (half, 2 * half), 1)
    base = k + k // vectors * vectors
    to_mine = jnp.where(s == base + core * vectors, 1.0, 0.0).astype(BF)
    to_other = jnp.where(s == base + (1 - core) * vectors, 1.0, 0.0).astype(BF)
    mine_cols = pl.ds(pl.multiple_of(core * half, half), half)
    other_cols = pl.ds(pl.multiple_of((1 - core) * half, half), half)
    for level in range(mine_ref.shape[0]):
        mine, other = mine_ref[level], other_ref[level]
        out_ref[0, level, 0, :, mine_cols] = mine[0]
        out_ref[0, level, 0, :, other_cols] = other[0]
        out_ref[0, level, 1] = (mm(mine[1], to_mine) + mm(other[1], to_other)).astype(BF)


def swapped(x, axis, bit):
    return lax.ppermute(x, axis, [(i, i ^ (1 << bit)) for i in range(lax.axis_size(axis))])


def local(omega, adj_tests, near_tiles, tile_cols, leaf_perms, leaf_interp, node_perms, node_maps):
    rows, samples = omega.shape
    half = samples // 2
    vectors = adj_tests.shape[0]
    rank = leaf_interp.shape[-1]
    levels = node_maps.shape[1]
    count = lax.axis_size("sub")
    chips = count // 2
    sub_bits = count.bit_length() - 1
    outward = [(i, i + 1) for i in range(1, count - 1, 2)]
    outward += [(j, i) for i, j in outward] + [(0, 0), (count - 1, count - 1)]

    blocks, packed = call(
        functools.partial(pack_body, 2 * rows),
        [shape((chips, vectors, 2 * rows)), shape((rows + 16, samples))],
        (adj_tests, omega, leaf_perms, node_perms),
        scratch=[
            pltpu.VMEM((chips, vectors, 2 * rows), BF),
            pltpu.VMEM(omega.shape, BF),
            pltpu.VMEM((16, samples), BF),
            pltpu.SemaphoreType.DMA((2 * chips + 3,)),
        ],
        specs="hhvv",
        out="a",
        limit=56 << 20,
    )
    packed_outer = lax.ppermute(packed, "sub", outward)
    packed_inner = swapped(packed, "sub", 0)
    groups = [[2 * m + c for m in range(chips)] for c in range(2)]
    panel = lax.all_to_all(
        blocks, "sub", split_axis=0, concat_axis=0, tiled=True, axis_index_groups=groups
    ).reshape(half, 2 * rows)

    tables = shape((2, 2, 3 * rank, rank))
    maps = call(
        maps_body,
        [tables] * levels,
        (node_maps, node_perms),
        flops=1 << 30,
    )
    keep, near, tests, dense = call(
        dense_body,
        [
            shape((2 * rank, rows)),
            shape((rank, 3 * rows)),
            shape((rank, rows)),
            shape((rows, 3 * rows)),
        ],
        (tile_cols, near_tiles, leaf_perms, jnp.swapaxes(leaf_interp, 2, 3), maps[0]),
        specs="svvva",
        flops=1 << 30,
    )
    keep_other = swapped(keep, "sub", 0)
    beside, fwd_mine, fwd_send = call(
        halo_body,
        [shape((2 * rank + 16, rows))] + [shape((2 * rank, half))] * 2,
        (dense, near, tests, omega, packed_inner, packed_outer),
    )
    beside_other = swapped(beside, "sub", 0)
    fwd_other = swapped(fwd_send, "sub", 0)
    near_rims, far_rims = call(
        edge_body, [shape((rank, half))] * 2, (beside, beside_other, panel)
    )
    ring = list(range(1, chips, 2)) + list(range(chips - 2, -1, -2))
    route = [(2 * a + c, 2 * b + c) for a, b in zip(ring, ring[1:] + ring[:1]) for c in range(2)]
    far_rims = lax.ppermute(far_rims, "sub", route)
    fwd = call(
        node_body,
        shape((2 * rank, half)),
        (maps[0], fwd_mine, fwd_other, near_rims),
        specs="vvva",
    )
    adj = call(
        adjoint_body,
        shape((2 * rank, half)),
        (maps[0], keep, keep_other, beside, beside_other, panel, near_rims),
        specs="vvvvvva",
        flops=4 << 30,
    )
    given = call(rim_body, shape((rank, half)), (beside, beside_other, near_rims, far_rims))
    new, node = call(
        functools.partial(joined_body, 1),
        [shape((2 * rank, half)), shape((rank, half))],
        (maps[1], adj, swapped(adj, "sub", 1), swapped(given, "sub", 1), given),
    )
    chains = [[fwd], [node, new]]
    steps = [("sub", bit) for bit in range(1, sub_bits)]
    steps += [("grp", bit) for bit in range(levels - sub_bits)]
    for level, (axis, bit) in enumerate(steps[:-1], 1):
        for kind, chain in enumerate(chains):
            if len(chain) == level:
                chain.append(
                    call(
                        functools.partial(level_body, kind, axis, bit),
                        shape((2 * rank, half)),
                        (maps[level], chain[-1], swapped(chain[-1], axis, bit)),
                    )
                )
    axis, bit = steps[-1]
    ends = [swapped(chain[-1], axis, bit) for chain in chains]
    x = call(
        functools.partial(last_body, axis, bit, levels),
        shape((levels, 2, rank, half)),
        (maps[-1], *chains[0], ends[0], *chains[1], ends[1]),
    )
    return call(
        functools.partial(output_body, vectors),
        shape((1, levels, 2, rank, samples)),
        (x, swapped(x, "sub", 0)),
    )


def solution(mesh):
    both = ("grp", "sub")
    return jax.shard_map(
        local,
        mesh=mesh,
        in_specs=(
            P(both, None),
            P("sub", "grp"),
            P(both, None, None, None),
            P(both, None),
            P(both, None, None),
            P(both, None, None, None),
            P(both, None, None, None),
            P(both, None, None, None, None),
        ),
        out_specs=P(both, None, None, None, None),
        check_vma=False,
    )
```

```python
import functools

import jax
import jax.numpy as jnp
from jax import lax
from jax.experimental import pallas as pl
from jax.experimental.pallas import tpu as pltpu
from jax.sharding import PartitionSpec as P

BF = jnp.bfloat16
F32 = jnp.float32
SPACES = {
    "h": pl.BlockSpec(memory_space=pltpu.HBM),
    "a": pl.BlockSpec(memory_space=pl.ANY),
    "s": pl.BlockSpec(memory_space=pltpu.SMEM),
    "v": pl.BlockSpec(memory_space=pltpu.VMEM),
}


def mm(a, b):
    return jnp.dot(a, b, preferred_element_type=F32)


def mm_t(a, b):
    return lax.dot_general(a, b, (((1,), (1,)), ((), ())), preferred_element_type=F32)


def eye(n):
    same = lax.broadcasted_iota(jnp.int32, (n, n), 0) == lax.broadcasted_iota(jnp.int32, (n, n), 1)
    return jnp.where(same, 1.0, 0.0).astype(BF)


def one_hot(order, n):
    hit = lax.broadcasted_iota(jnp.int32, (n, order.shape[1]), 0) == order
    return jnp.where(hit, 1.0, 0.0).astype(BF)


def call(body, out_shape, args, scratch=(), specs=None, out="v", limit=40 << 20, flops=1000):
    return pl.pallas_call(
        body,
        out_shape=out_shape,
        in_specs=[SPACES[c] for c in specs or "v" * len(args)],
        out_specs=jax.tree.map(lambda _: SPACES[out], out_shape),
        scratch_shapes=list(scratch),
        compiler_params=pltpu.CompilerParams(vmem_limit_bytes=limit),
        cost_estimate=pl.CostEstimate(flops=flops, bytes_accessed=1000, transcendentals=0),
    )(*args)


def shape(dims, dtype=BF):
    return jax.ShapeDtypeStruct(dims, dtype)


DIGIT = 32


def pack_body(
    width, tests_hbm, omega_hbm, perms_ref, nodes_ref, out_hbm, packed_hbm, tests_ref, omega_ref, order_ref, sems
):
    rows = omega_ref.shape[0]
    chips = out_hbm.shape[0]
    come = [pltpu.make_async_copy(omega_hbm, omega_ref, sems.at[0])]
    go = [pltpu.make_async_copy(omega_ref, packed_hbm.at[:rows], sems.at[1])]
    for chip in range(chips):
        part = slice(chip * width, (chip + 1) * width)
        come.append(
            pltpu.make_async_copy(tests_hbm.at[:, part], tests_ref.at[chip], sems.at[2 + 2 * chip])
        )
        go.append(pltpu.make_async_copy(tests_ref.at[chip], out_hbm.at[chip], sems.at[3 + 2 * chip]))
    for copy in come:
        copy.start()
    kept = nodes_ref.shape[-1] // 2
    for order, at in ((perms_ref[0, 1:2, :kept], 0), (nodes_ref[0, 0, 1:2, :kept], 2)):
        row = lax.broadcasted_iota(jnp.int32, (order_ref.shape[0], kept), 0)
        digits = jnp.where(row == at, order // DIGIT, jnp.where(row == at + 1, order % DIGIT, 0))
        total = digits if at == 0 else total + digits
    order_ref[...] = jnp.zeros_like(order_ref)
    order_ref[:, :kept] = total.astype(F32).astype(BF)
    last = pltpu.make_async_copy(order_ref, packed_hbm.at[rows:], sems.at[2 + 2 * chips])
    last.start()
    for first, second in zip(come, go):
        first.wait()
        second.start()
    last.wait()
    for copy in go:
        copy.wait()


def dense_body(cols_ref, tiles_ref, perms_ref, interp_ref, after_ref, keep_ref, near_ref, tests_ref, dense_ref):
    del after_ref
    per_dev, slots, tile = tiles_ref.shape[:3]
    rows = per_dev * tile
    rank = interp_ref.shape[-2]
    core = lax.axis_index("sub") & 1
    first = (lax.axis_index("grp") * lax.axis_size("sub") + lax.axis_index("sub")) * per_dev
    dense_ref[...] = jnp.zeros_like(dense_ref)
    for q in range(per_dev):
        for t in range(slots):
            col = cols_ref[q, t] - first
            below, above = col < 0, col >= per_dev
            place = jnp.where(below, col + per_dev, jnp.where(above, col - per_dev, col))
            inner = jnp.where(core == 0, above, below)
            block = jnp.where(below | above, jnp.where(inner, 1, 2), 0)
            at = pl.multiple_of((block * per_dev + place) * tile, tile)
            dense_ref[q * tile : (q + 1) * tile, pl.ds(at, tile)] = tiles_ref[q, t]
    unit = eye(rank)
    keeps = []
    for i in range(2):
        keep = mm_t(unit, one_hot(perms_ref[0, i : i + 1, :rank], rows))
        rest = one_hot(perms_ref[0, i : i + 1, rank:], rows)
        every = (keep + mm_t(interp_ref[0, i], rest)).astype(BF)
        keeps.append(keep.astype(BF))
        if i == 0:
            keep_ref[rank:] = every
        else:
            tests_ref[...] = every
    keep_ref[:rank] = mm_t(keeps[1], dense_ref[:, :rows]).astype(BF)
    near_ref[...] = mm(keeps[0], dense_ref[...]).astype(BF)


def from_digits(digits, at):
    digits = digits.astype(F32)
    return (digits[at : at + 1] * DIGIT + digits[at + 1 : at + 2]).astype(jnp.int32)


def halo_body(
    keep_ref,
    dense_ref,
    near_ref,
    tests_ref,
    omega_ref,
    inner_ref,
    outer_ref,
    sel_ref,
    mine_ref,
    other_ref,
):
    rows = dense_ref.shape[0]
    rank = near_ref.shape[0]
    half = omega_ref.shape[1] // 2
    core = lax.axis_index("sub") & 1
    unit = eye(rank)
    sel_ref[: 2 * rank] = keep_ref[...]
    for b, ref in enumerate((inner_ref, outer_ref), 1):
        keep = mm_t(unit, one_hot(from_digits(ref[rows:, :rank], 0), rows)).astype(BF)
        block = dense_ref[:, b * rows : (b + 1) * rows]
        sel_ref[(b + 1) * rank : (b + 2) * rank] = mm_t(keep, block).astype(BF)
    sel_ref[4 * rank :] = jnp.zeros_like(sel_ref[4 * rank :])
    sel_ref[4 * rank :, : outer_ref.shape[1]] = outer_ref[rows:]
    for out_ref, place in ((mine_ref, core), (other_ref, 1 - core)):
        cols = pl.ds(pl.multiple_of(place * half, half), half)
        own = omega_ref[:, cols]
        fwd = (
            mm(near_ref[:, :rows], own)
            + mm(near_ref[:, rows : 2 * rows], inner_ref[:rows, cols])
            + mm(near_ref[:, 2 * rows :], outer_ref[:rows, cols])
        )
        out_ref[:rank] = fwd.astype(BF)
        out_ref[rank:] = mm(tests_ref[...], own).astype(BF)


def maps_body(maps_ref, perms_ref, *out_refs):
    rank = maps_ref.shape[-1]
    unit = eye(rank)
    for level, out_ref in enumerate(out_refs):
        row_interp, col_interp, low_high, high_low = (maps_ref[0, level, i] for i in range(4))
        row_hot = one_hot(perms_ref[0, level, 0:1, :], 2 * rank)
        col_hot = one_hot(perms_ref[0, level, 1:2, :], 2 * rank)
        row_all = mm(row_hot, jnp.concatenate([unit, row_interp], axis=0)).astype(BF)
        col_all = mm(col_hot, jnp.concatenate([unit, col_interp], axis=0)).astype(BF)
        for kind, (hot, every) in enumerate(((row_hot, col_all), (col_hot, row_all))):
            keep = [mm_t(unit, hot[side * rank : (side + 1) * rank, :rank]).astype(BF) for side in range(2)]
            if kind == 0:
                cross = [mm(keep[1], high_low), mm(keep[0], low_high)]
            else:
                cross = [mm_t(keep[1], low_high), mm_t(keep[0], high_low)]
            for side in range(2):
                out_ref[kind, side, :rank] = keep[side]
                out_ref[kind, side, rank : 2 * rank] = (-cross[side]).astype(BF)
                out_ref[kind, side, 2 * rank :] = mm_t(
                    unit, every[side * rank : (side + 1) * rank]
                ).astype(BF)


def near_rim():
    sub = lax.axis_index("sub")
    return (sub & 1) != ((sub >> 1) & 1)


def merged(maps_ref, kind, side, mine_first, mine_second, other_first, other_second, rank):
    wide = mm(maps_ref[kind, side, rank:], mine_second) + mm(maps_ref[kind, 1 - side, rank:], other_second)
    kept = mm(maps_ref[kind, side, :rank], mine_first) + mm(maps_ref[kind, 1 - side, :rank], other_first)
    return kept + wide[:rank], wide[rank:]


def node_body(maps_ref, mine_ref, other_ref, after_ref, out_ref):
    del after_ref
    rank = mine_ref.shape[0] // 2
    core = lax.axis_index("sub") & 1
    kept, tests = merged(
        maps_ref, 0, core, mine_ref[:rank], mine_ref[rank:], other_ref[:rank], other_ref[rank:], rank
    )
    out_ref[:rank] = kept.astype(BF)
    out_ref[rank:] = tests.astype(BF)


def halves(panel_ref):
    rows = panel_ref.shape[1] // 2
    core = lax.axis_index("sub") & 1
    return [panel_ref[:, pl.ds(pl.multiple_of(at * rows, 128), rows)] for at in (core, 1 - core)]


def edge_body(sel_ref, sel_other, panel_ref, near_out, far_out):
    rank = near_out.shape[0]
    panel, panel_other = halves(panel_ref)
    mine = mm_t(sel_ref[3 * rank : 4 * rank], panel)
    other = mm_t(sel_other[3 * rank : 4 * rank], panel_other)
    near = near_rim()
    near_out[...] = jnp.where(near, mine, other).astype(BF)
    far_out[...] = jnp.where(near, other, mine).astype(BF)


def adjoint_body(maps_ref, sel_ref, sel_other, panel_ref, after_ref, out_ref):
    del after_ref
    rank = out_ref.shape[0] // 2
    core = lax.axis_index("sub") & 1
    panel, panel_other = halves(panel_ref)
    mine = mm_t(sel_ref[: 3 * rank], panel)
    other = mm_t(sel_other[: 3 * rank], panel_other)
    kept, tests = merged(
        maps_ref,
        1,
        core,
        (mine[:rank] + other[2 * rank :]).astype(BF),
        mine[rank : 2 * rank].astype(BF),
        (other[:rank] + mine[2 * rank :]).astype(BF),
        other[rank : 2 * rank].astype(BF),
        rank,
    )
    out_ref[:rank] = kept.astype(BF)
    out_ref[rank:] = tests.astype(BF)


def rim_body(sel_ref, sel_other, near_ref, far_ref, adj_ref, out_ref):
    rank = near_ref.shape[0]
    chip = (lax.axis_index("sub") >> 1) & 1
    digits = [ref[4 * rank :, :rank].astype(F32) for ref in (sel_ref, sel_other)]
    order = from_digits(jnp.where(near_rim(), *digits), 2)
    hot = one_hot(order, 2 * rank)
    keeps = [mm_t(eye(rank), hot[side * rank : (side + 1) * rank]) for side in range(2)]
    upper = chip == 1
    near_keep = jnp.where(upper, keeps[1], keeps[0]).astype(BF)
    far_keep = jnp.where(upper, keeps[0], keeps[1]).astype(BF)
    out_ref[: 2 * rank] = adj_ref[...]
    out_ref[2 * rank :] = (mm(near_keep, near_ref[...]) + mm(far_keep, far_ref[...])).astype(BF)


def joined_body(bit, maps_ref, mine_ref, other_ref, out_ref, node_ref):
    rank = node_ref.shape[0]
    side = (lax.axis_index("sub") >> bit) & 1
    a, p, r = (slice(i * rank, (i + 1) * rank) for i in range(3))
    mine = (mine_ref[a].astype(F32) + other_ref[r].astype(F32)).astype(BF)
    other = (other_ref[a].astype(F32) + mine_ref[r].astype(F32)).astype(BF)
    node_ref[...] = mine
    kept, tests = merged(maps_ref, 1, side, mine, mine_ref[p], other, other_ref[p], rank)
    out_ref[:rank] = kept.astype(BF)
    out_ref[rank:] = tests.astype(BF)


def level_body(kind, axis, bit, maps_ref, mine_ref, other_ref, out_ref):
    rank = mine_ref.shape[0] // 2
    side = (lax.axis_index(axis) >> bit) & 1
    kept, tests = merged(
        maps_ref, kind, side, mine_ref[:rank], mine_ref[rank:], other_ref[:rank], other_ref[rank:], rank
    )
    out_ref[:rank] = kept.astype(BF)
    out_ref[rank:] = tests.astype(BF)


def last_body(axis, bit, levels, maps_ref, *refs):
    out_ref = refs[-1]
    rank = out_ref.shape[2]
    side = (lax.axis_index(axis) >> bit) & 1
    for kind in range(2):
        nodes = refs[kind * levels : kind * levels + levels - 1]
        mine_ref, other_ref = nodes[-1], refs[kind * levels + levels - 1]
        for level, ref in enumerate(nodes):
            out_ref[level, kind] = ref[:rank]
        kept, _ = merged(
            maps_ref,
            kind,
            side,
            mine_ref[:rank],
            mine_ref[rank:],
            other_ref[:rank],
            other_ref[rank:],
            rank,
        )
        out_ref[levels - 1, kind] = kept.astype(BF)


def output_body(vectors, mine_ref, other_ref, out_ref):
    half = mine_ref.shape[-1]
    core = lax.axis_index("sub") & 1
    k = lax.broadcasted_iota(jnp.int32, (half, 2 * half), 0)
    s = lax.broadcasted_iota(jnp.int32, (half, 2 * half), 1)
    base = k + k // vectors * vectors
    to_mine = jnp.where(s == base + core * vectors, 1.0, 0.0).astype(BF)
    to_other = jnp.where(s == base + (1 - core) * vectors, 1.0, 0.0).astype(BF)
    mine_cols = pl.ds(pl.multiple_of(core * half, half), half)
    other_cols = pl.ds(pl.multiple_of((1 - core) * half, half), half)
    for level in range(mine_ref.shape[0]):
        mine, other = mine_ref[level], other_ref[level]
        out_ref[0, level, 0, :, mine_cols] = mine[0]
        out_ref[0, level, 0, :, other_cols] = other[0]
        out_ref[0, level, 1] = (mm(mine[1], to_mine) + mm(other[1], to_other)).astype(BF)


def swapped(x, axis, bit):
    return lax.ppermute(x, axis, [(i, i ^ (1 << bit)) for i in range(lax.axis_size(axis))])


def local(omega, adj_tests, near_tiles, tile_cols, leaf_perms, leaf_interp, node_perms, node_maps):
    rows, samples = omega.shape
    half = samples // 2
    vectors = adj_tests.shape[0]
    rank = leaf_interp.shape[-1]
    levels = node_maps.shape[1]
    count = lax.axis_size("sub")
    chips = count // 2
    sub_bits = count.bit_length() - 1
    outward = [(i, i + 1) for i in range(1, count - 1, 2)]
    outward += [(j, i) for i, j in outward] + [(0, 0), (count - 1, count - 1)]

    blocks, packed = call(
        functools.partial(pack_body, 2 * rows),
        [shape((chips, vectors, 2 * rows)), shape((rows + 16, samples))],
        (adj_tests, omega, leaf_perms, node_perms),
        scratch=[
            pltpu.VMEM((chips, vectors, 2 * rows), BF),
            pltpu.VMEM(omega.shape, BF),
            pltpu.VMEM((16, samples), BF),
            pltpu.SemaphoreType.DMA((2 * chips + 3,)),
        ],
        specs="hhvv",
        out="a",
        limit=56 << 20,
    )
    packed_outer = lax.ppermute(packed, "sub", outward)
    packed_inner = swapped(packed, "sub", 0)
    groups = [[2 * m + c for m in range(chips)] for c in range(2)]
    panel = lax.all_to_all(
        blocks, "sub", split_axis=0, concat_axis=0, tiled=True, axis_index_groups=groups
    ).reshape(half, 2 * rows)

    tables = shape((2, 2, 3 * rank, rank))
    maps = call(
        maps_body,
        [tables] * levels,
        (node_maps, node_perms),
        flops=1 << 30,
    )
    keep, near, tests, dense = call(
        dense_body,
        [
            shape((2 * rank, rows)),
            shape((rank, 3 * rows)),
            shape((rank, rows)),
            shape((rows, 3 * rows)),
        ],
        (tile_cols, near_tiles, leaf_perms, jnp.swapaxes(leaf_interp, 2, 3), maps[0]),
        specs="svvva",
        flops=1 << 30,
    )
    sel, fwd_mine, fwd_send = call(
        halo_body,
        [shape((4 * rank + 16, rows))] + [shape((2 * rank, half))] * 2,
        (keep, dense, near, tests, omega, packed_inner, packed_outer),
    )
    sel_other = swapped(sel, "sub", 0)
    fwd_other = swapped(fwd_send, "sub", 0)
    near_rims, far_rims = call(edge_body, [shape((rank, half))] * 2, (sel, sel_other, panel))
    ring = list(range(1, chips, 2)) + list(range(chips - 2, -1, -2))
    route = [(2 * a + c, 2 * b + c) for a, b in zip(ring, ring[1:] + ring[:1]) for c in range(2)]
    far_rims = lax.ppermute(far_rims, "sub", route)
    fwd = call(
        node_body,
        shape((2 * rank, half)),
        (maps[0], fwd_mine, fwd_other, near_rims),
        specs="vvva",
    )
    adj = call(
        adjoint_body,
        shape((2 * rank, half)),
        (maps[0], sel, sel_other, panel, fwd),
        specs="vvvva",
        flops=4 << 30,
    )
    adj = call(rim_body, shape((3 * rank, half)), (sel, sel_other, near_rims, far_rims, adj))
    new, node = call(
        functools.partial(joined_body, 1),
        [shape((2 * rank, half)), shape((rank, half))],
        (maps[1], adj, swapped(adj, "sub", 1)),
    )
    chains = [[fwd], [node, new]]
    steps = [("sub", bit) for bit in range(1, sub_bits)]
    steps += [("grp", bit) for bit in range(levels - sub_bits)]
    for level, (axis, bit) in enumerate(steps[:-1], 1):
        for kind, chain in enumerate(chains):
            if len(chain) == level:
                chain.append(
                    call(
                        functools.partial(level_body, kind, axis, bit),
                        shape((2 * rank, half)),
                        (maps[level], chain[-1], swapped(chain[-1], axis, bit)),
                    )
                )
    axis, bit = steps[-1]
    ends = [swapped(chain[-1], axis, bit) for chain in chains]
    x = call(
        functools.partial(last_body, axis, bit, levels),
        shape((levels, 2, rank, half)),
        (maps[-1], *chains[0], ends[0], *chains[1], ends[1]),
    )
    return call(
        functools.partial(output_body, vectors),
        shape((1, levels, 2, rank, samples)),
        (x, swapped(x, "sub", 0)),
    )


def solution(mesh):
    both = ("grp", "sub")
    return jax.shard_map(
        local,
        mesh=mesh,
        in_specs=(
            P(both, None),
            P("sub", "grp"),
            P(both, None, None, None),
            P(both, None),
            P(both, None, None),
            P(both, None, None, None),
            P(both, None, None, None),
            P(both, None, None, None, None),
        ),
        out_specs=P(both, None, None, None, None),
        check_vma=False,
    )
```

```python
import functools

import jax
import jax.numpy as jnp
from jax import lax
from jax.experimental import pallas as pl
from jax.experimental.pallas import tpu as pltpu
from jax.sharding import PartitionSpec as P

BF = jnp.bfloat16
F32 = jnp.float32
SPACES = {
    "h": pl.BlockSpec(memory_space=pltpu.HBM),
    "a": pl.BlockSpec(memory_space=pl.ANY),
    "s": pl.BlockSpec(memory_space=pltpu.SMEM),
    "v": pl.BlockSpec(memory_space=pltpu.VMEM),
}


def mm(a, b):
    return jnp.dot(a, b, preferred_element_type=F32)


def mm_t(a, b):
    return lax.dot_general(a, b, (((1,), (1,)), ((), ())), preferred_element_type=F32)


def eye(n):
    same = lax.broadcasted_iota(jnp.int32, (n, n), 0) == lax.broadcasted_iota(jnp.int32, (n, n), 1)
    return jnp.where(same, 1.0, 0.0).astype(BF)


def one_hot(order, n):
    hit = lax.broadcasted_iota(jnp.int32, (n, order.shape[1]), 0) == order
    return jnp.where(hit, 1.0, 0.0).astype(BF)


def call(body, out_shape, args, scratch=(), specs=None, out="v", limit=40 << 20, flops=1000):
    return pl.pallas_call(
        body,
        out_shape=out_shape,
        in_specs=[SPACES[c] for c in specs or "v" * len(args)],
        out_specs=jax.tree.map(lambda _: SPACES[out], out_shape),
        scratch_shapes=list(scratch),
        compiler_params=pltpu.CompilerParams(vmem_limit_bytes=limit),
        cost_estimate=pl.CostEstimate(flops=flops, bytes_accessed=1000, transcendentals=0),
    )(*args)


def shape(dims, dtype=BF):
    return jax.ShapeDtypeStruct(dims, dtype)


DIGIT = 32


def pack_body(
    width, tests_hbm, omega_hbm, perms_ref, nodes_ref, out_hbm, packed_hbm, tests_ref, omega_ref, order_ref, sems
):
    rows = omega_ref.shape[0]
    chips = out_hbm.shape[0]
    come = [pltpu.make_async_copy(omega_hbm, omega_ref, sems.at[0])]
    go = [pltpu.make_async_copy(omega_ref, packed_hbm.at[:rows], sems.at[1])]
    for chip in range(chips):
        part = slice(chip * width, (chip + 1) * width)
        come.append(
            pltpu.make_async_copy(tests_hbm.at[:, part], tests_ref.at[chip], sems.at[2 + 2 * chip])
        )
        go.append(pltpu.make_async_copy(tests_ref.at[chip], out_hbm.at[chip], sems.at[3 + 2 * chip]))
    for copy in come:
        copy.start()
    kept = nodes_ref.shape[-1] // 2
    for order, at in ((perms_ref[0, 1:2, :kept], 0), (nodes_ref[0, 0, 1:2, :kept], 2)):
        row = lax.broadcasted_iota(jnp.int32, (order_ref.shape[0], kept), 0)
        digits = jnp.where(row == at, order // DIGIT, jnp.where(row == at + 1, order % DIGIT, 0))
        total = digits if at == 0 else total + digits
    order_ref[...] = jnp.zeros_like(order_ref)
    order_ref[:, :kept] = total.astype(F32).astype(BF)
    last = pltpu.make_async_copy(order_ref, packed_hbm.at[rows:], sems.at[2 + 2 * chips])
    last.start()
    for first, second in zip(come, go):
        first.wait()
        second.start()
    last.wait()
    for copy in go:
        copy.wait()


def dense_body(cols_ref, tiles_ref, perms_ref, interp_ref, after_ref, keep_ref, near_ref, tests_ref, dense_ref):
    del after_ref
    per_dev, slots, tile = tiles_ref.shape[:3]
    rows = per_dev * tile
    rank = interp_ref.shape[-2]
    core = lax.axis_index("sub") & 1
    first = (lax.axis_index("grp") * lax.axis_size("sub") + lax.axis_index("sub")) * per_dev
    dense_ref[...] = jnp.zeros_like(dense_ref)
    for q in range(per_dev):
        for t in range(slots):
            col = cols_ref[q, t] - first
            below, above = col < 0, col >= per_dev
            place = jnp.where(below, col + per_dev, jnp.where(above, col - per_dev, col))
            inner = jnp.where(core == 0, above, below)
            block = jnp.where(below | above, jnp.where(inner, 1, 2), 0)
            at = pl.multiple_of((block * per_dev + place) * tile, tile)
            dense_ref[q * tile : (q + 1) * tile, pl.ds(at, tile)] = tiles_ref[q, t]
    unit = eye(rank)
    keeps = []
    for i in range(2):
        keep = mm_t(unit, one_hot(perms_ref[0, i : i + 1, :rank], rows))
        rest = one_hot(perms_ref[0, i : i + 1, rank:], rows)
        every = (keep + mm_t(interp_ref[0, i], rest)).astype(BF)
        keeps.append(keep.astype(BF))
        if i == 0:
            keep_ref[rank:] = every
        else:
            tests_ref[...] = every
    keep_ref[:rank] = mm_t(keeps[1], dense_ref[:, :rows]).astype(BF)
    near_ref[...] = mm(keeps[0], dense_ref[...]).astype(BF)


def from_digits(digits, at):
    digits = digits.astype(F32)
    return (digits[at : at + 1] * DIGIT + digits[at + 1 : at + 2]).astype(jnp.int32)


def halo_body(
    keep_ref,
    dense_ref,
    near_ref,
    tests_ref,
    omega_ref,
    inner_ref,
    outer_ref,
    sel_ref,
    mine_ref,
    other_ref,
):
    rows = dense_ref.shape[0]
    rank = near_ref.shape[0]
    half = omega_ref.shape[1] // 2
    core = lax.axis_index("sub") & 1
    unit = eye(rank)
    sel_ref[: 2 * rank] = keep_ref[...]
    for b, ref in enumerate((inner_ref, outer_ref), 1):
        keep = mm_t(unit, one_hot(from_digits(ref[rows:, :rank], 0), rows)).astype(BF)
        block = dense_ref[:, b * rows : (b + 1) * rows]
        sel_ref[(b + 1) * rank : (b + 2) * rank] = mm_t(keep, block).astype(BF)
    sel_ref[4 * rank :] = jnp.zeros_like(sel_ref[4 * rank :])
    sel_ref[4 * rank :, : outer_ref.shape[1]] = outer_ref[rows:]
    for out_ref, place in ((mine_ref, core), (other_ref, 1 - core)):
        cols = pl.ds(pl.multiple_of(place * half, half), half)
        own = omega_ref[:, cols]
        fwd = (
            mm(near_ref[:, :rows], own)
            + mm(near_ref[:, rows : 2 * rows], inner_ref[:rows, cols])
            + mm(near_ref[:, 2 * rows :], outer_ref[:rows, cols])
        )
        out_ref[:rank] = fwd.astype(BF)
        out_ref[rank:] = mm(tests_ref[...], own).astype(BF)


def maps_body(maps_ref, perms_ref, *out_refs):
    rank = maps_ref.shape[-1]
    unit = eye(rank)
    for level, out_ref in enumerate(out_refs):
        row_interp, col_interp, low_high, high_low = (maps_ref[0, level, i] for i in range(4))
        row_hot = one_hot(perms_ref[0, level, 0:1, :], 2 * rank)
        col_hot = one_hot(perms_ref[0, level, 1:2, :], 2 * rank)
        row_all = mm(row_hot, jnp.concatenate([unit, row_interp], axis=0)).astype(BF)
        col_all = mm(col_hot, jnp.concatenate([unit, col_interp], axis=0)).astype(BF)
        for kind, (hot, every) in enumerate(((row_hot, col_all), (col_hot, row_all))):
            keep = [mm_t(unit, hot[side * rank : (side + 1) * rank, :rank]).astype(BF) for side in range(2)]
            if kind == 0:
                cross = [mm(keep[1], high_low), mm(keep[0], low_high)]
            else:
                cross = [mm_t(keep[1], low_high), mm_t(keep[0], high_low)]
            for side in range(2):
                out_ref[kind, side, :rank] = keep[side]
                out_ref[kind, side, rank : 2 * rank] = (-cross[side]).astype(BF)
                out_ref[kind, side, 2 * rank :] = mm_t(
                    unit, every[side * rank : (side + 1) * rank]
                ).astype(BF)


def near_rim():
    sub = lax.axis_index("sub")
    return (sub & 1) != ((sub >> 1) & 1)


def merged(maps_ref, kind, side, mine_first, mine_second, other_first, other_second, rank):
    wide = mm(maps_ref[kind, side, rank:], mine_second) + mm(maps_ref[kind, 1 - side, rank:], other_second)
    kept = mm(maps_ref[kind, side, :rank], mine_first) + mm(maps_ref[kind, 1 - side, :rank], other_first)
    return kept + wide[:rank], wide[rank:]


def node_body(maps_ref, mine_ref, other_ref, after_ref, out_ref):
    del after_ref
    rank = mine_ref.shape[0] // 2
    core = lax.axis_index("sub") & 1
    kept, tests = merged(
        maps_ref, 0, core, mine_ref[:rank], mine_ref[rank:], other_ref[:rank], other_ref[rank:], rank
    )
    out_ref[:rank] = kept.astype(BF)
    out_ref[rank:] = tests.astype(BF)


def halves(panel_ref):
    rows = panel_ref.shape[1] // 2
    core = lax.axis_index("sub") & 1
    return [panel_ref[:, pl.ds(pl.multiple_of(at * rows, 128), rows)] for at in (core, 1 - core)]


def edge_body(sel_ref, sel_other, panel_ref, near_out, far_out):
    rank = near_out.shape[0]
    panel, panel_other = halves(panel_ref)
    mine = mm_t(sel_ref[3 * rank : 4 * rank], panel)
    other = mm_t(sel_other[3 * rank : 4 * rank], panel_other)
    near = near_rim()
    near_out[...] = jnp.where(near, mine, other).astype(BF)
    far_out[...] = jnp.where(near, other, mine).astype(BF)


def adjoint_body(maps_ref, sel_ref, sel_other, panel_ref, after_ref, out_ref):
    del after_ref
    rank = out_ref.shape[0] // 2
    core = lax.axis_index("sub") & 1
    panel, panel_other = halves(panel_ref)
    mine = mm_t(sel_ref[: 3 * rank], panel)
    other = mm_t(sel_other[: 3 * rank], panel_other)
    kept, tests = merged(
        maps_ref,
        1,
        core,
        (mine[:rank] + other[2 * rank :]).astype(BF),
        mine[rank : 2 * rank].astype(BF),
        (other[:rank] + mine[2 * rank :]).astype(BF),
        other[rank : 2 * rank].astype(BF),
        rank,
    )
    out_ref[:rank] = kept.astype(BF)
    out_ref[rank:] = tests.astype(BF)


def rim_body(sel_ref, sel_other, near_ref, far_ref, adj_ref, out_ref):
    rank = near_ref.shape[0]
    chip = (lax.axis_index("sub") >> 1) & 1
    digits = [ref[4 * rank :, :rank].astype(F32) for ref in (sel_ref, sel_other)]
    order = from_digits(jnp.where(near_rim(), *digits), 2)
    hot = one_hot(order, 2 * rank)
    keeps = [mm_t(eye(rank), hot[side * rank : (side + 1) * rank]) for side in range(2)]
    upper = chip == 1
    near_keep = jnp.where(upper, keeps[1], keeps[0]).astype(BF)
    far_keep = jnp.where(upper, keeps[0], keeps[1]).astype(BF)
    out_ref[: 2 * rank] = adj_ref[...]
    out_ref[2 * rank :] = (mm(near_keep, near_ref[...]) + mm(far_keep, far_ref[...])).astype(BF)


def joined_body(bit, maps_ref, mine_ref, other_ref, out_ref, node_ref):
    rank = node_ref.shape[0]
    side = (lax.axis_index("sub") >> bit) & 1
    a, p, r = (slice(i * rank, (i + 1) * rank) for i in range(3))
    mine = (mine_ref[a].astype(F32) + other_ref[r].astype(F32)).astype(BF)
    other = (other_ref[a].astype(F32) + mine_ref[r].astype(F32)).astype(BF)
    node_ref[...] = mine
    kept, tests = merged(maps_ref, 1, side, mine, mine_ref[p], other, other_ref[p], rank)
    out_ref[:rank] = kept.astype(BF)
    out_ref[rank:] = tests.astype(BF)


def level_body(kind, axis, bit, maps_ref, mine_ref, other_ref, out_ref):
    rank = mine_ref.shape[0] // 2
    side = (lax.axis_index(axis) >> bit) & 1
    kept, tests = merged(
        maps_ref, kind, side, mine_ref[:rank], mine_ref[rank:], other_ref[:rank], other_ref[rank:], rank
    )
    out_ref[:rank] = kept.astype(BF)
    out_ref[rank:] = tests.astype(BF)


def last_body(axis, bit, levels, maps_ref, *refs):
    out_ref = refs[-1]
    rank = out_ref.shape[2]
    side = (lax.axis_index(axis) >> bit) & 1
    for kind in range(2):
        nodes = refs[kind * levels : kind * levels + levels - 1]
        mine_ref, other_ref = nodes[-1], refs[kind * levels + levels - 1]
        for level, ref in enumerate(nodes):
            out_ref[level, kind] = ref[:rank]
        kept, _ = merged(
            maps_ref,
            kind,
            side,
            mine_ref[:rank],
            mine_ref[rank:],
            other_ref[:rank],
            other_ref[rank:],
            rank,
        )
        out_ref[levels - 1, kind] = kept.astype(BF)


def output_body(vectors, mine_ref, other_ref, out_ref):
    half = mine_ref.shape[-1]
    core = lax.axis_index("sub") & 1
    k = lax.broadcasted_iota(jnp.int32, (half, 2 * half), 0)
    s = lax.broadcasted_iota(jnp.int32, (half, 2 * half), 1)
    base = k + k // vectors * vectors
    to_mine = jnp.where(s == base + core * vectors, 1.0, 0.0).astype(BF)
    to_other = jnp.where(s == base + (1 - core) * vectors, 1.0, 0.0).astype(BF)
    mine_cols = pl.ds(pl.multiple_of(core * half, half), half)
    other_cols = pl.ds(pl.multiple_of((1 - core) * half, half), half)
    for level in range(mine_ref.shape[0]):
        mine, other = mine_ref[level], other_ref[level]
        out_ref[0, level, 0, :, mine_cols] = mine[0]
        out_ref[0, level, 0, :, other_cols] = other[0]
        out_ref[0, level, 1] = (mm(mine[1], to_mine) + mm(other[1], to_other)).astype(BF)


def swapped(x, axis, bit):
    return lax.ppermute(x, axis, [(i, i ^ (1 << bit)) for i in range(lax.axis_size(axis))])


def local(omega, adj_tests, near_tiles, tile_cols, leaf_perms, leaf_interp, node_perms, node_maps):
    rows, samples = omega.shape
    half = samples // 2
    vectors = adj_tests.shape[0]
    rank = leaf_interp.shape[-1]
    levels = node_maps.shape[1]
    count = lax.axis_size("sub")
    chips = count // 2
    sub_bits = count.bit_length() - 1
    outward = [(i, i + 1) for i in range(1, count - 1, 2)]
    outward += [(j, i) for i, j in outward] + [(0, 0), (count - 1, count - 1)]

    blocks, packed = call(
        functools.partial(pack_body, 2 * rows),
        [shape((chips, vectors, 2 * rows)), shape((rows + 16, samples))],
        (adj_tests, omega, leaf_perms, node_perms),
        scratch=[
            pltpu.VMEM((chips, vectors, 2 * rows), BF),
            pltpu.VMEM(omega.shape, BF),
            pltpu.VMEM((16, samples), BF),
            pltpu.SemaphoreType.DMA((2 * chips + 3,)),
        ],
        specs="hhvv",
        out="a",
        limit=56 << 20,
    )
    packed_outer = lax.ppermute(packed, "sub", outward)
    packed_inner = swapped(packed, "sub", 0)
    groups = [[2 * m + c for m in range(chips)] for c in range(2)]
    panel = lax.all_to_all(
        blocks, "sub", split_axis=0, concat_axis=0, tiled=True, axis_index_groups=groups
    ).reshape(half, 2 * rows)

    tables = shape((2, 2, 3 * rank, rank))
    maps = call(
        maps_body,
        [tables] * levels,
        (node_maps, node_perms),
        flops=1 << 30,
    )
    keep, near, tests, dense = call(
        dense_body,
        [
            shape((2 * rank, rows)),
            shape((rank, 3 * rows)),
            shape((rank, rows)),
            shape((rows, 3 * rows)),
        ],
        (tile_cols, near_tiles, leaf_perms, jnp.swapaxes(leaf_interp, 2, 3), maps[0]),
        specs="svvva",
        flops=1 << 30,
    )
    sel, fwd_mine, fwd_send = call(
        halo_body,
        [shape((4 * rank + 16, rows))] + [shape((2 * rank, half))] * 2,
        (keep, dense, near, tests, omega, packed_inner, packed_outer),
    )
    sel_other = swapped(sel, "sub", 0)
    fwd_other = swapped(fwd_send, "sub", 0)
    near_rims, far_rims = call(edge_body, [shape((rank, half))] * 2, (sel, sel_other, panel))
    ring = list(range(1, chips, 2)) + list(range(chips - 2, -1, -2))
    route = [(2 * a + c, 2 * b + c) for a, b in zip(ring, ring[1:] + ring[:1]) for c in range(2)]
    far_rims = lax.ppermute(far_rims, "sub", route)
    fwd = call(
        node_body,
        shape((2 * rank, half)),
        (maps[0], fwd_mine, fwd_other, near_rims),
        specs="vvva",
    )
    adj = call(
        adjoint_body,
        shape((2 * rank, half)),
        (maps[0], sel, sel_other, panel, near_rims),
        specs="vvvva",
        flops=4 << 30,
    )
    adj = call(
        rim_body,
        shape((3 * rank, half)),
        (sel, sel_other, near_rims, far_rims, adj),
        flops=1000,
    )
    new, node = call(
        functools.partial(joined_body, 1),
        [shape((2 * rank, half)), shape((rank, half))],
        (maps[1], adj, swapped(adj, "sub", 1)),
    )
    chains = [[fwd], [node, new]]
    steps = [("sub", bit) for bit in range(1, sub_bits)]
    steps += [("grp", bit) for bit in range(levels - sub_bits)]
    for level, (axis, bit) in enumerate(steps[:-1], 1):
        for kind, chain in enumerate(chains):
            if len(chain) == level:
                chain.append(
                    call(
                        functools.partial(level_body, kind, axis, bit),
                        shape((2 * rank, half)),
                        (maps[level], chain[-1], swapped(chain[-1], axis, bit)),
                        flops=4 << 30 if (level, kind) == (1, 0) else 1000,
                    )
                )
    axis, bit = steps[-1]
    ends = [swapped(chain[-1], axis, bit) for chain in chains]
    x = call(
        functools.partial(last_body, axis, bit, levels),
        shape((levels, 2, rank, half)),
        (maps[-1], *chains[0], ends[0], *chains[1], ends[1]),
    )
    return call(
        functools.partial(output_body, vectors),
        shape((1, levels, 2, rank, samples)),
        (x, swapped(x, "sub", 0)),
    )


def solution(mesh):
    both = ("grp", "sub")
    return jax.shard_map(
        local,
        mesh=mesh,
        in_specs=(
            P(both, None),
            P("sub", "grp"),
            P(both, None, None, None),
            P(both, None),
            P(both, None, None),
            P(both, None, None, None),
            P(both, None, None, None),
            P(both, None, None, None, None),
        ),
        out_specs=P(both, None, None, None, None),
        check_vma=False,
    )
```

```python
import functools

import jax
import jax.numpy as jnp
from jax import lax
from jax.experimental import pallas as pl
from jax.experimental.pallas import tpu as pltpu
from jax.sharding import PartitionSpec as P

BF = jnp.bfloat16
F32 = jnp.float32
SPACES = {
    "h": pl.BlockSpec(memory_space=pltpu.HBM),
    "a": pl.BlockSpec(memory_space=pl.ANY),
    "s": pl.BlockSpec(memory_space=pltpu.SMEM),
    "v": pl.BlockSpec(memory_space=pltpu.VMEM),
}


def mm(a, b):
    return jnp.dot(a, b, preferred_element_type=F32)


def mm_t(a, b):
    return lax.dot_general(a, b, (((1,), (1,)), ((), ())), preferred_element_type=F32)


def eye(n):
    same = lax.broadcasted_iota(jnp.int32, (n, n), 0) == lax.broadcasted_iota(jnp.int32, (n, n), 1)
    return jnp.where(same, 1.0, 0.0).astype(BF)


def one_hot(order, n):
    hit = lax.broadcasted_iota(jnp.int32, (n, order.shape[1]), 0) == order
    return jnp.where(hit, 1.0, 0.0).astype(BF)


def call(body, out_shape, args, scratch=(), specs=None, out="v", limit=40 << 20, flops=1000):
    return pl.pallas_call(
        body,
        out_shape=out_shape,
        in_specs=[SPACES[c] for c in specs or "v" * len(args)],
        out_specs=jax.tree.map(lambda _: SPACES[out], out_shape),
        scratch_shapes=list(scratch),
        compiler_params=pltpu.CompilerParams(vmem_limit_bytes=limit),
        cost_estimate=pl.CostEstimate(flops=flops, bytes_accessed=1000, transcendentals=0),
    )(*args)


def shape(dims, dtype=BF):
    return jax.ShapeDtypeStruct(dims, dtype)


DIGIT = 32


def pack_body(
    width,
    tests_hbm,
    omega_hbm,
    perms_hbm,
    nodes_hbm,
    out_hbm,
    packed_hbm,
    tests_ref,
    omega_ref,
    perms_ref,
    nodes_ref,
    order_ref,
    sems,
):
    rows = omega_ref.shape[0]
    chips = out_hbm.shape[0]
    come = [pltpu.make_async_copy(omega_hbm, omega_ref, sems.at[0])]
    go = [pltpu.make_async_copy(omega_ref, packed_hbm.at[:rows], sems.at[1])]
    for chip in range(chips):
        part = slice(chip * width, (chip + 1) * width)
        come.append(
            pltpu.make_async_copy(tests_hbm.at[:, part], tests_ref.at[chip], sems.at[2 + 2 * chip])
        )
        go.append(pltpu.make_async_copy(tests_ref.at[chip], out_hbm.at[chip], sems.at[3 + 2 * chip]))
    small = [
        pltpu.make_async_copy(perms_hbm, perms_ref, sems.at[3 + 2 * chips]),
        pltpu.make_async_copy(nodes_hbm, nodes_ref, sems.at[4 + 2 * chips]),
    ]
    for copy in small + come:
        copy.start()
    for copy in small:
        copy.wait()
    kept = nodes_ref.shape[-1] // 2
    for order, at in ((perms_ref[0, 1:2, :kept], 0), (nodes_ref[0, 0, 1:2, :kept], 2)):
        row = lax.broadcasted_iota(jnp.int32, (order_ref.shape[0], kept), 0)
        digits = jnp.where(row == at, order // DIGIT, jnp.where(row == at + 1, order % DIGIT, 0))
        total = digits if at == 0 else total + digits
    order_ref[...] = jnp.zeros_like(order_ref)
    order_ref[:, :kept] = total.astype(F32).astype(BF)
    last = pltpu.make_async_copy(order_ref, packed_hbm.at[rows:], sems.at[2 + 2 * chips])
    last.start()
    for first, second in zip(come, go):
        first.wait()
        second.start()
    last.wait()
    for copy in go:
        copy.wait()


def dense_body(cols_ref, tiles_ref, perms_ref, interp_ref, after_ref, keep_ref, near_ref, tests_ref, dense_ref):
    del after_ref
    per_dev, slots, tile = tiles_ref.shape[:3]
    rows = per_dev * tile
    rank = interp_ref.shape[-2]
    core = lax.axis_index("sub") & 1
    first = (lax.axis_index("grp") * lax.axis_size("sub") + lax.axis_index("sub")) * per_dev
    dense_ref[...] = jnp.zeros_like(dense_ref)
    for q in range(per_dev):
        for t in range(slots):
            col = cols_ref[q, t] - first
            below, above = col < 0, col >= per_dev
            place = jnp.where(below, col + per_dev, jnp.where(above, col - per_dev, col))
            inner = jnp.where(core == 0, above, below)
            block = jnp.where(below | above, jnp.where(inner, 1, 2), 0)
            at = pl.multiple_of((block * per_dev + place) * tile, tile)
            dense_ref[q * tile : (q + 1) * tile, pl.ds(at, tile)] = tiles_ref[q, t]
    unit = eye(rank)
    keeps = []
    for i in range(2):
        keep = mm_t(unit, one_hot(perms_ref[0, i : i + 1, :rank], rows))
        rest = one_hot(perms_ref[0, i : i + 1, rank:], rows)
        every = (keep + mm_t(interp_ref[0, i], rest)).astype(BF)
        keeps.append(keep.astype(BF))
        if i == 0:
            keep_ref[rank:] = every
        else:
            tests_ref[...] = every
    keep_ref[:rank] = mm_t(keeps[1], dense_ref[:, :rows]).astype(BF)
    near_ref[...] = mm(keeps[0], dense_ref[...]).astype(BF)


def from_digits(digits, at):
    digits = digits.astype(F32)
    return (digits[at : at + 1] * DIGIT + digits[at + 1 : at + 2]).astype(jnp.int32)


def halo_body(
    keep_ref,
    dense_ref,
    near_ref,
    tests_ref,
    omega_ref,
    inner_ref,
    outer_ref,
    sel_ref,
    mine_ref,
):
    rows = dense_ref.shape[0]
    rank = near_ref.shape[0]
    half = omega_ref.shape[1] // 2
    core = lax.axis_index("sub") & 1
    unit = eye(rank)
    sel_ref[: 2 * rank] = keep_ref[...]
    for b, ref in enumerate((inner_ref, outer_ref), 1):
        keep = mm_t(unit, one_hot(from_digits(ref[rows:, :rank], 0), rows)).astype(BF)
        block = dense_ref[:, b * rows : (b + 1) * rows]
        sel_ref[(b + 1) * rank : (b + 2) * rank] = mm_t(keep, block).astype(BF)
    spare = sel_ref.shape[0] - 4 * rank
    sel_ref[4 * rank :] = jnp.zeros((spare, rows), BF)
    sel_ref[4 * rank : 4 * rank + 16, : outer_ref.shape[1]] = outer_ref[rows:]
    panels = []
    for place in (core, 1 - core):
        cols = pl.ds(pl.multiple_of(place * half, half), half)
        own = omega_ref[:, cols]
        fwd = (
            mm(near_ref[:, :rows], own)
            + mm(near_ref[:, rows : 2 * rows], inner_ref[:rows, cols])
            + mm(near_ref[:, 2 * rows :], outer_ref[:rows, cols])
        )
        panels.append(jnp.concatenate([fwd, mm(tests_ref[...], own)], axis=0).astype(BF))
    mine_ref[...] = panels[0]
    height = sel_ref.shape[0] - 4 * rank - 16
    for at in range(2 * rank // height):
        part = panels[1][at * height : (at + 1) * height]
        sel_ref[4 * rank + 16 :, at * half : (at + 1) * half] = part


def maps_body(maps_ref, perms_ref, order_ref, *out_refs):
    rank = maps_ref.shape[-1]
    unit = eye(rank)
    order_ref[...] = jnp.zeros_like(order_ref)
    for level, out_ref in enumerate(out_refs):
        row_interp, col_interp, low_high, high_low = (maps_ref[0, level, i] for i in range(4))
        row_hot = one_hot(perms_ref[0, level, 0:1, :], 2 * rank)
        col_hot = one_hot(perms_ref[0, level, 1:2, :], 2 * rank)
        row_all = mm(row_hot, jnp.concatenate([unit, row_interp], axis=0)).astype(BF)
        col_all = mm(col_hot, jnp.concatenate([unit, col_interp], axis=0)).astype(BF)
        for kind, (hot, every) in enumerate(((row_hot, col_all), (col_hot, row_all))):
            keep = [mm_t(unit, hot[side * rank : (side + 1) * rank, :rank]).astype(BF) for side in range(2)]
            if kind == 0:
                cross = [mm(keep[1], high_low), mm(keep[0], low_high)]
            else:
                cross = [mm_t(keep[1], low_high), mm_t(keep[0], high_low)]
            for side in range(2):
                out_ref[kind, side, :rank] = keep[side]
                out_ref[kind, side, rank : 2 * rank] = (-cross[side]).astype(BF)
                out_ref[kind, side, 2 * rank :] = mm_t(
                    unit, every[side * rank : (side + 1) * rank]
                ).astype(BF)


def near_rim():
    sub = lax.axis_index("sub")
    return (sub & 1) != ((sub >> 1) & 1)


def merged(maps_ref, kind, side, mine_first, mine_second, other_first, other_second, rank):
    wide = mm(maps_ref[kind, side, rank:], mine_second) + mm(maps_ref[kind, 1 - side, rank:], other_second)
    kept = mm(maps_ref[kind, side, :rank], mine_first) + mm(maps_ref[kind, 1 - side, :rank], other_first)
    return kept + wide[:rank], wide[rank:]


def node_body(maps_ref, mine_ref, sel_other, after_ref, out_ref):
    del after_ref
    rank = mine_ref.shape[0] // 2
    half = mine_ref.shape[1]
    core = lax.axis_index("sub") & 1
    height = sel_other.shape[0] - 4 * rank - 16
    parts = [
        sel_other[4 * rank + 16 :, at * half : (at + 1) * half] for at in range(2 * rank // height)
    ]
    other = jnp.concatenate(parts, axis=0)
    kept, tests = merged(
        maps_ref, 0, core, mine_ref[:rank], mine_ref[rank:], other[:rank], other[rank:], rank
    )
    out_ref[:rank] = kept.astype(BF)
    out_ref[rank:] = tests.astype(BF)


def halves(panel_ref):
    rows = panel_ref.shape[1] // 2
    core = lax.axis_index("sub") & 1
    return [panel_ref[:, pl.ds(pl.multiple_of(at * rows, 128), rows)] for at in (core, 1 - core)]


def edge_body(sel_ref, sel_other, panel_ref, near_out, far_out):
    rank = near_out.shape[0]
    panel, panel_other = halves(panel_ref)
    mine = mm_t(sel_ref[3 * rank : 4 * rank], panel)
    other = mm_t(sel_other[3 * rank : 4 * rank], panel_other)
    near = near_rim()
    near_out[...] = jnp.where(near, mine, other).astype(BF)
    far_out[...] = jnp.where(near, other, mine).astype(BF)


def adjoint_body(maps_ref, sel_ref, sel_other, panel_ref, after_ref, out_ref):
    del after_ref
    rank = out_ref.shape[0] // 2
    core = lax.axis_index("sub") & 1
    panel, panel_other = halves(panel_ref)
    mine = mm_t(sel_ref[: 3 * rank], panel)
    other = mm_t(sel_other[: 3 * rank], panel_other)
    kept, tests = merged(
        maps_ref,
        1,
        core,
        (mine[:rank] + other[2 * rank :]).astype(BF),
        mine[rank : 2 * rank].astype(BF),
        (other[:rank] + mine[2 * rank :]).astype(BF),
        other[rank : 2 * rank].astype(BF),
        rank,
    )
    out_ref[:rank] = kept.astype(BF)
    out_ref[rank:] = tests.astype(BF)


def rim_body(sel_ref, sel_other, near_ref, far_ref, adj_ref, out_ref):
    rank = near_ref.shape[0]
    chip = (lax.axis_index("sub") >> 1) & 1
    digits = [ref[4 * rank : 4 * rank + 16, :rank].astype(F32) for ref in (sel_ref, sel_other)]
    order = from_digits(jnp.where(near_rim(), *digits), 2)
    hot = one_hot(order, 2 * rank)
    keeps = [mm_t(eye(rank), hot[side * rank : (side + 1) * rank]) for side in range(2)]
    upper = chip == 1
    near_keep = jnp.where(upper, keeps[1], keeps[0]).astype(BF)
    far_keep = jnp.where(upper, keeps[0], keeps[1]).astype(BF)
    out_ref[: 2 * rank] = adj_ref[...]
    out_ref[2 * rank :] = (mm(near_keep, near_ref[...]) + mm(far_keep, far_ref[...])).astype(BF)


def joined_body(bit, maps_ref, mine_ref, other_ref, out_ref, node_ref):
    rank = node_ref.shape[0]
    side = (lax.axis_index("sub") >> bit) & 1
    a, p, r = (slice(i * rank, (i + 1) * rank) for i in range(3))
    mine = (mine_ref[a].astype(F32) + other_ref[r].astype(F32)).astype(BF)
    other = (other_ref[a].astype(F32) + mine_ref[r].astype(F32)).astype(BF)
    node_ref[...] = mine
    kept, tests = merged(maps_ref, 1, side, mine, mine_ref[p], other, other_ref[p], rank)
    out_ref[:rank] = kept.astype(BF)
    out_ref[rank:] = tests.astype(BF)


def level_body(kind, axis, bit, maps_ref, mine_ref, other_ref, out_ref):
    rank = mine_ref.shape[0] // 2
    side = (lax.axis_index(axis) >> bit) & 1
    kept, tests = merged(
        maps_ref, kind, side, mine_ref[:rank], mine_ref[rank:], other_ref[:rank], other_ref[rank:], rank
    )
    out_ref[:rank] = kept.astype(BF)
    out_ref[rank:] = tests.astype(BF)


def last_body(axis, bit, levels, maps_ref, *refs):
    out_ref = refs[-1]
    rank = out_ref.shape[2]
    side = (lax.axis_index(axis) >> bit) & 1
    for kind in range(2):
        nodes = refs[kind * levels : kind * levels + levels - 1]
        mine_ref, other_ref = nodes[-1], refs[kind * levels + levels - 1]
        for level, ref in enumerate(nodes):
            out_ref[level, kind] = ref[:rank]
        kept, _ = merged(
            maps_ref,
            kind,
            side,
            mine_ref[:rank],
            mine_ref[rank:],
            other_ref[:rank],
            other_ref[rank:],
            rank,
        )
        out_ref[levels - 1, kind] = kept.astype(BF)


def output_body(vectors, mine_ref, other_ref, out_hbm, out_ref, sems):
    half = mine_ref.shape[-1]
    core = lax.axis_index("sub") & 1
    k = lax.broadcasted_iota(jnp.int32, (half, 2 * half), 0)
    s = lax.broadcasted_iota(jnp.int32, (half, 2 * half), 1)
    base = k + k // vectors * vectors
    to_mine = jnp.where(s == base + core * vectors, 1.0, 0.0).astype(BF)
    to_other = jnp.where(s == base + (1 - core) * vectors, 1.0, 0.0).astype(BF)
    mine_cols = pl.ds(pl.multiple_of(core * half, half), half)
    other_cols = pl.ds(pl.multiple_of((1 - core) * half, half), half)
    copies = []
    for level in range(mine_ref.shape[0]):
        mine, other = mine_ref[level], other_ref[level]
        out_ref[level, 0, :, mine_cols] = mine[0]
        out_ref[level, 0, :, other_cols] = other[0]
        out_ref[level, 1] = (mm(mine[1], to_mine) + mm(other[1], to_other)).astype(BF)
        copies.append(pltpu.make_async_copy(out_ref.at[level], out_hbm.at[0, level], sems.at[level]))
        copies[-1].start()
    for copy in copies:
        copy.wait()


def swapped(x, axis, bit):
    return lax.ppermute(x, axis, [(i, i ^ (1 << bit)) for i in range(lax.axis_size(axis))])


def local(omega, adj_tests, near_tiles, tile_cols, leaf_perms, leaf_interp, node_perms, node_maps):
    rows, samples = omega.shape
    half = samples // 2
    vectors = adj_tests.shape[0]
    rank = leaf_interp.shape[-1]
    levels = node_maps.shape[1]
    count = lax.axis_size("sub")
    chips = count // 2
    sub_bits = count.bit_length() - 1
    outward = [(i, i + 1) for i in range(1, count - 1, 2)]
    outward += [(j, i) for i, j in outward] + [(0, 0), (count - 1, count - 1)]

    blocks, packed = call(
        functools.partial(pack_body, 2 * rows),
        [shape((chips, vectors, 2 * rows)), shape((rows + 16, samples))],
        (adj_tests, omega, leaf_perms, node_perms),
        scratch=[
            pltpu.VMEM((chips, vectors, 2 * rows), BF),
            pltpu.VMEM(omega.shape, BF),
            pltpu.VMEM(leaf_perms.shape, jnp.int32),
            pltpu.VMEM(node_perms.shape, jnp.int32),
            pltpu.VMEM((16, samples), BF),
            pltpu.SemaphoreType.DMA((2 * chips + 5,)),
        ],
        specs="hhhh",
        out="a",
        limit=56 << 20,
    )
    packed_outer = lax.ppermute(packed, "sub", outward)
    packed_inner = swapped(packed, "sub", 0)
    groups = [[2 * m + c for m in range(chips)] for c in range(2)]
    panel = lax.all_to_all(
        blocks, "sub", split_axis=0, concat_axis=0, tiled=True, axis_index_groups=groups
    ).reshape(half, 2 * rows)

    tables = shape((2, 2, 3 * rank, rank))
    order, *maps = call(
        maps_body,
        [shape((16, 128))] + [tables] * levels,
        (node_maps, node_perms),
        flops=1 << 30,
    )
    keep, near, tests, dense = call(
        dense_body,
        [
            shape((2 * rank, rows)),
            shape((rank, 3 * rows)),
            shape((rank, rows)),
            shape((rows, 3 * rows)),
        ],
        (tile_cols, near_tiles, leaf_perms, jnp.swapaxes(leaf_interp, 2, 3), order),
        specs="svvva",
        flops=1 << 30,
    )
    height = -(-2 * rank * half // rows // 16) * 16
    while 2 * rank % height:
        height += 16
    sel, fwd_mine = call(
        halo_body,
        [shape((4 * rank + 16 + height, rows)), shape((2 * rank, half))],
        (keep, dense, near, tests, omega, packed_inner, packed_outer),
    )
    sel_other = swapped(sel, "sub", 0)
    near_rims, far_rims = call(edge_body, [shape((rank, half))] * 2, (sel, sel_other, panel))
    ring = list(range(1, chips, 2)) + list(range(chips - 2, -1, -2))
    route = [(2 * a + c, 2 * b + c) for a, b in zip(ring, ring[1:] + ring[:1]) for c in range(2)]
    far_rims = lax.ppermute(far_rims, "sub", route)
    fwd = call(
        node_body,
        shape((2 * rank, half)),
        (maps[0], fwd_mine, sel_other, near_rims),
        specs="vvva",
    )
    adj = call(
        adjoint_body,
        shape((2 * rank, half)),
        (maps[0], sel, sel_other, panel, near_rims),
        specs="vvvva",
        flops=4 << 30,
    )
    adj = call(
        rim_body,
        shape((3 * rank, half)),
        (sel, sel_other, near_rims, far_rims, adj),
        flops=1000,
    )
    new, node = call(
        functools.partial(joined_body, 1),
        [shape((2 * rank, half)), shape((rank, half))],
        (maps[1], adj, swapped(adj, "sub", 1)),
    )
    chains = [[fwd], [node, new]]
    steps = [("sub", bit) for bit in range(1, sub_bits)]
    steps += [("grp", bit) for bit in range(levels - sub_bits)]
    for level, (axis, bit) in enumerate(steps[:-1], 1):
        for kind, chain in enumerate(chains):
            if len(chain) == level:
                chain.append(
                    call(
                        functools.partial(level_body, kind, axis, bit),
                        shape((2 * rank, half)),
                        (maps[level], chain[-1], swapped(chain[-1], axis, bit)),
                        flops=4 << 30 if (level, kind) == (1, 0) else 1000,
                    )
                )
    axis, bit = steps[-1]
    ends = [swapped(chain[-1], axis, bit) for chain in chains]
    x = call(
        functools.partial(last_body, axis, bit, levels),
        shape((levels, 2, rank, half)),
        (maps[-1], *chains[0], ends[0], *chains[1], ends[1]),
    )
    return call(
        functools.partial(output_body, vectors),
        shape((1, levels, 2, rank, samples)),
        (x, swapped(x, "sub", 0)),
        scratch=[pltpu.VMEM((levels, 2, rank, samples), BF), pltpu.SemaphoreType.DMA((levels,))],
        out="a",
    )


def solution(mesh):
    both = ("grp", "sub")
    return jax.shard_map(
        local,
        mesh=mesh,
        in_specs=(
            P(both, None),
            P("sub", "grp"),
            P(both, None, None, None),
            P(both, None),
            P(both, None, None),
            P(both, None, None, None),
            P(both, None, None, None),
            P(both, None, None, None, None),
        ),
        out_specs=P(both, None, None, None, None),
        check_vma=False,
    )
```

```python
import functools

import jax
import jax.numpy as jnp
from jax import lax
from jax.experimental import pallas as pl
from jax.experimental.pallas import tpu as pltpu
from jax.sharding import PartitionSpec as P

BF = jnp.bfloat16
F32 = jnp.float32
SPACES = {
    "h": pl.BlockSpec(memory_space=pltpu.HBM),
    "a": pl.BlockSpec(memory_space=pl.ANY),
    "s": pl.BlockSpec(memory_space=pltpu.SMEM),
    "v": pl.BlockSpec(memory_space=pltpu.VMEM),
}


def mm(a, b):
    return jnp.dot(a, b, preferred_element_type=F32)


def mm_t(a, b):
    return lax.dot_general(a, b, (((1,), (1,)), ((), ())), preferred_element_type=F32)


def eye(n):
    same = lax.broadcasted_iota(jnp.int32, (n, n), 0) == lax.broadcasted_iota(jnp.int32, (n, n), 1)
    return jnp.where(same, 1.0, 0.0).astype(BF)


def one_hot(order, n):
    hit = lax.broadcasted_iota(jnp.int32, (n, order.shape[1]), 0) == order
    return jnp.where(hit, 1.0, 0.0).astype(BF)


def call(body, out_shape, args, scratch=(), specs=None, out="v", limit=40 << 20, flops=1000):
    return pl.pallas_call(
        body,
        out_shape=out_shape,
        in_specs=[SPACES[c] for c in specs or "v" * len(args)],
        out_specs=jax.tree.map(lambda _: SPACES[out], out_shape),
        scratch_shapes=list(scratch),
        compiler_params=pltpu.CompilerParams(vmem_limit_bytes=limit),
        cost_estimate=pl.CostEstimate(flops=flops, bytes_accessed=1000, transcendentals=0),
    )(*args)


def shape(dims, dtype=BF):
    return jax.ShapeDtypeStruct(dims, dtype)


DIGIT = 32


def pack_body(
    width,
    tests_hbm,
    omega_hbm,
    perms_hbm,
    nodes_hbm,
    out_hbm,
    packed_hbm,
    tests_ref,
    omega_ref,
    perms_ref,
    nodes_ref,
    order_ref,
    sems,
):
    rows = omega_ref.shape[0]
    chips = out_hbm.shape[0]
    come = [pltpu.make_async_copy(omega_hbm, omega_ref, sems.at[0])]
    go = [pltpu.make_async_copy(omega_ref, packed_hbm.at[:rows], sems.at[1])]
    for chip in range(chips):
        part = slice(chip * width, (chip + 1) * width)
        come.append(
            pltpu.make_async_copy(tests_hbm.at[:, part], tests_ref.at[chip], sems.at[2 + 2 * chip])
        )
        go.append(pltpu.make_async_copy(tests_ref.at[chip], out_hbm.at[chip], sems.at[3 + 2 * chip]))
    small = [
        pltpu.make_async_copy(perms_hbm, perms_ref, sems.at[3 + 2 * chips]),
        pltpu.make_async_copy(nodes_hbm, nodes_ref, sems.at[4 + 2 * chips]),
    ]
    for copy in small + come:
        copy.start()
    for copy in small:
        copy.wait()
    kept = nodes_ref.shape[-1] // 2
    for order, at in ((perms_ref[0, 1:2, :kept], 0), (nodes_ref[0, 0, 1:2, :kept], 2)):
        row = lax.broadcasted_iota(jnp.int32, (order_ref.shape[0], kept), 0)
        digits = jnp.where(row == at, order // DIGIT, jnp.where(row == at + 1, order % DIGIT, 0))
        total = digits if at == 0 else total + digits
    order_ref[...] = jnp.zeros_like(order_ref)
    order_ref[:, :kept] = total.astype(F32).astype(BF)
    last = pltpu.make_async_copy(order_ref, packed_hbm.at[rows:], sems.at[2 + 2 * chips])
    last.start()
    for first, second in zip(come, go):
        first.wait()
        second.start()
    last.wait()
    for copy in go:
        copy.wait()


def dense_body(cols_ref, tiles_ref, perms_ref, interp_ref, after_ref, keep_ref, near_ref, tests_ref, dense_ref):
    del after_ref
    per_dev, slots, tile = tiles_ref.shape[:3]
    rows = per_dev * tile
    rank = interp_ref.shape[-2]
    core = lax.axis_index("sub") & 1
    first = (lax.axis_index("grp") * lax.axis_size("sub") + lax.axis_index("sub")) * per_dev
    dense_ref[...] = jnp.zeros_like(dense_ref)
    for q in range(per_dev):
        for t in range(slots):
            col = cols_ref[q, t] - first
            below, above = col < 0, col >= per_dev
            place = jnp.where(below, col + per_dev, jnp.where(above, col - per_dev, col))
            inner = jnp.where(core == 0, above, below)
            block = jnp.where(below | above, jnp.where(inner, 1, 2), 0)
            at = pl.multiple_of((block * per_dev + place) * tile, tile)
            dense_ref[q * tile : (q + 1) * tile, pl.ds(at, tile)] = tiles_ref[q, t]
    unit = eye(rank)
    keeps = []
    for i in range(2):
        keep = mm_t(unit, one_hot(perms_ref[0, i : i + 1, :rank], rows))
        rest = one_hot(perms_ref[0, i : i + 1, rank:], rows)
        every = (keep + mm_t(interp_ref[0, i], rest)).astype(BF)
        keeps.append(keep.astype(BF))
        if i == 0:
            keep_ref[rank:] = every
        else:
            tests_ref[...] = every
    keep_ref[:rank] = mm_t(keeps[1], dense_ref[:, :rows]).astype(BF)
    near_ref[...] = mm(keeps[0], dense_ref[...]).astype(BF)


def from_digits(digits, at):
    digits = digits.astype(F32)
    return (digits[at : at + 1] * DIGIT + digits[at + 1 : at + 2]).astype(jnp.int32)


def halo_body(
    keep_ref,
    dense_ref,
    near_ref,
    tests_ref,
    omega_ref,
    inner_ref,
    outer_ref,
    sel_ref,
    mine_ref,
):
    rows = dense_ref.shape[0]
    rank = near_ref.shape[0]
    half = omega_ref.shape[1] // 2
    core = lax.axis_index("sub") & 1
    unit = eye(rank)
    sel_ref[: 2 * rank] = keep_ref[...]
    for b, ref in enumerate((inner_ref, outer_ref), 1):
        keep = mm_t(unit, one_hot(from_digits(ref[rows:, :rank], 0), rows)).astype(BF)
        block = dense_ref[:, b * rows : (b + 1) * rows]
        sel_ref[(b + 1) * rank : (b + 2) * rank] = mm_t(keep, block).astype(BF)
    spare = sel_ref.shape[0] - 4 * rank
    sel_ref[4 * rank :] = jnp.zeros((spare, rows), BF)
    sel_ref[4 * rank : 4 * rank + 16, : outer_ref.shape[1]] = outer_ref[rows:]
    panels = []
    for place in (core, 1 - core):
        cols = pl.ds(pl.multiple_of(place * half, half), half)
        own = omega_ref[:, cols]
        fwd = (
            mm(near_ref[:, :rows], own)
            + mm(near_ref[:, rows : 2 * rows], inner_ref[:rows, cols])
            + mm(near_ref[:, 2 * rows :], outer_ref[:rows, cols])
        )
        panels.append(jnp.concatenate([fwd, mm(tests_ref[...], own)], axis=0).astype(BF))
    mine_ref[...] = panels[0]
    height = sel_ref.shape[0] - 4 * rank - 16
    for at in range(2 * rank // height):
        part = panels[1][at * height : (at + 1) * height]
        sel_ref[4 * rank + 16 :, at * half : (at + 1) * half] = part


def maps_body(first, maps_ref, perms_ref, after_ref, order_ref, *out_refs):
    rank = maps_ref.shape[-1]
    unit = eye(rank)
    del after_ref
    order_ref[...] = jnp.zeros_like(order_ref)
    for level, out_ref in enumerate(out_refs, first):
        row_interp, col_interp, low_high, high_low = (maps_ref[0, level, i] for i in range(4))
        row_hot = one_hot(perms_ref[0, level, 0:1, :], 2 * rank)
        col_hot = one_hot(perms_ref[0, level, 1:2, :], 2 * rank)
        row_all = mm(row_hot, jnp.concatenate([unit, row_interp], axis=0)).astype(BF)
        col_all = mm(col_hot, jnp.concatenate([unit, col_interp], axis=0)).astype(BF)
        for kind, (hot, every) in enumerate(((row_hot, col_all), (col_hot, row_all))):
            keep = [mm_t(unit, hot[side * rank : (side + 1) * rank, :rank]).astype(BF) for side in range(2)]
            if kind == 0:
                cross = [mm(keep[1], high_low), mm(keep[0], low_high)]
            else:
                cross = [mm_t(keep[1], low_high), mm_t(keep[0], high_low)]
            for side in range(2):
                out_ref[kind, side, :rank] = keep[side]
                out_ref[kind, side, rank : 2 * rank] = (-cross[side]).astype(BF)
                out_ref[kind, side, 2 * rank :] = mm_t(
                    unit, every[side * rank : (side + 1) * rank]
                ).astype(BF)


def near_rim():
    sub = lax.axis_index("sub")
    return (sub & 1) != ((sub >> 1) & 1)


def merged(maps_ref, kind, side, mine_first, mine_second, other_first, other_second, rank):
    wide = mm(maps_ref[kind, side, rank:], mine_second) + mm(maps_ref[kind, 1 - side, rank:], other_second)
    kept = mm(maps_ref[kind, side, :rank], mine_first) + mm(maps_ref[kind, 1 - side, :rank], other_first)
    return kept + wide[:rank], wide[rank:]


def node_body(maps_ref, mine_ref, sel_other, after_ref, out_ref):
    del after_ref
    rank = mine_ref.shape[0] // 2
    half = mine_ref.shape[1]
    core = lax.axis_index("sub") & 1
    height = sel_other.shape[0] - 4 * rank - 16
    parts = [
        sel_other[4 * rank + 16 :, at * half : (at + 1) * half] for at in range(2 * rank // height)
    ]
    other = jnp.concatenate(parts, axis=0)
    kept, tests = merged(
        maps_ref, 0, core, mine_ref[:rank], mine_ref[rank:], other[:rank], other[rank:], rank
    )
    out_ref[:rank] = kept.astype(BF)
    out_ref[rank:] = tests.astype(BF)


def halves(panel_ref):
    rows = panel_ref.shape[1] // 2
    core = lax.axis_index("sub") & 1
    return [panel_ref[:, pl.ds(pl.multiple_of(at * rows, 128), rows)] for at in (core, 1 - core)]


def edge_body(sel_ref, sel_other, panel_ref, after_ref, near_out, far_out):
    del after_ref
    rank = near_out.shape[0]
    panel, panel_other = halves(panel_ref)
    mine = mm_t(sel_ref[3 * rank : 4 * rank], panel)
    other = mm_t(sel_other[3 * rank : 4 * rank], panel_other)
    near = near_rim()
    near_out[...] = jnp.where(near, mine, other).astype(BF)
    far_out[...] = jnp.where(near, other, mine).astype(BF)


def adjoint_body(maps_ref, sel_ref, sel_other, panel_ref, after_ref, out_ref):
    del after_ref
    rank = out_ref.shape[0] // 2
    core = lax.axis_index("sub") & 1
    panel, panel_other = halves(panel_ref)
    mine = mm_t(sel_ref[: 3 * rank], panel)
    other = mm_t(sel_other[: 3 * rank], panel_other)
    kept, tests = merged(
        maps_ref,
        1,
        core,
        (mine[:rank] + other[2 * rank :]).astype(BF),
        mine[rank : 2 * rank].astype(BF),
        (other[:rank] + mine[2 * rank :]).astype(BF),
        other[rank : 2 * rank].astype(BF),
        rank,
    )
    out_ref[:rank] = kept.astype(BF)
    out_ref[rank:] = tests.astype(BF)


def rim_body(sel_ref, sel_other, near_ref, far_ref, adj_ref, out_ref):
    rank = near_ref.shape[0]
    chip = (lax.axis_index("sub") >> 1) & 1
    digits = [ref[4 * rank : 4 * rank + 16, :rank].astype(F32) for ref in (sel_ref, sel_other)]
    order = from_digits(jnp.where(near_rim(), *digits), 2)
    hot = one_hot(order, 2 * rank)
    keeps = [mm_t(eye(rank), hot[side * rank : (side + 1) * rank]) for side in range(2)]
    upper = chip == 1
    near_keep = jnp.where(upper, keeps[1], keeps[0]).astype(BF)
    far_keep = jnp.where(upper, keeps[0], keeps[1]).astype(BF)
    out_ref[: 2 * rank] = adj_ref[...]
    out_ref[2 * rank :] = (mm(near_keep, near_ref[...]) + mm(far_keep, far_ref[...])).astype(BF)


def joined_body(bit, maps_ref, mine_ref, other_ref, out_ref, node_ref):
    rank = node_ref.shape[0]
    side = (lax.axis_index("sub") >> bit) & 1
    a, p, r = (slice(i * rank, (i + 1) * rank) for i in range(3))
    mine = (mine_ref[a].astype(F32) + other_ref[r].astype(F32)).astype(BF)
    other = (other_ref[a].astype(F32) + mine_ref[r].astype(F32)).astype(BF)
    node_ref[...] = mine
    kept, tests = merged(maps_ref, 1, side, mine, mine_ref[p], other, other_ref[p], rank)
    out_ref[:rank] = kept.astype(BF)
    out_ref[rank:] = tests.astype(BF)


def level_body(kind, axis, bit, maps_ref, mine_ref, other_ref, out_ref):
    rank = mine_ref.shape[0] // 2
    side = (lax.axis_index(axis) >> bit) & 1
    kept, tests = merged(
        maps_ref, kind, side, mine_ref[:rank], mine_ref[rank:], other_ref[:rank], other_ref[rank:], rank
    )
    out_ref[:rank] = kept.astype(BF)
    out_ref[rank:] = tests.astype(BF)


def last_body(axis, bit, levels, maps_ref, *refs):
    out_ref = refs[-1]
    rank = out_ref.shape[2]
    side = (lax.axis_index(axis) >> bit) & 1
    for kind in range(2):
        nodes = refs[kind * levels : kind * levels + levels - 1]
        mine_ref, other_ref = nodes[-1], refs[kind * levels + levels - 1]
        for level, ref in enumerate(nodes):
            out_ref[level, kind] = ref[:rank]
        kept, _ = merged(
            maps_ref,
            kind,
            side,
            mine_ref[:rank],
            mine_ref[rank:],
            other_ref[:rank],
            other_ref[rank:],
            rank,
        )
        out_ref[levels - 1, kind] = kept.astype(BF)


def output_body(vectors, mine_ref, other_ref, out_hbm, out_ref, sems):
    half = mine_ref.shape[-1]
    core = lax.axis_index("sub") & 1
    k = lax.broadcasted_iota(jnp.int32, (half, 2 * half), 0)
    s = lax.broadcasted_iota(jnp.int32, (half, 2 * half), 1)
    base = k + k // vectors * vectors
    to_mine = jnp.where(s == base + core * vectors, 1.0, 0.0).astype(BF)
    to_other = jnp.where(s == base + (1 - core) * vectors, 1.0, 0.0).astype(BF)
    mine_cols = pl.ds(pl.multiple_of(core * half, half), half)
    other_cols = pl.ds(pl.multiple_of((1 - core) * half, half), half)
    copies = []
    for level in range(mine_ref.shape[0]):
        mine, other = mine_ref[level], other_ref[level]
        out_ref[level, 0, :, mine_cols] = mine[0]
        out_ref[level, 0, :, other_cols] = other[0]
        out_ref[level, 1] = (mm(mine[1], to_mine) + mm(other[1], to_other)).astype(BF)
        copies.append(pltpu.make_async_copy(out_ref.at[level], out_hbm.at[0, level], sems.at[level]))
        copies[-1].start()
    for copy in copies:
        copy.wait()


def swapped(x, axis, bit):
    return lax.ppermute(x, axis, [(i, i ^ (1 << bit)) for i in range(lax.axis_size(axis))])


def local(omega, adj_tests, near_tiles, tile_cols, leaf_perms, leaf_interp, node_perms, node_maps):
    rows, samples = omega.shape
    half = samples // 2
    vectors = adj_tests.shape[0]
    rank = leaf_interp.shape[-1]
    levels = node_maps.shape[1]
    count = lax.axis_size("sub")
    chips = count // 2
    sub_bits = count.bit_length() - 1
    outward = [(i, i + 1) for i in range(1, count - 1, 2)]
    outward += [(j, i) for i, j in outward] + [(0, 0), (count - 1, count - 1)]

    blocks, packed = call(
        functools.partial(pack_body, 2 * rows),
        [shape((chips, vectors, 2 * rows)), shape((rows + 16, samples))],
        (adj_tests, omega, leaf_perms, node_perms),
        scratch=[
            pltpu.VMEM((chips, vectors, 2 * rows), BF),
            pltpu.VMEM(omega.shape, BF),
            pltpu.VMEM(leaf_perms.shape, jnp.int32),
            pltpu.VMEM(node_perms.shape, jnp.int32),
            pltpu.VMEM((16, samples), BF),
            pltpu.SemaphoreType.DMA((2 * chips + 5,)),
        ],
        specs="hhhh",
        out="a",
        limit=56 << 20,
    )
    packed_outer = lax.ppermute(packed, "sub", outward)
    packed_inner = swapped(packed, "sub", 0)
    groups = [[2 * m + c for m in range(chips)] for c in range(2)]
    panel = lax.all_to_all(
        blocks, "sub", split_axis=0, concat_axis=0, tiled=True, axis_index_groups=groups
    ).reshape(half, 2 * rows)

    tables = shape((2, 2, 3 * rank, rank))
    order, *maps = call(
        functools.partial(maps_body, 1),
        [shape((16, 128))] + [tables] * (levels - 1),
        (node_maps, node_perms, node_perms),
        specs="vva",
        flops=1 << 30,
    )
    keep, near, tests, dense = call(
        dense_body,
        [
            shape((2 * rank, rows)),
            shape((rank, 3 * rows)),
            shape((rank, rows)),
            shape((rows, 3 * rows)),
        ],
        (tile_cols, near_tiles, leaf_perms, jnp.swapaxes(leaf_interp, 2, 3), order),
        specs="svvva",
        flops=1 << 30,
    )
    height = -(-2 * rank * half // rows // 16) * 16
    while 2 * rank % height:
        height += 16
    sel, fwd_mine = call(
        halo_body,
        [shape((4 * rank + 16 + height, rows)), shape((2 * rank, half))],
        (keep, dense, near, tests, omega, packed_inner, packed_outer),
    )
    sel_other = swapped(sel, "sub", 0)
    order, first_maps = call(
        functools.partial(maps_body, 0),
        [shape((16, 128)), tables],
        (node_maps, node_perms, fwd_mine),
        specs="vva",
    )
    maps = [first_maps, *maps]
    near_rims, far_rims = call(
        edge_body, [shape((rank, half))] * 2, (sel, sel_other, panel, order), specs="vvva"
    )
    ring = list(range(1, chips, 2)) + list(range(chips - 2, -1, -2))
    route = [(2 * a + c, 2 * b + c) for a, b in zip(ring, ring[1:] + ring[:1]) for c in range(2)]
    far_rims = lax.ppermute(far_rims, "sub", route)
    fwd = call(
        node_body,
        shape((2 * rank, half)),
        (maps[0], fwd_mine, sel_other, near_rims),
        specs="vvva",
    )
    adj = call(
        adjoint_body,
        shape((2 * rank, half)),
        (maps[0], sel, sel_other, panel, near_rims),
        specs="vvvva",
        flops=4 << 30,
    )
    adj = call(
        rim_body,
        shape((3 * rank, half)),
        (sel, sel_other, near_rims, far_rims, adj),
        flops=1000,
    )
    new, node = call(
        functools.partial(joined_body, 1),
        [shape((2 * rank, half)), shape((rank, half))],
        (maps[1], adj, swapped(adj, "sub", 1)),
    )
    chains = [[fwd], [node, new]]
    steps = [("sub", bit) for bit in range(1, sub_bits)]
    steps += [("grp", bit) for bit in range(levels - sub_bits)]
    for level, (axis, bit) in enumerate(steps[:-1], 1):
        for kind, chain in enumerate(chains):
            if len(chain) == level:
                chain.append(
                    call(
                        functools.partial(level_body, kind, axis, bit),
                        shape((2 * rank, half)),
                        (maps[level], chain[-1], swapped(chain[-1], axis, bit)),
                        flops=4 << 30 if (level, kind) == (1, 0) else 1000,
                    )
                )
    axis, bit = steps[-1]
    ends = [swapped(chain[-1], axis, bit) for chain in chains]
    x = call(
        functools.partial(last_body, axis, bit, levels),
        shape((levels, 2, rank, half)),
        (maps[-1], *chains[0], ends[0], *chains[1], ends[1]),
    )
    return call(
        functools.partial(output_body, vectors),
        shape((1, levels, 2, rank, samples)),
        (x, swapped(x, "sub", 0)),
        scratch=[pltpu.VMEM((levels, 2, rank, samples), BF), pltpu.SemaphoreType.DMA((levels,))],
        out="a",
    )


def solution(mesh):
    both = ("grp", "sub")
    return jax.shard_map(
        local,
        mesh=mesh,
        in_specs=(
            P(both, None),
            P("sub", "grp"),
            P(both, None, None, None),
            P(both, None),
            P(both, None, None),
            P(both, None, None, None),
            P(both, None, None, None),
            P(both, None, None, None, None),
        ),
        out_specs=P(both, None, None, None, None),
        check_vma=False,
    )
```

```python
import functools

import jax
import jax.numpy as jnp
from jax import lax
from jax.experimental import pallas as pl
from jax.experimental.pallas import tpu as pltpu
from jax.sharding import PartitionSpec as P

BF = jnp.bfloat16
F32 = jnp.float32
SPACES = {
    "h": pl.BlockSpec(memory_space=pltpu.HBM),
    "a": pl.BlockSpec(memory_space=pl.ANY),
    "s": pl.BlockSpec(memory_space=pltpu.SMEM),
    "v": pl.BlockSpec(memory_space=pltpu.VMEM),
}


def mm(a, b):
    return jnp.dot(a, b, preferred_element_type=F32)


def mm_t(a, b):
    return lax.dot_general(a, b, (((1,), (1,)), ((), ())), preferred_element_type=F32)


def eye(n):
    same = lax.broadcasted_iota(jnp.int32, (n, n), 0) == lax.broadcasted_iota(jnp.int32, (n, n), 1)
    return jnp.where(same, 1.0, 0.0).astype(BF)


def one_hot(order, n):
    hit = lax.broadcasted_iota(jnp.int32, (n, order.shape[1]), 0) == order
    return jnp.where(hit, 1.0, 0.0).astype(BF)


def call(body, out_shape, args, scratch=(), specs=None, out="v", limit=40 << 20, flops=1000):
    return pl.pallas_call(
        body,
        out_shape=out_shape,
        in_specs=[SPACES[c] for c in specs or "v" * len(args)],
        out_specs=jax.tree.map(lambda _: SPACES[out], out_shape),
        scratch_shapes=list(scratch),
        compiler_params=pltpu.CompilerParams(vmem_limit_bytes=limit),
        cost_estimate=pl.CostEstimate(flops=flops, bytes_accessed=1000, transcendentals=0),
    )(*args)


def shape(dims, dtype=BF):
    return jax.ShapeDtypeStruct(dims, dtype)


DIGIT = 32


def pack_body(
    width,
    tests_hbm,
    omega_hbm,
    perms_hbm,
    nodes_hbm,
    out_hbm,
    packed_hbm,
    tests_ref,
    omega_ref,
    perms_ref,
    nodes_ref,
    order_ref,
    sems,
):
    rows = omega_ref.shape[0]
    chips = out_hbm.shape[0]
    come = [pltpu.make_async_copy(omega_hbm, omega_ref, sems.at[0])]
    go = [pltpu.make_async_copy(omega_ref, packed_hbm.at[:rows], sems.at[1])]
    for chip in range(chips):
        part = slice(chip * width, (chip + 1) * width)
        come.append(
            pltpu.make_async_copy(tests_hbm.at[:, part], tests_ref.at[chip], sems.at[2 + 2 * chip])
        )
        go.append(pltpu.make_async_copy(tests_ref.at[chip], out_hbm.at[chip], sems.at[3 + 2 * chip]))
    small = [
        pltpu.make_async_copy(perms_hbm, perms_ref, sems.at[3 + 2 * chips]),
        pltpu.make_async_copy(nodes_hbm, nodes_ref, sems.at[4 + 2 * chips]),
    ]
    for copy in small + come:
        copy.start()
    for copy in small:
        copy.wait()
    kept = nodes_ref.shape[-1] // 2
    for order, at in ((perms_ref[0, 1:2, :kept], 0), (nodes_ref[0, 0, 1:2, :kept], 2)):
        row = lax.broadcasted_iota(jnp.int32, (order_ref.shape[0], kept), 0)
        digits = jnp.where(row == at, order // DIGIT, jnp.where(row == at + 1, order % DIGIT, 0))
        total = digits if at == 0 else total + digits
    order_ref[...] = jnp.zeros_like(order_ref)
    order_ref[:, :kept] = total.astype(F32).astype(BF)
    last = pltpu.make_async_copy(order_ref, packed_hbm.at[rows:], sems.at[2 + 2 * chips])
    last.start()
    for first, second in zip(come, go):
        first.wait()
        second.start()
    last.wait()
    for copy in go:
        copy.wait()


def dense_body(cols_ref, tiles_ref, perms_ref, interp_ref, after_ref, keep_ref, near_ref, tests_ref, dense_ref):
    del after_ref
    per_dev, slots, tile = tiles_ref.shape[:3]
    rows = per_dev * tile
    rank = interp_ref.shape[-2]
    core = lax.axis_index("sub") & 1
    first = (lax.axis_index("grp") * lax.axis_size("sub") + lax.axis_index("sub")) * per_dev
    dense_ref[...] = jnp.zeros_like(dense_ref)
    for q in range(per_dev):
        for t in range(slots):
            col = cols_ref[q, t] - first
            below, above = col < 0, col >= per_dev
            place = jnp.where(below, col + per_dev, jnp.where(above, col - per_dev, col))
            inner = jnp.where(core == 0, above, below)
            block = jnp.where(below | above, jnp.where(inner, 1, 2), 0)
            at = pl.multiple_of((block * per_dev + place) * tile, tile)
            dense_ref[q * tile : (q + 1) * tile, pl.ds(at, tile)] = tiles_ref[q, t]
    unit = eye(rank)
    keeps = []
    for i in range(2):
        keep = mm_t(unit, one_hot(perms_ref[0, i : i + 1, :rank], rows))
        rest = one_hot(perms_ref[0, i : i + 1, rank:], rows)
        every = (keep + mm_t(interp_ref[0, i], rest)).astype(BF)
        keeps.append(keep.astype(BF))
        if i == 0:
            keep_ref[rank:] = every
        else:
            tests_ref[...] = every
    keep_ref[:rank] = mm_t(keeps[1], dense_ref[:, :rows]).astype(BF)
    near_ref[...] = mm(keeps[0], dense_ref[...]).astype(BF)


def from_digits(digits, at):
    digits = digits.astype(F32)
    return (digits[at : at + 1] * DIGIT + digits[at + 1 : at + 2]).astype(jnp.int32)


def halo_body(
    keep_ref,
    dense_ref,
    near_ref,
    tests_ref,
    omega_ref,
    inner_ref,
    outer_ref,
    sel_ref,
    mine_ref,
):
    rows = dense_ref.shape[0]
    rank = near_ref.shape[0]
    half = omega_ref.shape[1] // 2
    core = lax.axis_index("sub") & 1
    unit = eye(rank)
    sel_ref[: 2 * rank] = keep_ref[...]
    for b, ref in enumerate((inner_ref, outer_ref), 1):
        keep = mm_t(unit, one_hot(from_digits(ref[rows:, :rank], 0), rows)).astype(BF)
        block = dense_ref[:, b * rows : (b + 1) * rows]
        sel_ref[(b + 1) * rank : (b + 2) * rank] = mm_t(keep, block).astype(BF)
    spare = sel_ref.shape[0] - 4 * rank
    sel_ref[4 * rank :] = jnp.zeros((spare, rows), BF)
    sel_ref[4 * rank : 4 * rank + 16, : outer_ref.shape[1]] = outer_ref[rows:]
    panels = []
    for place in (core, 1 - core):
        cols = pl.ds(pl.multiple_of(place * half, half), half)
        own = omega_ref[:, cols]
        fwd = (
            mm(near_ref[:, :rows], own)
            + mm(near_ref[:, rows : 2 * rows], inner_ref[:rows, cols])
            + mm(near_ref[:, 2 * rows :], outer_ref[:rows, cols])
        )
        panels.append(jnp.concatenate([fwd, mm(tests_ref[...], own)], axis=0).astype(BF))
    mine_ref[...] = panels[0]
    height = sel_ref.shape[0] - 4 * rank - 16
    for at in range(2 * rank // height):
        part = panels[1][at * height : (at + 1) * height]
        sel_ref[4 * rank + 16 :, at * half : (at + 1) * half] = part


def maps_body(first, maps_ref, perms_ref, after_ref, order_ref, *out_refs):
    rank = maps_ref.shape[-1]
    unit = eye(rank)
    del after_ref
    order_ref[...] = jnp.zeros_like(order_ref)
    for level, out_ref in enumerate(out_refs, first):
        row_interp, col_interp, low_high, high_low = (maps_ref[0, level, i] for i in range(4))
        row_hot = one_hot(perms_ref[0, level, 0:1, :], 2 * rank)
        col_hot = one_hot(perms_ref[0, level, 1:2, :], 2 * rank)
        row_all = mm(row_hot, jnp.concatenate([unit, row_interp], axis=0)).astype(BF)
        col_all = mm(col_hot, jnp.concatenate([unit, col_interp], axis=0)).astype(BF)
        for kind, (hot, every) in enumerate(((row_hot, col_all), (col_hot, row_all))):
            keep = [mm_t(unit, hot[side * rank : (side + 1) * rank, :rank]).astype(BF) for side in range(2)]
            if kind == 0:
                cross = [mm(keep[1], high_low), mm(keep[0], low_high)]
            else:
                cross = [mm_t(keep[1], low_high), mm_t(keep[0], high_low)]
            for side in range(2):
                out_ref[kind, side, :rank] = keep[side]
                out_ref[kind, side, rank : 2 * rank] = (-cross[side]).astype(BF)
                out_ref[kind, side, 2 * rank :] = mm_t(
                    unit, every[side * rank : (side + 1) * rank]
                ).astype(BF)


def near_rim():
    sub = lax.axis_index("sub")
    return (sub & 1) != ((sub >> 1) & 1)


def merged(maps_ref, kind, side, mine_first, mine_second, other_first, other_second, rank):
    wide = mm(maps_ref[kind, side, rank:], mine_second) + mm(maps_ref[kind, 1 - side, rank:], other_second)
    kept = mm(maps_ref[kind, side, :rank], mine_first) + mm(maps_ref[kind, 1 - side, :rank], other_first)
    return kept + wide[:rank], wide[rank:]


def node_body(maps_ref, mine_ref, sel_other, after_ref, out_ref):
    del after_ref
    rank = mine_ref.shape[0] // 2
    half = mine_ref.shape[1]
    core = lax.axis_index("sub") & 1
    height = sel_other.shape[0] - 4 * rank - 16
    parts = [
        sel_other[4 * rank + 16 :, at * half : (at + 1) * half] for at in range(2 * rank // height)
    ]
    other = jnp.concatenate(parts, axis=0)
    kept, tests = merged(
        maps_ref, 0, core, mine_ref[:rank], mine_ref[rank:], other[:rank], other[rank:], rank
    )
    out_ref[:rank] = kept.astype(BF)
    out_ref[rank:] = tests.astype(BF)


def halves(panel_ref):
    rows = panel_ref.shape[1] // 2
    core = lax.axis_index("sub") & 1
    return [panel_ref[:, pl.ds(pl.multiple_of(at * rows, 128), rows)] for at in (core, 1 - core)]


def edge_body(sel_ref, sel_other, panel_ref, after_ref, near_out, far_out):
    del after_ref
    rank = near_out.shape[0]
    panel, panel_other = halves(panel_ref)
    mine = mm_t(sel_ref[3 * rank : 4 * rank], panel)
    other = mm_t(sel_other[3 * rank : 4 * rank], panel_other)
    near = near_rim()
    near_out[...] = jnp.where(near, mine, other).astype(BF)
    far_out[...] = jnp.where(near, other, mine).astype(BF)


def adjoint_body(maps_ref, sel_ref, sel_other, panel_ref, after_ref, out_ref):
    del after_ref
    rank = out_ref.shape[0] // 2
    core = lax.axis_index("sub") & 1
    panel, panel_other = halves(panel_ref)
    mine = mm_t(sel_ref[: 3 * rank], panel)
    other = mm_t(sel_other[: 3 * rank], panel_other)
    kept, tests = merged(
        maps_ref,
        1,
        core,
        (mine[:rank] + other[2 * rank :]).astype(BF),
        mine[rank : 2 * rank].astype(BF),
        (other[:rank] + mine[2 * rank :]).astype(BF),
        other[rank : 2 * rank].astype(BF),
        rank,
    )
    out_ref[:rank] = kept.astype(BF)
    out_ref[rank:] = tests.astype(BF)


def rim_body(sel_ref, sel_other, near_ref, far_ref, adj_ref, out_ref):
    rank = near_ref.shape[0]
    chip = (lax.axis_index("sub") >> 1) & 1
    digits = [ref[4 * rank : 4 * rank + 16, :rank].astype(F32) for ref in (sel_ref, sel_other)]
    order = from_digits(jnp.where(near_rim(), *digits), 2)
    hot = one_hot(order, 2 * rank)
    keeps = [mm_t(eye(rank), hot[side * rank : (side + 1) * rank]) for side in range(2)]
    upper = chip == 1
    near_keep = jnp.where(upper, keeps[1], keeps[0]).astype(BF)
    far_keep = jnp.where(upper, keeps[0], keeps[1]).astype(BF)
    out_ref[: 2 * rank] = adj_ref[...]
    out_ref[2 * rank :] = (mm(near_keep, near_ref[...]) + mm(far_keep, far_ref[...])).astype(BF)


def joined_body(bit, maps_ref, mine_ref, other_ref, out_ref, node_ref):
    rank = node_ref.shape[0]
    side = (lax.axis_index("sub") >> bit) & 1
    a, p, r = (slice(i * rank, (i + 1) * rank) for i in range(3))
    mine = (mine_ref[a].astype(F32) + other_ref[r].astype(F32)).astype(BF)
    other = (other_ref[a].astype(F32) + mine_ref[r].astype(F32)).astype(BF)
    node_ref[...] = mine
    kept, tests = merged(maps_ref, 1, side, mine, mine_ref[p], other, other_ref[p], rank)
    out_ref[:rank] = kept.astype(BF)
    out_ref[rank:] = tests.astype(BF)


def level_body(kind, axis, bit, maps_ref, mine_ref, other_ref, out_ref):
    rank = mine_ref.shape[0] // 2
    side = (lax.axis_index(axis) >> bit) & 1
    kept, tests = merged(
        maps_ref, kind, side, mine_ref[:rank], mine_ref[rank:], other_ref[:rank], other_ref[rank:], rank
    )
    out_ref[:rank] = kept.astype(BF)
    out_ref[rank:] = tests.astype(BF)


def collect_body(*refs):
    out_ref = refs[-1]
    levels, _, rank, _ = out_ref.shape
    for i, ref in enumerate(refs[:-2]):
        out_ref[i % levels, i // levels] = ref[:rank]


def last_body(axis, bit, maps_ref, *refs):
    out_ref = refs[-1]
    rank = out_ref.shape[1]
    side = (lax.axis_index(axis) >> bit) & 1
    for kind in range(2):
        mine_ref, other_ref = refs[2 * kind : 2 * kind + 2]
        kept, _ = merged(
            maps_ref,
            kind,
            side,
            mine_ref[:rank],
            mine_ref[rank:],
            other_ref[:rank],
            other_ref[rank:],
            rank,
        )
        out_ref[kind] = kept.astype(BF)


def output_body(vectors, early_ref, early_other, mine_ref, other_ref, out_hbm, out_ref, sems):
    half = mine_ref.shape[-1]
    early = early_ref.shape[0]
    core = lax.axis_index("sub") & 1
    k = lax.broadcasted_iota(jnp.int32, (half, 2 * half), 0)
    s = lax.broadcasted_iota(jnp.int32, (half, 2 * half), 1)
    base = k + k // vectors * vectors
    to_mine = jnp.where(s == base + core * vectors, 1.0, 0.0).astype(BF)
    to_other = jnp.where(s == base + (1 - core) * vectors, 1.0, 0.0).astype(BF)
    mine_cols = pl.ds(pl.multiple_of(core * half, half), half)
    other_cols = pl.ds(pl.multiple_of((1 - core) * half, half), half)
    copies = []
    for level in range(early + 1):
        mine = early_ref[level] if level < early else mine_ref[...]
        other = early_other[level] if level < early else other_ref[...]
        out_ref[level, 0, :, mine_cols] = mine[0]
        out_ref[level, 0, :, other_cols] = other[0]
        out_ref[level, 1] = (mm(mine[1], to_mine) + mm(other[1], to_other)).astype(BF)
        copies.append(pltpu.make_async_copy(out_ref.at[level], out_hbm.at[0, level], sems.at[level]))
        copies[-1].start()
    for copy in copies:
        copy.wait()


def swapped(x, axis, bit):
    return lax.ppermute(x, axis, [(i, i ^ (1 << bit)) for i in range(lax.axis_size(axis))])


def local(omega, adj_tests, near_tiles, tile_cols, leaf_perms, leaf_interp, node_perms, node_maps):
    rows, samples = omega.shape
    half = samples // 2
    vectors = adj_tests.shape[0]
    rank = leaf_interp.shape[-1]
    levels = node_maps.shape[1]
    count = lax.axis_size("sub")
    chips = count // 2
    sub_bits = count.bit_length() - 1
    outward = [(i, i + 1) for i in range(1, count - 1, 2)]
    outward += [(j, i) for i, j in outward] + [(0, 0), (count - 1, count - 1)]

    blocks, packed = call(
        functools.partial(pack_body, 2 * rows),
        [shape((chips, vectors, 2 * rows)), shape((rows + 16, samples))],
        (adj_tests, omega, leaf_perms, node_perms),
        scratch=[
            pltpu.VMEM((chips, vectors, 2 * rows), BF),
            pltpu.VMEM(omega.shape, BF),
            pltpu.VMEM(leaf_perms.shape, jnp.int32),
            pltpu.VMEM(node_perms.shape, jnp.int32),
            pltpu.VMEM((16, samples), BF),
            pltpu.SemaphoreType.DMA((2 * chips + 5,)),
        ],
        specs="hhhh",
        out="a",
        limit=56 << 20,
    )
    packed_outer = lax.ppermute(packed, "sub", outward)
    packed_inner = swapped(packed, "sub", 0)
    groups = [[2 * m + c for m in range(chips)] for c in range(2)]
    panel = lax.all_to_all(
        blocks, "sub", split_axis=0, concat_axis=0, tiled=True, axis_index_groups=groups
    ).reshape(half, 2 * rows)

    tables = shape((2, 2, 3 * rank, rank))
    order, *maps = call(
        functools.partial(maps_body, 1),
        [shape((16, 128))] + [tables] * (levels - 1),
        (node_maps, node_perms, node_perms),
        specs="vva",
        flops=1 << 30,
    )
    keep, near, tests, dense = call(
        dense_body,
        [
            shape((2 * rank, rows)),
            shape((rank, 3 * rows)),
            shape((rank, rows)),
            shape((rows, 3 * rows)),
        ],
        (tile_cols, near_tiles, leaf_perms, jnp.swapaxes(leaf_interp, 2, 3), order),
        specs="svvva",
        flops=1 << 30,
    )
    height = -(-2 * rank * half // rows // 16) * 16
    while 2 * rank % height:
        height += 16
    sel, fwd_mine = call(
        halo_body,
        [shape((4 * rank + 16 + height, rows)), shape((2 * rank, half))],
        (keep, dense, near, tests, omega, packed_inner, packed_outer),
    )
    sel_other = swapped(sel, "sub", 0)
    order, first_maps = call(
        functools.partial(maps_body, 0),
        [shape((16, 128)), tables],
        (node_maps, node_perms, fwd_mine),
        specs="vva",
    )
    maps = [first_maps, *maps]
    near_rims, far_rims = call(
        edge_body, [shape((rank, half))] * 2, (sel, sel_other, panel, order), specs="vvva"
    )
    ring = list(range(1, chips, 2)) + list(range(chips - 2, -1, -2))
    route = [(2 * a + c, 2 * b + c) for a, b in zip(ring, ring[1:] + ring[:1]) for c in range(2)]
    far_rims = lax.ppermute(far_rims, "sub", route)
    fwd = call(
        node_body,
        shape((2 * rank, half)),
        (maps[0], fwd_mine, sel_other, near_rims),
        specs="vvva",
    )
    adj = call(
        adjoint_body,
        shape((2 * rank, half)),
        (maps[0], sel, sel_other, panel, near_rims),
        specs="vvvva",
        flops=4 << 30,
    )
    adj = call(
        rim_body,
        shape((3 * rank, half)),
        (sel, sel_other, near_rims, far_rims, adj),
        flops=1000,
    )
    new, node = call(
        functools.partial(joined_body, 1),
        [shape((2 * rank, half)), shape((rank, half))],
        (maps[1], adj, swapped(adj, "sub", 1)),
    )
    chains = [[fwd], [node, new]]
    steps = [("sub", bit) for bit in range(1, sub_bits)]
    steps += [("grp", bit) for bit in range(levels - sub_bits)]
    for level, (axis, bit) in enumerate(steps[:-1], 1):
        for kind, chain in enumerate(chains):
            if len(chain) == level:
                chain.append(
                    call(
                        functools.partial(level_body, kind, axis, bit),
                        shape((2 * rank, half)),
                        (maps[level], chain[-1], swapped(chain[-1], axis, bit)),
                        flops=4 << 30 if (level, kind) == (1, 0) else 1000,
                    )
                )
    axis, bit = steps[-1]
    ends = [swapped(chain[-1], axis, bit) for chain in chains]
    early = call(
        collect_body,
        shape((levels - 1, 2, rank, half)),
        (*chains[0], *chains[1], ends[0]),
        specs="v" * (2 * levels - 2) + "a",
        flops=4 << 30,
    )
    early_other = swapped(early, "sub", 0)
    x = call(
        functools.partial(last_body, axis, bit),
        shape((2, rank, half)),
        (maps[-1], chains[0][-1], ends[0], chains[1][-1], ends[1]),
        flops=4 << 30,
    )
    return call(
        functools.partial(output_body, vectors),
        shape((1, levels, 2, rank, samples)),
        (early, early_other, x, swapped(x, "sub", 0)),
        scratch=[pltpu.VMEM((levels, 2, rank, samples), BF), pltpu.SemaphoreType.DMA((levels,))],
        out="a",
    )


def solution(mesh):
    both = ("grp", "sub")
    return jax.shard_map(
        local,
        mesh=mesh,
        in_specs=(
            P(both, None),
            P("sub", "grp"),
            P(both, None, None, None),
            P(both, None),
            P(both, None, None),
            P(both, None, None, None),
            P(both, None, None, None),
            P(both, None, None, None, None),
        ),
        out_specs=P(both, None, None, None, None),
        check_vma=False,
    )
```
